32 devices in a mesh: dp: 16 (over z, y, core), mp: 2 (over x).
Axes of the slice: x: 2, y: 2, z: 4, core: 2. Of those that a mesh axis runs over, the one named last changes fastest.
Arguments:
- atoms: bfloat16 [64, 256, 512], P('dp', 'mp'), may hold values from -6 to 6
- atom_counts: int32 [64], P('dp'), may hold values from 64 to 256, as said below
- hydrogen: int32 [64, 256], P('dp'), may hold values 0 or 1
- atom_types: int32 [64, 256], P('dp'), may hold values from 0 to 29
- cotangent: bfloat16 [64, 256, 512], P('dp', 'mp'), may hold values from -6 to 6
- qkv_weight: float32 [512, 1536], replicated, may hold values from -0.25 to 0.25
- out_weight: float32 [512, 512], replicated, may hold values from -2 to 2
- up_weight: float32 [512, 2048], P(None, 'mp'), may hold values from -0.25 to 0.25
- down_weight: float32 [2048, 512], P('mp'), may hold values from -0.125 to 0.125
- ffn_bias: float32 [2048], P('mp'), may hold values from -3 to 3
- norm_params: float32 [4, 512], replicated
- pair_table: float32 [30, 30, 64], replicated, may hold values from -8 to 8
- qkv_state: float32 [512, 1536], replicated, may hold values from -384 to 384
- out_state: float32 [512, 512], replicated, may hold values from -80 to 80
- up_state: float32 [512, 2048], P(None, 'mp'), may hold values from -160 to 160
- down_state: float32 [2048, 512], P('mp'), may hold values from -256 to 256
- bias_state: float32 [2048], P('mp'), may hold values from -160 to 160
- norm_state: float32 [4, 512], replicated, may hold values from -640 to 640
- pair_state: float32 [30, 30, 64], replicated, may hold values from -32 to 32
Outputs:
- mixed_out: bfloat16 [64, 256, 512], P('dp', 'mp')
- atoms_grad: float32 [64, 256, 512], P('dp', 'mp')
- qkv_moment: float32 [512, 1536], replicated
- qkv_updated: float32 [512, 1536], replicated
- out_moment: float32 [512, 512], replicated
- out_updated: float32 [512, 512], replicated
- up_moment: float32 [512, 2048], P(None, 'mp')
- up_updated: float32 [512, 2048], P(None, 'mp')
- down_moment: float32 [2048, 512], P('mp')
- down_updated: float32 [2048, 512], P('mp')
- bias_moment: float32 [2048], P('mp')
- bias_updated: float32 [2048], P('mp')
- norm_moment: float32 [4, 512], replicated
- norm_updated: float32 [4, 512], replicated
- pair_moment: float32 [30, 30, 64], replicated
- pair_updated: float32 [30, 30, 64], replicated
The draws below stay inside these ranges and needn't reach their ends.
Inputs may be any that keep to these rules, and one draw needn't show every extreme that they name: `atom_counts`: among the 4 molecules of each index of dp, at least one fills all 256 slots.
All inputs are finite; a program needn't handle non-finite values. No bound on the sum of `hydrogen` on one device may be relied on, other than what follows from the above.
Results may differ from the reference program's by a relative error of at most 0.012.
The reference program's roundings to bfloat16 on the way count: a program that leaves them out, or rounds other values in their place, can miss the bound.
Values may be sent and summed in bfloat16 or wider, within the bound.
No kernel may reach another device: no remote copies, remote signals or barrier semaphores. Data moves between devices by JAX's collectives and lax.ppermute only.
A program may use at most 256 MiB of HBM per device.

```python
import math
import jax
import jax.numpy as jnp
from jax import lax

D = 512
H = 64
FF = 2048
NTYPE = 30
S = 256
MOL_DEV = 4
MOLS = 64


def draw_atom_counts(key, part):
    key = jax.random.fold_in(key, 11)
    first_key, second_key = jax.random.split(key)
    counts = jax.random.randint(first_key, (MOLS,), S // 4, S + 1)
    chosen = jax.random.randint(second_key, (MOLS // MOL_DEV,), 0, MOL_DEV)
    position = jnp.arange(MOLS) % MOL_DEV
    is_full = jnp.repeat(chosen, MOL_DEV) == position
    return jnp.where(is_full, S, counts).astype(jnp.int32)


def draw_norm_params(key, part):
    key = jax.random.fold_in(key, 5)
    normal_draw = jax.random.normal(key, (4, D), jnp.float32)
    gain_rows = 1.0 + 0.15 * normal_draw
    offset_rows = 0.3 * normal_draw
    is_gain = (jnp.arange(4) % 2 == 0)[:, None]
    return jnp.where(is_gain, gain_rows, offset_rows).astype(jnp.float32)


def set_ends(drawn, own_key, least, high):
    shape = drawn.shape
    index_at = [jax.random.randint(jax.random.fold_in(own_key, axis), (), 0, shape[axis]) for axis in range(len(shape))]
    drawn = drawn.at[tuple(index_at)].set(least)
    longest = shape.index(max(shape))
    index_at[longest] = (index_at[longest] + 1) % shape[longest]
    return drawn.at[tuple(index_at)].set(high)


def block_scale(rng, extent, cuts, least, largest):
    def one(dim, blocks):
        heights = jax.random.uniform(jax.random.fold_in(jax.random.fold_in(rng, 6), dim), (blocks,), jnp.float32, least / len(cuts), largest / len(cuts))
        return jnp.repeat(jnp.exp(heights), extent[dim] // blocks).reshape((-1,) + (1,) * (len(extent) - dim - 1))

    level = one(*cuts[0])
    for cut in cuts[1:]:
        level = level * one(*cut)
    return level


def centred(rng, shape, deviation, most, cuts=(), held_as=jnp.bfloat16):
    drawn = deviation * jax.random.normal(rng, shape, jnp.float32)
    if cuts:
        drawn = drawn * block_scale(rng, shape, cuts, -0.22, 0.18)
    return jnp.clip(drawn, -most, most).astype(held_as)


def setup_inputs(seed: int = 0) -> dict:
    splits = jax.random.split(jax.random.key(seed), 20)
    atoms = centred(splits[0], (MOLS, S, D), 1.0, 6.0, ((0, 16), (1, 2)))
    atom_counts = draw_atom_counts(jax.random.fold_in(splits[19], 71), 0)
    hydrogen = set_ends((jax.random.randint(splits[2], (MOLS, S), 0, 3) < 1).astype(jnp.int32), jax.random.fold_in(splits[2], 1), 0, 1)
    atom_types = set_ends(jax.random.randint(splits[3], (MOLS, S), 0, NTYPE), jax.random.fold_in(splits[3], 1), 0, NTYPE - 1).astype(jnp.int32)
    cotangent = centred(splits[4], (MOLS, S, D), 1.0, 6.0, ((0, 16), (1, 2)))
    qkv_weight = centred(splits[5], (D, 3 * D), D ** -0.5, 0.25, (), jnp.float32)
    out_weight = centred(splits[6], (D, D), 8 ** -0.5, 2.0, (), jnp.float32)
    up_weight = centred(splits[7], (D, FF), D ** -0.5, 0.25, ((1, 2),), jnp.float32)
    down_weight = centred(splits[8], (FF, D), FF ** -0.5, 0.125, ((0, 2),), jnp.float32)
    ffn_bias = centred(splits[9], (FF,), 0.5, 3.0, ((0, 2),), jnp.float32)
    norm_params = draw_norm_params(jax.random.fold_in(splits[19], 71), 0)
    pair_table = centred(splits[11], (NTYPE, NTYPE, H), 1.5, 8.0, (), jnp.float32)
    qkv_state = centred(splits[12], (D, 3 * D), (0.5 * (MOLS * S) ** 0.5), 384.0, (), jnp.float32)
    out_state = centred(splits[13], (D, D), (0.1 * (MOLS * S) ** 0.5), 80.0, (), jnp.float32)
    up_state = centred(splits[14], (D, FF), (0.2 * (MOLS * S) ** 0.5), 160.0, ((1, 2),), jnp.float32)
    down_state = centred(splits[15], (FF, D), (0.35 * (MOLS * S) ** 0.5), 256.0, ((0, 2),), jnp.float32)
    bias_state = centred(splits[16], (FF,), (0.2 * (MOLS * S) ** 0.5), 160.0, ((0, 2),), jnp.float32)
    norm_state = centred(splits[17], (4, D), (0.8 * (MOLS * S) ** 0.5), 640.0, (), jnp.float32)
    pair_state = centred(splits[18], (NTYPE, NTYPE, H), (0.08 * S * MOLS ** 0.5 * NTYPE ** -1), 32.0, (), jnp.float32)
    return dict(atoms=atoms, atom_counts=atom_counts, hydrogen=hydrogen, atom_types=atom_types, cotangent=cotangent, qkv_weight=qkv_weight, out_weight=out_weight, up_weight=up_weight, down_weight=down_weight, ffn_bias=ffn_bias, norm_params=norm_params, pair_table=pair_table, qkv_state=qkv_state, out_state=out_state, up_state=up_state, down_state=down_state, bias_state=bias_state, norm_state=norm_state, pair_state=pair_state)


norm_eps = 1e-05
masked_score = -1000000000.0
exact_precision = lax.Precision.HIGHEST
coef_first = 3.4445
coef_second = -4.775
coef_third = 2.0315
momentum_keep = 0.5
rate_qkv = 1.0
rate_out = 4.0
rate_up = 1.0
rate_down = 1.0
rate_norm = 0.001
rate_bias = 0.01
rate_pair = 0.05

@jax.custom_vjp
def low(v):
    return lax.optimization_barrier(v.astype(jnp.bfloat16)).astype(jnp.float32)

@jax.custom_vjp
def low_back(v):
    return v

def low_keep(v):
    return (low(v), None)

def low_pass(kept, grad):
    return (grad,)

def back_keep(v):
    return (v, None)

def back_low(kept, grad):
    return (low(grad),)
low.defvjp(low_keep, low_pass)
low_back.defvjp(back_keep, back_low)

def layer_norm(values, gain_vec, offset):
    center = values - lax.optimization_barrier(jnp.mean(values, axis=-1, keepdims=True))
    spread = lax.optimization_barrier(jnp.mean(center * center, axis=-1, keepdims=True))
    return center * lax.rsqrt(spread + norm_eps) * gain_vec + offset

def split_heads(tensor, head_count):
    return tensor.reshape(tensor.shape[:-1] + (head_count, tensor.shape[-1] // head_count))

def group_forward(params, group_data):
    qkv_weight, out_weight, up_weight, down_weight, ffn_bias, norm_params, pair_table = params
    inputs, counts, hydrogen, type_ids = group_data
    model_width = inputs.shape[-1]
    head_count = pair_table.shape[-1]
    scale_factor = (model_width // head_count) ** (-0.5)
    slot_ids = jnp.arange(inputs.shape[1])
    present = slot_ids[None, :] < counts[:, None]
    valid_rows = present.astype(jnp.float32)[..., None]
    key_ok = present & (hydrogen == 0)
    allowed = key_ok[:, None, :] | (slot_ids[:, None] == slot_ids[None, :])[None]
    normed = low(layer_norm(inputs, norm_params[0], norm_params[1]))
    projected = jnp.einsum('gsd,de->gse', normed, low(qkv_weight), precision=exact_precision)
    queries = split_heads(low(low_back(projected[..., :model_width])), head_count)
    keys_all = split_heads(low(low_back(projected[..., model_width:2 * model_width])), head_count)
    values_all = split_heads(low(low_back(projected[..., 2 * model_width:])), head_count)
    looked = low(pair_table)[type_ids[:, :, None], type_ids[:, None, :]]
    pair_bias = jnp.transpose(looked, (0, 3, 1, 2))
    scores = jnp.einsum('gihd,gjhd->ghij', queries, keys_all, precision=exact_precision) * scale_factor + pair_bias
    scores = low_back(scores)
    scores = jnp.where(allowed[:, None], scores, masked_score)
    attn_probs = low(jax.nn.softmax(scores, axis=-1))
    attended = jnp.einsum('ghij,gjhd->gihd', attn_probs, values_all, precision=exact_precision)
    attended = low(low_back(attended.reshape(inputs.shape)))
    branch = low_back(jnp.einsum('gsd,de->gse', attended, low(out_weight), precision=exact_precision))
    middle = inputs + valid_rows * branch
    normed_two = low(layer_norm(middle, norm_params[2], norm_params[3]))
    hidden = low_back(jnp.einsum('gsd,df->gsf', normed_two, low(up_weight), precision=exact_precision) + ffn_bias)
    activated = low(jax.nn.gelu(hidden, approximate=False))
    ffn_out = low_back(jnp.einsum('gsf,fd->gsd', activated, low(down_weight), precision=exact_precision))
    return middle + valid_rows * ffn_out

def orthogonalize(matrix):
    flipped = matrix.shape[0] > matrix.shape[1]
    current = matrix.T if flipped else matrix
    current = current / (jnp.sqrt(jnp.sum(current * current)) + 1e-07)
    for iteration in range(5):
        gram_matrix = jnp.dot(current, current.T, precision=exact_precision)
        polynomial = coef_second * gram_matrix + coef_third * jnp.dot(gram_matrix, gram_matrix, precision=exact_precision)
        current = coef_first * current + jnp.dot(polynomial, current, precision=exact_precision)
    return current.T if flipped else current

def muon_step(weight, moment, gradient, step_rate):
    renewed = momentum_keep * moment + gradient
    aspect = max(1.0, weight.shape[0] / weight.shape[1])
    return (renewed, weight - step_rate * math.sqrt(aspect) * orthogonalize(renewed))

def plain_step(weight, moment, gradient, step_rate):
    renewed = momentum_keep * moment + gradient
    return (renewed, weight - step_rate * renewed)

def reference(atoms, atom_counts, hydrogen, atom_types, cotangent, qkv_weight, out_weight, up_weight, down_weight, ffn_bias, norm_params, pair_table, qkv_state, out_state, up_state, down_state, bias_state, norm_state, pair_state):
    group_count = MOLS // 8

    def regroup(tensor):
        return tensor.reshape((group_count, 8) + tensor.shape[1:])
    fixed_data = (regroup(atom_counts), regroup(hydrogen), regroup(atom_types))
    params = (qkv_weight, out_weight, up_weight, down_weight, ffn_bias, norm_params, pair_table)

    def forward(inputs, weights):

        def one_group(group_data):
            return group_forward(weights, group_data)
        return lax.map(jax.checkpoint(one_group), (inputs,) + fixed_data)
    result, pullback = jax.vjp(forward, regroup(atoms.astype(jnp.float32)), params)
    input_grad, weight_grads = pullback(regroup(cotangent.astype(jnp.float32)))
    qkv_grad, out_grad, up_grad, down_grad, bias_grad, norm_grad, pair_grad = weight_grads
    qkv_moment, qkv_updated = muon_step(qkv_weight, qkv_state, qkv_grad, rate_qkv)
    out_moment, out_updated = muon_step(out_weight, out_state, out_grad, rate_out)
    up_moment, up_updated = muon_step(up_weight, up_state, up_grad, rate_up)
    down_moment, down_updated = muon_step(down_weight, down_state, down_grad, rate_down)
    bias_moment, bias_updated = plain_step(ffn_bias, bias_state, bias_grad, rate_bias)
    norm_moment, norm_updated = plain_step(norm_params, norm_state, norm_grad, rate_norm)
    pair_moment, pair_updated = plain_step(pair_table, pair_state, pair_grad, rate_pair)
    return (result.reshape(atoms.shape).astype(jnp.bfloat16), input_grad.reshape(atoms.shape), qkv_moment, qkv_updated, out_moment, out_updated, up_moment, up_updated, down_moment, down_updated, bias_moment, bias_updated, norm_moment, norm_updated, pair_moment, pair_updated)
```

```python
import functools
import math

import jax
import jax.numpy as jnp
from jax import lax
from jax.experimental import pallas as pl
from jax.experimental.pallas import tpu as pltpu
from jax.sharding import PartitionSpec as P

norm_eps = 1e-05
masked_score = -1000000000.0
coef_first = 3.4445
coef_second = -4.775
coef_third = 2.0315
momentum_keep = 0.5
rate_qkv = 1.0
rate_out = 4.0
rate_up = 1.0
rate_down = 1.0
rate_norm = 0.001
rate_bias = 0.01
rate_pair = 0.05

bf16 = jnp.bfloat16
f32 = jnp.float32
log2_e = 1.4426950408889634
NN = (((1,), (0,)), ((), ()))
NT = (((1,), (1,)), ((), ()))
TN = (((0,), (0,)), ((), ()))
vmem_bytes = 56 * 2**20


def mxu(left, right, dims=NN):
    return lax.dot_general(left, right, dims, preferred_element_type=f32)


def norm_parts(values):
    center = values - jnp.mean(values, axis=-1, keepdims=True)
    inverse = lax.rsqrt(jnp.mean(center * center, axis=-1, keepdims=True) + norm_eps)
    return center * inverse, inverse


def norm_back(grad_rows, unit_rows, inverse, gain_vec):
    scaled = grad_rows * gain_vec
    mean_one = jnp.mean(scaled, axis=-1, keepdims=True)
    mean_two = jnp.mean(scaled * unit_rows, axis=-1, keepdims=True)
    return inverse * (scaled - mean_one - unit_rows * mean_two)


def two_parts(values):
    high = values.astype(bf16)
    return high, (values - high.astype(f32)).astype(bf16)


def attend_kernel(
    groups, state_steps, own_ref, other_ref, qkv_w_ref, norm_ref, table_ref, type_t_ref, type_ref, ok_ref, valid_ref, out_w_ref,
    core_ref, up_state_ref, down_state_ref,
    prob_ref, read_t_ref, query_t_ref, key_t_ref, value_ref, normed_t_ref, attended_t_ref, middle_ref, normed_two_ref,
    own_state_ref, leaving_ref,
    left_all, query_high, query_low, value_t, bias_all, cap, read_all, qkv_low,
):
    group = pl.program_id(1)
    slots = ok_ref.shape[1]
    width = own_ref.shape[2]
    span = width // groups
    heads = prob_ref.shape[1]
    kinds = type_t_ref.shape[1]

    def load_rows():
        return jnp.concatenate([own_ref[0], other_ref[0]], axis=0).astype(f32)

    @pl.when((group == 0) & (pl.program_id(0) == 0))
    def _():
        qkv_low[...] = qkv_w_ref[...].astype(bf16)

    @pl.when(group == 0)
    def _():
        unit, _ = norm_parts(load_rows())
        normed = unit * norm_ref[0:1] + norm_ref[1:2]
        normed_t_ref[0] = normed.T.astype(bf16)
        normed = normed.astype(bf16)
        query = mxu(normed, qkv_low[:, 0:width]).T.astype(bf16)
        query_t_ref[0] = query
        keys = mxu(normed, qkv_low[:, width : 2 * width])
        key_t_ref[0] = keys.T.astype(bf16)
        keys = keys.astype(bf16)
        values = mxu(normed, qkv_low[:, 2 * width :])
        value_t[...] = values.T.astype(bf16)
        values = values.astype(bf16)
        head_width = span // heads
        scaled = query.astype(f32) * (head_width**-0.5 * log2_e)
        high = scaled.astype(bf16).astype(f32)
        query_high[...] = high
        query_low[...] = scaled - high
        bias_all[...] = mxu(table_ref[...], type_t_ref[0]).astype(bf16)
        blank = jnp.zeros((slots, 256 - 2 * span - 2 * kinds), bf16)
        for index in range(groups):
            part = keys[:, span * index : span * (index + 1)]
            left_all[index] = jnp.concatenate([part, part, type_ref[0], type_ref[0], blank], axis=1)
            value_ref[0, index] = values[:, span * index : span * (index + 1)]
        row = lax.broadcasted_iota(jnp.int32, (slots, slots), 0)
        column = lax.broadcasted_iota(jnp.int32, (slots, slots), 1)
        cap[...] = jnp.where((ok_ref[0] > 0.0) | (row == column), 3e38, masked_score * log2_e)

    step = pl.program_id(0) * groups + group
    early = step < state_steps

    def keep_state(state):
        own_state_ref[...] = state
        leaving_ref[...] = state.astype(bf16)

    @pl.when(early & (core_ref[0] == 0))
    def _():
        keep_state(up_state_ref[...].T)

    @pl.when(early & (core_ref[0] == 1))
    def _():
        keep_state(down_state_ref[...])

    left = left_all[group]
    owner = lax.broadcasted_iota(jnp.int32, (span, slots), 0) // (span // heads)
    start = pl.multiple_of(group * span, span)
    high = query_high[pl.ds(start, span), :]
    low = query_low[pl.ds(start, span), :]
    zero = jnp.zeros_like(high)
    blank = jnp.zeros((256 - 2 * span - 2 * kinds, slots), bf16)

    def scores(head):
        mine = owner == head
        place = pl.multiple_of((group * heads + head) * 2 * kinds, 2 * kinds)
        bias = bias_all[pl.ds(place, 2 * kinds), :]
        parts = [jnp.where(mine, high, zero).astype(bf16), jnp.where(mine, low, zero).astype(bf16), bias, blank]
        return mxu(left, jnp.concatenate(parts, axis=0))

    def softmax(head, logits):
        logits = jnp.minimum(logits, cap[...])
        raised = jnp.exp2(logits - jnp.max(logits, axis=0, keepdims=True))
        low_probs = (raised * (1.0 / jnp.sum(raised, axis=0, keepdims=True))).astype(bf16)
        prob_ref[0, head] = low_probs
        return low_probs

    def weigh(head, low_probs):
        pair = value_t[pl.ds(pl.multiple_of(group * span + (head // 2) * 16, 16), 16), :]
        both = mxu(pair, low_probs)
        return both[0:8] if head % 2 == 0 else both[8:16]

    ahead = 3
    waiting = [scores(head) for head in range(ahead)]
    probs, results = [], []
    for head in range(heads):
        probs.append(softmax(head, waiting[head]))
        if head + ahead < heads:
            waiting.append(scores(head + ahead))
        if head:
            results.append(weigh(head - 1, probs[head - 1]))
    results.append(weigh(heads - 1, probs[heads - 1]))
    read = jnp.concatenate(results, axis=0)
    read_t_ref[0] = read
    read_all[pl.ds(start, span), :] = read.astype(bf16)

    @pl.when(group == groups - 1)
    def _():
        attended = read_all[...]
        attended_t_ref[0] = attended
        middle = load_rows() + valid_ref[0] * mxu(attended, out_w_ref[...].astype(bf16), TN)
        middle_ref[0] = middle
        unit, _ = norm_parts(middle)
        normed_two_ref[0] = (unit * norm_ref[2:3] + norm_ref[3:4]).astype(bf16)


def attend(own, other, qkv_w, norms, table, type_t, types, ok, valid, out_w, core, up_state, down_state):
    mols, half, width = own.shape
    slots = 2 * half
    groups = 8
    heads = width // 8 // groups
    kinds = type_t.shape[1]
    span = width // groups
    whole = lambda a: pl.BlockSpec(a.shape, lambda m, g: (0,) * a.ndim)
    each = lambda *s: pl.BlockSpec((1,) + s, lambda m, g: (m,) + (0,) * len(s))
    state_steps = mols * groups // 2
    state_rows = down_state.shape[0] // state_steps
    state_at = lambda m, g: jnp.minimum(m * groups + g, state_steps - 1)
    state_block = pl.BlockSpec((state_rows, width), lambda m, g: (state_at(m, g), 0))
    shape = jax.ShapeDtypeStruct
    return pl.pallas_call(
        functools.partial(attend_kernel, groups, state_steps),
        grid=(mols, groups),
        in_specs=[each(half, width), each(half, width), whole(qkv_w), whole(norms), whole(table),
                  each(kinds, slots), each(slots, kinds), each(slots, 1), each(slots, 1), whole(out_w),
                  pl.BlockSpec(memory_space=pltpu.SMEM), pl.BlockSpec((width, state_rows), lambda m, g: (0, state_at(m, g))), state_block],
        out_specs=[pl.BlockSpec((1, heads, slots, slots), lambda m, g: (m, g, 0, 0)),
                   pl.BlockSpec((1, span, slots), lambda m, g: (m, g, 0)),
                   each(width, slots), each(width, slots), each(groups, slots, span), each(width, slots), each(width, slots),
                   each(slots, width), each(slots, width), state_block, state_block],
        out_shape=[shape((mols, groups * heads, slots, slots), bf16), shape((mols, width, slots), f32),
                   shape((mols, width, slots), bf16), shape((mols, width, slots), bf16),
                   shape((mols, groups, slots, span), bf16), shape((mols, width, slots), bf16),
                   shape((mols, width, slots), bf16), shape((mols, slots, width), f32), shape((mols, slots, width), bf16),
                   shape(down_state.shape, f32), shape(down_state.shape, bf16)],
        scratch_shapes=[pltpu.VMEM((groups, slots, 256), bf16), pltpu.VMEM((width, slots), f32), pltpu.VMEM((width, slots), f32),
                        pltpu.VMEM((width, slots), bf16), pltpu.VMEM((table.shape[0], slots), bf16),
                        pltpu.VMEM((slots, slots), f32), pltpu.VMEM((width, slots), bf16), pltpu.VMEM(qkv_w.shape, bf16)],
        compiler_params=pltpu.CompilerParams(vmem_limit_bytes=vmem_bytes),
        cost_estimate=pl.CostEstimate(flops=22 * 10**9, bytes_accessed=24 * 10**6, transcendentals=8 * 10**6),
        name="attend",
    )(own, other, qkv_w, norms, table, type_t, types, ok, valid, out_w, core, up_state, down_state)


def feed_kernel(
    piece_rows,
    place_ref, normed_ref, middle_ref, own_grad_ref, other_grad_ref, valid_ref, attended_t_ref, norm_ref, out_w_ref,
    up_own_ref, down_own_ref, first_ref, second_ref, bias_ref,
    keep_ref, send_ref, bias_grad_ref, mixed_ref, middle_grad_ref, attended_grad_t_ref, out_grad_ref, norm_grad_ref,
    rows_grad, sum_out, sum_back, up_used, down_used, out_low,
):
    step = pl.program_id(0)
    steps = pl.num_programs(0)
    core = place_ref[0]
    me = place_ref[4]
    mols, half, width = own_grad_ref.shape
    rows = mols * 2 * half

    def given():
        return jnp.concatenate([part for m in range(mols) for part in (own_grad_ref[m], other_grad_ref[m])], axis=0)

    @pl.when(step == 0)
    def _():
        rows_grad[...] = (valid_ref[...] * given().astype(f32)).astype(bf16)
        out_low[...] = out_w_ref[...].astype(bf16)
        sum_out[...] = jnp.zeros_like(sum_out)
        sum_back[...] = jnp.zeros_like(sum_back)

    is_own = step < steps // 2

    def choose(condition, up_ref, down_ref):
        @pl.when(condition)
        def _():
            up_used[...] = up_ref[...]
            down_used[...] = down_ref[...]

    choose(is_own, up_own_ref, down_own_ref)
    choose(jnp.logical_not(is_own) & (core == 0), first_ref, second_ref)
    choose(jnp.logical_not(is_own) & (core == 1), second_ref, first_ref)
    up = up_used[...]
    down = down_used[...]
    normed = normed_ref[...]
    grads = rows_grad[...]
    hidden = mxu(normed, up, NT) + bias_ref[...]
    back = mxu(grads, down, NT)
    cumulative = 0.5 * (1.0 + lax.erf(hidden * 0.7071067811865476))
    activated = (hidden * cumulative).astype(bf16)
    slope = cumulative + hidden * jnp.exp(-0.5 * hidden * hidden) * 0.3989422804014327
    hidden_grad = (back * slope).astype(bf16)
    sum_out[...] += mxu(activated, down)
    sum_back[...] += mxu(hidden_grad, up)
    up_grad = mxu(hidden_grad, normed, TN).astype(bf16)
    down_grad = mxu(activated, grads, TN).astype(bf16)
    bias_grad_ref[...] = jnp.sum(hidden_grad.astype(f32), axis=0, keepdims=True)
    place_half = step // (steps // 2)
    first_piece = step % (steps // 2) * (up.shape[0] // piece_rows)

    def place_rows(kept, sent):
        for piece in range(up.shape[0] // piece_rows):
            at = jnp.bitwise_xor(first_piece + piece, me)
            keep_ref[place_half, at] = kept[piece * piece_rows : (piece + 1) * piece_rows]
            send_ref[place_half, at] = sent[piece * piece_rows : (piece + 1) * piece_rows]

    @pl.when(core == 0)
    def _():
        place_rows(up_grad, down_grad)

    @pl.when(core == 1)
    def _():
        place_rows(down_grad, up_grad)

    @pl.when(step == steps - 1)
    def _():
        middle = middle_ref[...]
        valid = valid_ref[...]
        mixed_ref[...] = (middle + valid * sum_out[...]).astype(bf16)
        unit, inverse = norm_parts(middle)
        grad_two = sum_back[...]
        norm_grad_ref[0:1] = jnp.sum(grad_two * unit, axis=0, keepdims=True)
        norm_grad_ref[1:2] = jnp.sum(grad_two, axis=0, keepdims=True)
        middle_grad = given().astype(f32) + norm_back(grad_two, unit, inverse, norm_ref[2:3])
        middle_grad_ref[...] = middle_grad
        branch_grad = (valid * middle_grad).astype(bf16)
        total = None
        for m in range(mols):
            part = branch_grad[m * 2 * half : (m + 1) * 2 * half]
            attended_grad_t_ref[m] = mxu(out_low[...], part, NT).astype(bf16)
            term = mxu(attended_t_ref[m], part)
            total = term if total is None else total + term
        out_grad_ref[...] = total


def feed(place, normed, middle, own_grad, other_grad, valid, attended_t, norms, out_w, up_own, down_own, first, second, bias,
         half_pieces):
    mols, half, width = own_grad.shape
    rows = mols * 2 * half
    held = up_own.shape[0]
    block = 256
    per_half = held // block
    steps = 2 * per_half
    piece_rows = held // half_pieces
    whole = lambda a: pl.BlockSpec(a.shape, lambda j, s: (0,) * a.ndim)
    fixed = lambda *s: pl.BlockSpec(s, lambda j, s_: (0,) * len(s))
    mine = pl.BlockSpec((block, width), lambda j, s: (jnp.minimum(j, per_half - 1), 0))
    theirs = pl.BlockSpec((block, width), lambda j, s: (jnp.maximum(j - per_half, 0), 0))
    shape = jax.ShapeDtypeStruct
    return pl.pallas_call(
        functools.partial(feed_kernel, piece_rows),
        grid_spec=pltpu.PrefetchScalarGridSpec(
            num_scalar_prefetch=1,
            grid=(steps,),
            in_specs=[whole(normed), whole(middle), whole(own_grad), whole(other_grad), whole(valid), whole(attended_t),
                      whole(norms), whole(out_w), mine, mine, theirs, theirs, pl.BlockSpec((1, block), lambda j, s: (0, j))],
            out_specs=[fixed(2, half_pieces, piece_rows, width), fixed(2, half_pieces, piece_rows, width),
                       pl.BlockSpec((1, block), lambda j, s: (0, j)),
                       fixed(rows, width), fixed(rows, width), fixed(mols, width, 2 * half),
                       fixed(width, width), fixed(2, width)],
            scratch_shapes=[pltpu.VMEM((rows, width), bf16), pltpu.VMEM((rows, width), f32), pltpu.VMEM((rows, width), f32),
                            pltpu.VMEM((block, width), bf16), pltpu.VMEM((block, width), bf16), pltpu.VMEM(out_w.shape, bf16)],
        ),
        out_shape=[shape((2, half_pieces, piece_rows, width), bf16), shape((2, half_pieces, piece_rows, width), bf16), shape((1, 2 * held), f32), shape((rows, width), bf16),
                   shape((rows, width), f32), shape((mols, width, 2 * half), bf16),
                   shape((width, width), f32), shape((2, width), f32)],
        compiler_params=pltpu.CompilerParams(vmem_limit_bytes=vmem_bytes),
        cost_estimate=pl.CostEstimate(flops=14 * 10**9, bytes_accessed=14 * 10**6, transcendentals=2 * 10**6),
        name="feed",
    )(place, normed, middle, own_grad, other_grad, valid, attended_t, norms, out_w, up_own, down_own, first, second, bias)


def score_kernel(
    prob_ref, grad_t_ref, read_t_ref, value_ref, key_t_ref, query_t_ref, type_t_ref, after_ref,
    query_grad_ref, key_grad_ref, value_grad_ref, pair_grad_ref,
):
    molecule = pl.program_id(1)
    heads, slots = prob_ref.shape[1], prob_ref.shape[2]
    span = grad_t_ref.shape[1]
    head_width = span // heads
    scale = head_width**-0.5
    values = value_ref[0, 0]
    grads = grad_t_ref[0]
    keys = key_t_ref[0]
    queries = query_t_ref[0]
    kinds = type_t_ref[0]
    count = kinds.shape[0]
    owner = lax.broadcasted_iota(jnp.int32, (span, slots), 0) // head_width
    wide_grads = grads.astype(f32)
    zero = jnp.zeros_like(wide_grads)
    dotted = wide_grads * read_t_ref[0]

    def pair_of(array, head):
        return array[(head // 2) * 16 : (head // 2) * 16 + 16]

    def own_half(both, head):
        return both[0:8] if head % 2 == 0 else both[8:16]

    def prob_grads(head):
        return mxu(values, jnp.where(owner == head, wide_grads, zero).astype(bf16))

    def score_grads(head, prob_grad):
        center = jnp.sum(dotted[head * head_width : (head + 1) * head_width], axis=0, keepdims=True)
        return (prob_ref[0, head].astype(f32) * (prob_grad - center)).astype(bf16)

    query_parts, key_parts, value_parts, type_parts = [], [], [], []

    def products(head, score_grad):
        left = jnp.concatenate([pair_of(keys, head), kinds], axis=0)
        both = mxu(left, score_grad)
        query_parts.append(own_half(both, head) * scale)
        type_parts.append(both[16:])
        key_parts.append(own_half(mxu(pair_of(queries, head), score_grad, NT), head) * scale)

    ahead = 3
    waiting = [prob_grads(head) for head in range(ahead)]
    done = []
    for head in range(heads):
        done.append(score_grads(head, waiting[head]))
        value_parts.append(own_half(mxu(pair_of(grads, head), prob_ref[0, head], NT), head))
        if head + ahead < heads:
            waiting.append(prob_grads(head + ahead))
        if head:
            products(head - 1, done[head - 1])
    products(heads - 1, done[heads - 1])
    query_grad_ref[0] = jnp.concatenate(query_parts, axis=0).astype(bf16)
    key_grad_ref[0] = jnp.concatenate(key_parts, axis=0).astype(bf16)
    value_grad_ref[0] = jnp.concatenate(value_parts, axis=0).astype(bf16)
    high, low = two_parts(jnp.concatenate(type_parts, axis=0))
    pairs = mxu(kinds, high, NT) + mxu(kinds, low, NT)

    @pl.when(molecule == 0)
    def _():
        pair_grad_ref[...] = pairs

    @pl.when(molecule > 0)
    def _():
        pair_grad_ref[...] += pairs


def attend_back(first, count, probs, grad_t, read_t, values, key_t, query_t, type_t, after):
    mols, all_heads, slots, _ = probs.shape
    groups = values.shape[1]
    heads = all_heads // groups
    width = grad_t.shape[1]
    span = width // groups
    kinds = type_t.shape[1]
    rows = pl.BlockSpec((1, span, slots), lambda g, m: (m, first + g, 0))
    new_rows = pl.BlockSpec((1, span, slots), lambda g, m: (m, g, 0))
    shape = jax.ShapeDtypeStruct
    part = shape((mols, count * span, slots), bf16)
    return pl.pallas_call(
        score_kernel,
        grid=(count, mols),
        in_specs=[pl.BlockSpec((1, heads, slots, slots), lambda g, m: (m, first + g, 0, 0)), rows, rows,
                  pl.BlockSpec((1, 1, slots, span), lambda g, m: (m, first + g, 0, 0)), rows, rows,
                  pl.BlockSpec((1, kinds, slots), lambda g, m: (m, 0, 0)), pl.BlockSpec(memory_space=pl.ANY)],
        out_specs=[new_rows, new_rows, new_rows, pl.BlockSpec((kinds, heads * kinds), lambda g, m: (0, g))],
        out_shape=[part, part, part, shape((kinds, count * heads * kinds), f32)],
        compiler_params=pltpu.CompilerParams(vmem_limit_bytes=vmem_bytes),
        cost_estimate=pl.CostEstimate(flops=5 * 10**9 * count, bytes_accessed=3 * 10**6 * count, transcendentals=0),
        name="attend_back",
    )(probs, grad_t, read_t, values, key_t, query_t, type_t, after)


def project_kernel(
    pieces, calls, place_ref, normed_t_ref, weight_ref, own_ref, other_ref, middle_grad_ref, norm_ref, tiny_ref, after_ref, *refs,
):
    part_refs, refs = refs[: 4 * calls], refs[4 * calls :]
    keep_ref, send_ref, own_out_ref, other_out_ref, ordered, grad_t_ref = refs
    part_rows = part_refs[0].shape[1]
    for call in range(calls):
        for kind in range(3):
            start = kind * part_rows * calls + call * part_rows
            grad_t_ref[:, start : start + part_rows] = part_refs[4 * call + kind][...]
    pair_refs = part_refs[3::4]
    per_pair = pair_refs[0].shape[1] // 128
    me = place_ref[2]
    mols, width, slots = normed_t_ref.shape
    half = slots // 2
    rows = width // pieces
    block = 256
    for start in range(0, width, block):
        total = sum(mxu(normed_t_ref[m, start : start + block], grad_t_ref[m], NT) for m in range(mols))
        for piece in range(block // rows):
            ordered[start // rows + piece, :, 0 : total.shape[1]] = total[piece * rows : (piece + 1) * rows]
    weight = weight_ref[...].astype(bf16)
    gain_grad, offset_grad = 0.0, 0.0
    for m in range(mols):
        normed_grad = mxu(weight, grad_t_ref[m]).T
        unit, inverse = norm_parts(jnp.concatenate([own_ref[m], other_ref[m]], axis=0).astype(f32))
        gain_grad += jnp.sum(normed_grad * unit, axis=0, keepdims=True)
        offset_grad += jnp.sum(normed_grad, axis=0, keepdims=True)
        result = middle_grad_ref[m * slots : (m + 1) * slots] + norm_back(normed_grad, unit, inverse, norm_ref[0:1])
        own_out_ref[m] = result[:half]
        other_out_ref[m] = result[half:].astype(bf16)
    columns = weight_ref.shape[1]
    kinds = pair_refs[0].shape[0]
    for chunk in range(width // kinds):
        at = chunk % per_pair * 128
        ordered[:, chunk, columns : columns + 128] = pair_refs[chunk // per_pair][:, at : at + 128]
    vectors = jnp.concatenate([gain_grad, offset_grad, tiny_ref[...], jnp.zeros((128 - 8, width), f32)], axis=0)
    ordered[:, :, columns + 128 : columns + 256] = vectors.T.reshape(kinds, width // kinds, 128)
    core = place_ref[0]
    count = pieces // 2
    for piece in range(count):
        at = jnp.bitwise_xor(piece, me)
        keep_ref[at] = ordered[core * count + piece].astype(bf16)
        send_ref[at] = ordered[(1 - core) * count + piece].astype(bf16)


def project_back(place, parts, normed_t, weight, own, other, middle_grad, norms, tiny, after, pieces):
    mols, width, slots = normed_t.shape
    columns = weight.shape[1]
    shape = jax.ShapeDtypeStruct
    vmem = pl.BlockSpec(memory_space=pltpu.VMEM)
    return pl.pallas_call(
        functools.partial(project_kernel, pieces, len(parts)),
        in_specs=[pl.BlockSpec(memory_space=pltpu.SMEM)] + [vmem] * 7 + [pl.BlockSpec(memory_space=pl.ANY)] + [vmem] * 4 * len(parts),
        out_specs=[vmem] * 4,
        out_shape=[shape((pieces // 2, width // pieces, columns + 256), bf16), shape((pieces // 2, width // pieces, columns + 256), bf16),
                   shape((mols, slots // 2, width), f32),
                   shape((mols, slots // 2, width), bf16)],
        scratch_shapes=[pltpu.VMEM((pieces, width // pieces, columns + 256), f32), pltpu.VMEM((mols, columns, slots), bf16)],
        compiler_params=pltpu.CompilerParams(vmem_limit_bytes=vmem_bytes),
        cost_estimate=pl.CostEstimate(flops=4 * 10**9, bytes_accessed=10 * 10**6, transcendentals=0),
        name="project_back",
    )(place, normed_t, weight, own, other, middle_grad, norms, tiny, after, *[array for part in parts for array in part])


def swap(array, axis, bit, size):
    return lax.ppermute(array, axis, [(i, i ^ (1 << bit)) for i in range(size)])


def add_low(left, right):
    return (left.astype(f32) + right.astype(f32)).astype(bf16)


def halve(array, axes, digit, sizes):
    index = axes.index(digit)
    keep = lax.index_in_dim(array, 0, index, keepdims=False)
    send = lax.index_in_dim(array, 1, index, keepdims=False)
    return add_low(keep, swap(send, *digit, sizes[digit[0]])), axes[:index] + axes[index + 1 :]


def jump(array, digits, sizes):
    axis = digits[0][0]
    mask = sum(1 << bit for _, bit in digits)
    return lax.ppermute(array, axis, [(i, i ^ mask) for i in range(sizes[axis])])


def quarter(array, axes, pair, sizes, after=None):
    first, second = axes.index(pair[0]), axes.index(pair[1])
    array = jnp.moveaxis(array, (first, second), (0, 1))
    kept = array[0, 0]
    if after is not None:
        kept, _ = lax.optimization_barrier((kept, after))
    total = kept.astype(f32)
    for place, digits in (((1, 0), pair[:1]), ((0, 1), pair[1:]), ((1, 1), pair)):
        total = total + jump(array[place], digits, sizes).astype(f32)
    return total.astype(bf16), [digit for digit in axes if digit not in pair]


def double(array, digit, sizes):
    return jnp.stack([array, swap(array, *digit, sizes[digit[0]])])


def quadruple(array, pair, sizes):
    pieces = [array] + [jump(array, digits, sizes) for digits in (pair[1:], pair[:1], pair)]
    return jnp.stack(pieces).reshape((2, 2) + array.shape)


def split_middle(digits):
    middle = digits[1:-1]
    return middle[: len(middle) % 2], [middle[i : i + 2] for i in range(len(middle) % 2, len(middle), 2)]


def scatter_ends(array, digits, sizes):
    first, last = digits[0], digits[-1]
    cut = array.shape[-1] // 2
    left, left_axes = halve(array[..., :cut], digits, first, sizes)
    right, right_axes = halve(array[..., cut:], digits, last, sizes)
    step = (left, right)
    left, _ = halve(left, left_axes, last, sizes)
    right, _ = halve(right, right_axes, first, sizes)
    return step, jnp.concatenate([left, right], axis=-1)


def scatter_middle(both, digits, sizes, after=None):
    single, pairs = split_middle(digits)
    axes = digits[1:-1]
    for pair in pairs[::-1]:
        both, axes = quarter(both, axes, pair, sizes, after)
    for digit in single:
        both, axes = halve(both, axes, digit, sizes)
    return both


def gather(both, digits, sizes):
    first, last = digits[0], digits[-1]
    single, pairs = split_middle(digits)
    for digit in single:
        both = double(both, digit, sizes)
    for pair in pairs:
        both = quadruple(both, pair, sizes)
    cut = both.shape[-1] // 2
    left = double(double(both[..., :cut], last, sizes), first, sizes)
    right = double(double(both[..., cut:], first, sizes), last, sizes)
    return jnp.concatenate([left, jnp.swapaxes(right, 0, 1)], axis=-1)


def gather_order(digits):
    single, pairs = split_middle(digits)
    return [digits[0], digits[-1]] + [digit for pair in pairs[::-1] for digit in pair] + single


def place_list(order, digits):
    result = []
    for number in range(2 ** len(order)):
        bits = {digit: (number >> (len(order) - 1 - i)) & 1 for i, digit in enumerate(order)}
        result.append(sum(bits[digit] << (len(digits) - 1 - i) for i, digit in enumerate(digits)))
    return result


def absolute(array, digits, places):
    for index, (axis, bit) in enumerate(digits):
        flag = (places[axis] >> bit) & 1
        array = jnp.where(flag == 1, jnp.flip(array, index), array)
    return array


def muon_load(high_ref, low_ref, source_ref, scale, tall):
    block = 256
    for start in range(0, source_ref.shape[0], block):
        at = slice(start, start + block)
        high_ref[at], low_ref[at] = two_parts(source_ref[at] * scale)


def symmetric_product(left, right):
    half = left.shape[0] // 2
    left_high, left_low = two_parts(left)
    right_high, right_low = two_parts(right)
    rows = jnp.concatenate([left_high, left_low, left_high], axis=1)
    columns = jnp.concatenate([right_high, right_high, right_low], axis=0)
    top = mxu(rows[:half], columns)
    corner = mxu(rows[half:], columns[:, half:])
    return jnp.concatenate([top, jnp.concatenate([top[:, half:].T, corner], axis=1)], axis=0)


def muon_iterate(tall, plan, high_ref, low_ref, gram_ref, poly_ref, product_ref):
    size = gram_ref.shape[0]
    length = high_ref.shape[0] if tall else high_ref.shape[1]
    block = 256
    row = lax.broadcasted_iota(jnp.int32, (size, size), 0)
    column = lax.broadcasted_iota(jnp.int32, (size, size), 1)

    def polynomial():
        gram = gram_ref[...]
        poly_ref[...] = coef_second * gram + coef_third * symmetric_product(gram, gram)

    def inner(index, carry):
        poly = poly_ref[...]
        gram = gram_ref[...]
        step = coef_first * gram + symmetric_product(poly, gram)
        gram_ref[...] = coef_first * step + symmetric_product(poly, step)
        polynomial()
        product = product_ref[...]
        product_ref[...] = coef_first * product + symmetric_product(poly_ref[...], product)
        return carry

    def outer(inner_steps):
        if tall:
            both = mxu(high_ref[...], jnp.concatenate([high_ref[...], low_ref[...]], axis=1), TN)
        else:
            both = mxu(high_ref[...], jnp.concatenate([high_ref[...], low_ref[...]], axis=0), NT)
        crossing = both[:, size:]
        gram_ref[...] = both[:, :size] + crossing + crossing.T
        polynomial()
        product_ref[...] = poly_ref[...] + jnp.where(row == column, coef_first, 0.0)
        if isinstance(inner_steps, int) and inner_steps == 0:
            pass
        else:
            lax.fori_loop(0, inner_steps, inner, 0)
        high, low = two_parts(product_ref[...])
        if tall:
            right = jnp.concatenate([high, high, low], axis=0)
            for start in range(0, length, block):
                at = slice(start, start + block)
                left = jnp.concatenate([high_ref[at], low_ref[at], high_ref[at]], axis=1)
                high_ref[at], low_ref[at] = two_parts(mxu(left, right))
        else:
            left = jnp.concatenate([high, high, low], axis=1)
            for start in range(0, length, block):
                at = slice(start, start + block)
                right = jnp.concatenate([high_ref[:, at], low_ref[:, at], high_ref[:, at]], axis=0)
                high_ref[:, at], low_ref[:, at] = two_parts(mxu(left, right))

    if all(count == 1 for count in plan):
        lax.fori_loop(0, len(plan), lambda index, carry: (outer(0), carry)[1], 0)
    else:
        lax.fori_loop(0, len(plan), lambda index, carry: (outer(plan[0] - 1 - index), carry)[1], 0)


def inverse_norm(values):
    return 1.0 / (jnp.sqrt(jnp.full((1, 1), values, f32)) + 1e-07)


def muon_scratch(shape, size):
    return [pltpu.VMEM(shape, bf16), pltpu.VMEM(shape, bf16)] + [pltpu.VMEM((size, size), f32)] * 3


def muon_feed_kernel(numbers, place_ref, sum_ref, own_state_ref, other_state_ref, direction_ref, moment, high, low, gram, poly, product):
    me = place_ref[4]
    held, _ = own_state_ref.shape
    count = len(numbers) // 2
    rows = held // count
    total = jnp.zeros((1, 512), f32)
    for index, number in enumerate(numbers):
        state_ref = own_state_ref if index < count else other_state_ref
        start = pl.multiple_of(jnp.bitwise_xor(number % count, me) * rows, rows)
        state = state_ref[pl.ds(start, rows), :].astype(f32)
        value = momentum_keep * state + sum_ref[index, 0:rows].astype(f32)
        moment[pl.ds(start + (0 if index < count else held), rows), :] = value
        total += jnp.sum(value * value, axis=0, keepdims=True)
    muon_load(high, low, moment, inverse_norm(jnp.sum(total)), True)
    muon_iterate(True, (3, 2), high, low, gram, poly, product)
    for start in range(0, held, 256):
        at = slice(start, start + 256)
        direction_ref[at] = high[at]


def muon_feed(place, sums, own_state, other_state, numbers):
    held, width = own_state.shape
    vmem = pl.BlockSpec(memory_space=pltpu.VMEM)
    return pl.pallas_call(
        functools.partial(muon_feed_kernel, numbers),
        in_specs=[pl.BlockSpec(memory_space=pltpu.SMEM)] + [vmem] * 3,
        out_specs=vmem,
        out_shape=jax.ShapeDtypeStruct((held, width), bf16),
        scratch_shapes=[pltpu.VMEM((2 * held, width), f32)] + muon_scratch((2 * held, width), width),
        compiler_params=pltpu.CompilerParams(vmem_limit_bytes=vmem_bytes),
        cost_estimate=pl.CostEstimate(flops=26 * 10**9, bytes_accessed=8 * 10**6, transcendentals=0),
        name="muon_feed",
    )(place, sums, own_state, other_state)


def muon_qkv_kernel(numbers, rate, place_ref, sum_ref, swapped_ref, state_ref, weight_ref, moment_ref, updated_ref, high, low, gram, poly, product):
    me = place_ref[3]
    rows = sum_ref.shape[1]
    total = jnp.zeros((1, state_ref.shape[1]), f32)
    for core_place, ref in enumerate((sum_ref, swapped_ref)):
        for index, number in enumerate(numbers):
            number += core_place * len(numbers)
            start = pl.multiple_of(jnp.bitwise_xor(number, me) * rows, rows)
            value = momentum_keep * state_ref[pl.ds(start, rows), :] + ref[index, :, 0 : state_ref.shape[1]].astype(f32)
            moment_ref[pl.ds(start, rows), :] = value
            total += jnp.sum(value * value, axis=0, keepdims=True)
    muon_load(high, low, moment_ref, inverse_norm(jnp.sum(total)), False)
    muon_iterate(False, (3, 2), high, low, gram, poly, product)
    for start in range(0, weight_ref.shape[0], 64):
        at = slice(start, start + 64)
        updated_ref[at] = weight_ref[at] - rate * (high[at].astype(f32) + low[at].astype(f32))


def muon_qkv(place, sums, swapped, state, weight, numbers, rate):
    vmem = pl.BlockSpec(memory_space=pltpu.VMEM)
    shape = jax.ShapeDtypeStruct(state.shape, f32)
    return pl.pallas_call(
        functools.partial(muon_qkv_kernel, numbers, rate),
        in_specs=[pl.BlockSpec(memory_space=pltpu.SMEM)] + [vmem] * 4,
        out_specs=[vmem] * 2,
        out_shape=[shape, shape],
        scratch_shapes=muon_scratch(state.shape, state.shape[0]),
        compiler_params=pltpu.CompilerParams(vmem_limit_bytes=vmem_bytes),
        cost_estimate=pl.CostEstimate(flops=20 * 10**9, bytes_accessed=16 * 10**6, transcendentals=0),
        name="muon_qkv",
    )(place, sums, swapped, state, weight)


def muon_out_kernel(rate, moment_ref, weight_ref, updated_ref, high, low, gram, poly, product):
    moment = moment_ref[...]
    muon_load(high, low, moment_ref, inverse_norm(jnp.sum(moment * moment)), False)
    muon_iterate(False, (1, 1, 1, 1, 1), high, low, gram, poly, product)
    updated_ref[...] = weight_ref[...] - rate * (high[...].astype(f32) + low[...].astype(f32))


def muon_out(moment, weight, rate):
    vmem = pl.BlockSpec(memory_space=pltpu.VMEM)
    return pl.pallas_call(
        functools.partial(muon_out_kernel, rate),
        in_specs=[vmem] * 2,
        out_specs=vmem,
        out_shape=jax.ShapeDtypeStruct(weight.shape, f32),
        scratch_shapes=muon_scratch(weight.shape, weight.shape[0]),
        compiler_params=pltpu.CompilerParams(vmem_limit_bytes=vmem_bytes),
        cost_estimate=pl.CostEstimate(flops=14 * 10**9, bytes_accessed=3 * 10**6, transcendentals=0),
        name="muon_out",
    )(moment, weight)


def feed_moments_kernel(numbers, place_ref, own_ref, swapped_ref, up_state_ref, down_state_ref, up_ref, down_ref, up_sum):
    me = place_ref[4]
    core = place_ref[0]
    count, rows, _ = own_ref.shape

    def write(up_from, down_from):
        for index, number in enumerate(numbers):
            start = pl.multiple_of(jnp.bitwise_xor(number, me) * rows, rows)
            at = pl.ds(start, rows)
            up_sum[at, :] = up_from[index].astype(f32)
            down_ref[at, :] = momentum_keep * down_state_ref[at, :] + down_from[index].astype(f32)

    @pl.when(core == 0)
    def _():
        write(own_ref, swapped_ref)

    @pl.when(core == 1)
    def _():
        write(swapped_ref, own_ref)

    for start in range(0, up_sum.shape[0], 256):
        at = slice(start, start + 256)
        up_ref[:, at] = momentum_keep * up_state_ref[:, at] + up_sum[at].T


def feed_moments(place, own, swapped, up_state, down_state, numbers):
    vmem = pl.BlockSpec(memory_space=pltpu.VMEM)
    return pl.pallas_call(
        functools.partial(feed_moments_kernel, numbers),
        in_specs=[pl.BlockSpec(memory_space=pltpu.SMEM)] + [vmem] * 4,
        out_specs=[vmem] * 2,
        out_shape=[jax.ShapeDtypeStruct(up_state.shape, f32), jax.ShapeDtypeStruct(down_state.shape, f32)],
        scratch_shapes=[pltpu.VMEM(down_state.shape, f32)],
        compiler_params=pltpu.CompilerParams(vmem_limit_bytes=vmem_bytes),
        cost_estimate=pl.CostEstimate(flops=10**6, bytes_accessed=10 * 10**6, transcendentals=0),
        name="feed_moments",
    )(place, own, swapped, up_state, down_state)


def feed_update_kernel(rate_first, rate_second, place_ref, own_ref, swapped_ref, up_weight_ref, down_weight_ref, up_ref, down_ref):
    core = place_ref[0]

    def write(up_from, down_from):
        down_ref[...] = down_weight_ref[...] - rate_second * down_from[...].astype(f32)
        for start in range(0, up_from.shape[0], 256):
            at = slice(start, start + 256)
            up_ref[:, at] = up_weight_ref[:, at] - rate_first * up_from[at].astype(f32).T

    @pl.when(core == 0)
    def _():
        write(own_ref, swapped_ref)

    @pl.when(core == 1)
    def _():
        write(swapped_ref, own_ref)


def feed_update(place, own, swapped, up_weight, down_weight, rate_first, rate_second):
    vmem = pl.BlockSpec(memory_space=pltpu.VMEM)
    return pl.pallas_call(
        functools.partial(feed_update_kernel, rate_first, rate_second),
        in_specs=[pl.BlockSpec(memory_space=pltpu.SMEM)] + [vmem] * 4,
        out_specs=[vmem] * 2,
        out_shape=[jax.ShapeDtypeStruct(up_weight.shape, f32), jax.ShapeDtypeStruct(down_weight.shape, f32)],
        compiler_params=pltpu.CompilerParams(vmem_limit_bytes=vmem_bytes),
        cost_estimate=pl.CostEstimate(flops=10**6, bytes_accessed=10 * 10**6, transcendentals=0),
        name="feed_update",
    )(place, own, swapped, up_weight, down_weight)


def step_factor(rows, columns):
    return math.sqrt(max(1.0, rows / columns))


def on_device(
    dp_size, mp_size,
    atoms, atom_counts, hydrogen, atom_types, cotangent, qkv_weight, out_weight, up_weight, down_weight, ffn_bias, norm_params,
    pair_table, qkv_state, out_state, up_state, down_state, bias_state, norm_state, pair_state,
):
    sizes = {"dp": dp_size, "mp": mp_size}
    place_dp, place_mp = lax.axis_index("dp"), lax.axis_index("mp")
    places = {"dp": place_dp, "mp": place_mp}
    core = place_dp & 1
    dp_bits = dp_size.bit_length() - 1
    mols, half, width = atoms.shape
    mine = mols // 2
    slots = 2 * half
    types_count, _, head_count = pair_table.shape
    kinds = 32

    def mine_of(array, which):
        return lax.dynamic_slice_in_dim(array, which * mine, mine, 0)

    def other_slots(array):
        return swap(mine_of(array, 1 - place_mp), "mp", 0, mp_size)

    atoms_own, atoms_other = mine_of(atoms, place_mp), other_slots(atoms)
    up_own = up_weight.T.astype(bf16)
    down_own = down_weight.astype(bf16)
    cot_own, cot_other = mine_of(cotangent, place_mp), other_slots(cotangent)
    leaving, cot_other = lax.optimization_barrier((jnp.where(core == 0, up_own, down_own), cot_other))
    crossed = swap(leaving, "mp", 0, mp_size)
    bias_other = swap(ffn_bias, "mp", 0, mp_size)
    bias_rel = jnp.concatenate([ffn_bias, bias_other])[None]

    def local_order(array):
        return jnp.where(place_mp == 0, array, jnp.roll(array, half, axis=1))

    counts = mine_of(atom_counts, place_mp)
    slot_ids = (jnp.arange(slots) + place_mp * half) % slots
    present = slot_ids[None, :] < counts[:, None]
    ok = present & (local_order(mine_of(hydrogen, place_mp)) == 0)
    local_types = local_order(mine_of(atom_types, place_mp))
    types = (local_types[..., None] == jnp.arange(kinds)).astype(bf16)
    type_t = (local_types[:, None, :] == jnp.arange(kinds)[:, None]).astype(bf16)
    valid = present.astype(f32)[..., None]

    table = lax.reduce_precision(pair_table, 8, 7) * log2_e
    table = jnp.pad(table, ((0, kinds - types_count), (0, kinds - types_count), (0, 0))).transpose(2, 1, 0)
    table_high = lax.reduce_precision(table, 8, 7)
    table_rows = jnp.concatenate([table_high, table - table_high], axis=1).astype(bf16).reshape(head_count * 2 * kinds, kinds)

    (probs, read_t, query_t, key_t, values, normed_t, attended_t, middle, normed_two, own_state, leaving_state) = attend(
        atoms_own, atoms_other, qkv_weight, norm_params, table_rows, type_t, types, ok.astype(f32)[..., None], valid, out_weight,
        core[None].astype(jnp.int32), up_state, down_state,
    )

    crossed, normed_two = lax.optimization_barrier((crossed, normed_two))
    crossed_again = swap(crossed, "dp", 0, dp_size)
    other_state = swap(leaving_state, "mp", 0, mp_size)

    core_digit = ("dp", 0)
    half_digits = [("dp", bit) for bit in range(dp_bits - 1, 0, -1)]
    half_pieces = dp_size // 2
    chip_digits = [("mp", 0)] + half_digits
    some_digits = chip_digits[-4:]
    plain_digits = chip_digits[:-4]
    pieces = 2 ** (1 + len(some_digits))
    half_place = place_dp >> 1
    some_place = (place_mp * half_pieces + half_place) & (pieces // 2 - 1)
    piece_rows = up_own.shape[0] // half_pieces
    place = jnp.stack([core, core, some_place, core * (pieces // 2) + some_place, half_place]).astype(jnp.int32)

    rows = mine * slots
    (keep, send, bias_grad, mixed, middle_grad, attended_grad_t, out_grad, norm_grad_two) = feed(
        place, normed_two.reshape(rows, width), middle.reshape(rows, width), cot_own, cot_other, valid.reshape(rows, 1), attended_t,
        norm_params, out_weight, up_own, down_own, crossed, crossed_again, bias_rel, half_pieces,
    )
    out_sum = lax.psum(out_grad, ("dp", "mp"))

    early = add_low(keep, swap(send, "dp", 0, dp_size)).reshape((2,) * len(chip_digits) + (piece_rows, width))
    early_ends, early_both = scatter_ends(early, chip_digits, sizes)

    def corner(*arrays):
        return jnp.stack([array[(0,) * (array.ndim - 2)][:16, :128] for array in arrays])

    groups = values.shape[1]
    calls = 4
    waits = [corner(other_state), corner(early), corner(early), corner(*early_ends), corner(early_both)]
    parts = [
        attend_back(i * groups // calls, groups // calls, probs, attended_grad_t, read_t, values, key_t, query_t, type_t, waits[i])
        for i in range(calls)
    ]
    bias_grad = bias_grad.reshape(2, -1)
    bias_grad = jnp.where(place_mp == 0, bias_grad, bias_grad[::-1]).reshape(-1, width)
    tiny = jnp.concatenate([norm_grad_two, bias_grad], axis=0)
    late_keep, late_send, atoms_grad_own, atoms_grad_other = project_back(
        place, parts, normed_t, qkv_weight, atoms_own, atoms_other, middle_grad, norm_params, tiny, waits[4], pieces
    )

    early_sum = gather(scatter_middle(early_both, chip_digits, sizes, late_keep), chip_digits, sizes)
    early_order = gather_order(chip_digits)
    early_sum = early_sum.reshape((2 * half_pieces, piece_rows, width))

    late = add_low(late_keep, swap(late_send, "dp", 0, dp_size))
    late_shape = late.shape
    _, late_both = scatter_ends(late.reshape((2,) * len(some_digits) + late_shape[1:]), some_digits, sizes)
    late_both = scatter_middle(late_both, some_digits, sizes)
    for axis, bit in plain_digits:
        late_both = add_low(late_both, swap(late_both, axis, bit, sizes[axis]))
    late_sum = gather(late_both, some_digits, sizes).reshape(late_shape)

    def back_slots(own, other, after):
        other, _ = lax.optimization_barrier((other, after))
        moved = swap(other, "mp", 0, mp_size).astype(own.dtype)
        return jnp.where(place_mp == 0, jnp.concatenate([own, moved], 0), jnp.concatenate([moved, own], 0))

    mixed = mixed.reshape(mine, slots, width)
    mixed_out = back_slots(mixed[:, :half], mixed[:, half:], early_sum)
    atoms_grad = back_slots(atoms_grad_own, atoms_grad_other, early_sum)

    late_swapped = swap(late_sum, "dp", 0, dp_size)
    late_numbers = place_list(gather_order(some_digits), some_digits)
    qkv_moment, qkv_updated = muon_qkv(
        place, late_sum, late_swapped, qkv_state, qkv_weight, late_numbers, rate_qkv * step_factor(*qkv_weight.shape)
    )

    order = gather_order(some_digits)
    small = jnp.stack([late_sum[..., 3 * width :], late_swapped[..., 3 * width :]])
    small = absolute(small.reshape((2,) * (1 + len(order)) + small.shape[2:]), [core_digit] + order, places)
    spots = (0,) + tuple(1 + order.index(digit) for digit in some_digits)
    small = small.transpose(spots + (len(spots), len(spots) + 1)).reshape(kinds, width // kinds, 256).astype(f32)
    pair_sum = small[..., :128].reshape(kinds, head_count, kinds).transpose(0, 2, 1)[:types_count, :types_count]
    vectors = small[..., 128:136].reshape(width, 8).T
    norm_sum = vectors[:4]
    bias_sum = lax.dynamic_slice_in_dim(vectors[4:].reshape(-1), place_mp * ffn_bias.shape[0], ffn_bias.shape[0], 0)

    norm_moment = momentum_keep * norm_state + norm_sum
    norm_updated = norm_params - rate_norm * norm_moment
    bias_moment = momentum_keep * bias_state + bias_sum
    bias_updated = ffn_bias - rate_bias * bias_moment
    pair_moment = momentum_keep * pair_state + pair_sum
    pair_updated = pair_table - rate_pair * pair_moment

    hidden_units = mp_size * up_weight.shape[1]
    own_sum = early_sum[:half_pieces]
    own_numbers = place_list(early_order[1:], half_digits)
    up_moment, down_moment = feed_moments(place, own_sum, swap(own_sum, "dp", 0, dp_size), up_state, down_state, own_numbers)
    direction = muon_feed(place, early_sum, own_state, other_state, place_list(early_order, chip_digits))
    out_sum, _ = lax.optimization_barrier((out_sum, direction))
    out_moment = momentum_keep * out_state + out_sum
    out_updated = muon_out(out_moment, out_weight, rate_out * step_factor(*out_weight.shape))
    up_updated, down_updated = feed_update(
        place, direction, swap(direction, "dp", 0, dp_size), up_weight, down_weight,
        rate_up * step_factor(width, hidden_units), rate_down * step_factor(hidden_units, width),
    )
    return (
        mixed_out,
        atoms_grad,
        qkv_moment,
        qkv_updated,
        out_moment,
        out_updated,
        up_moment,
        up_updated,
        down_moment,
        down_updated,
        bias_moment,
        bias_updated,
        norm_moment,
        norm_updated,
        pair_moment,
        pair_updated,
    )


def solution(mesh):
    rows = P("dp", "mp", None)
    in_specs = (
        rows, P("dp"), P("dp", None), P("dp", None), rows, P(), P(), P(None, "mp"), P("mp", None), P("mp"), P(), P(),
        P(), P(), P(None, "mp"), P("mp", None), P("mp"), P(), P(),
    )
    out_specs = (
        rows, rows, P(), P(), P(), P(), P(None, "mp"), P(None, "mp"), P("mp", None), P("mp", None), P("mp"), P("mp"),
        P(), P(), P(), P(),
    )
    body = functools.partial(on_device, mesh.shape["dp"], mesh.shape["mp"])
    return jax.shard_map(body, mesh=mesh, in_specs=in_specs, out_specs=out_specs, check_vma=False)
```

```python
import functools
import math

import jax
import jax.numpy as jnp
from jax import lax
from jax.experimental import pallas as pl
from jax.experimental.pallas import tpu as pltpu
from jax.sharding import PartitionSpec as P

norm_eps = 1e-05
masked_score = -1000000000.0
coef_first = 3.4445
coef_second = -4.775
coef_third = 2.0315
momentum_keep = 0.5
rate_qkv = 1.0
rate_out = 4.0
rate_up = 1.0
rate_down = 1.0
rate_norm = 0.001
rate_bias = 0.01
rate_pair = 0.05

bf16 = jnp.bfloat16
f32 = jnp.float32
log2_e = 1.4426950408889634
NN = (((1,), (0,)), ((), ()))
NT = (((1,), (1,)), ((), ()))
TN = (((0,), (0,)), ((), ()))
vmem_bytes = 56 * 2**20


def mxu(left, right, dims=NN):
    return lax.dot_general(left, right, dims, preferred_element_type=f32)


def norm_parts(values):
    center = values - jnp.mean(values, axis=-1, keepdims=True)
    inverse = lax.rsqrt(jnp.mean(center * center, axis=-1, keepdims=True) + norm_eps)
    return center * inverse, inverse


def norm_back(grad_rows, unit_rows, inverse, gain_vec):
    scaled = grad_rows * gain_vec
    mean_one = jnp.mean(scaled, axis=-1, keepdims=True)
    mean_two = jnp.mean(scaled * unit_rows, axis=-1, keepdims=True)
    return inverse * (scaled - mean_one - unit_rows * mean_two)


def two_parts(values):
    high = values.astype(bf16)
    return high, (values - high.astype(f32)).astype(bf16)


def attend_kernel(
    groups, state_steps, scalar_ref, own_ref, other_ref, qkv_w_ref, norm_ref, table_ref, type_all_ref, hydrogen_ref, out_w_ref,
    up_state_ref, down_state_ref,
    prob_ref, read_t_ref, query_t_ref, key_t_ref, value_ref, normed_t_ref, attended_t_ref, middle_ref, normed_two_ref,
    own_state_ref, leaving_ref, type_t_ref, valid_ref,
    left_all, query_high, query_low, value_t, bias_all, cap, read_all, qkv_low,
):
    group = pl.program_id(1)
    core, side = scalar_ref[0], scalar_ref[1]
    molecule = side * pl.num_programs(0) + pl.program_id(0)
    count = scalar_ref[2 + molecule]
    slots = prob_ref.shape[2]
    width = own_ref.shape[2]
    half = slots // 2
    span = width // groups
    heads = prob_ref.shape[1]
    kinds = type_t_ref.shape[1]

    def slot_row(ref):
        row = ref[pl.ds(molecule, 1), :].astype(f32)
        turned = jnp.concatenate([row[:, half:], row[:, :half]], axis=1)
        second = side.astype(f32)
        return row * (1.0 - second) + turned * second

    def load_rows():
        return jnp.concatenate([own_ref[0], other_ref[0]], axis=0).astype(f32)

    @pl.when((group == 0) & (pl.program_id(0) == 0))
    def _():
        qkv_low[...] = qkv_w_ref[...].astype(bf16)

    @pl.when(group == 0)
    def _():
        unit, _ = norm_parts(load_rows())
        normed = unit * norm_ref[0:1] + norm_ref[1:2]
        normed_t_ref[0] = normed.T.astype(bf16)
        normed = normed.astype(bf16)
        query = mxu(normed, qkv_low[:, 0:width]).T.astype(bf16)
        query_t_ref[0] = query
        keys = mxu(normed, qkv_low[:, width : 2 * width])
        key_t_ref[0] = keys.T.astype(bf16)
        keys = keys.astype(bf16)
        values = mxu(normed, qkv_low[:, 2 * width :])
        value_t[...] = values.T.astype(bf16)
        values = values.astype(bf16)
        head_width = span // heads
        scaled = query.astype(f32) * (head_width**-0.5 * log2_e)
        high = scaled.astype(bf16).astype(f32)
        query_high[...] = high
        query_low[...] = scaled - high
        slot = lax.broadcasted_iota(jnp.int32, (1, slots), 1) + side * half
        slot = jnp.where(slot >= slots, slot - slots, slot)
        present = jnp.where(slot < count, 1.0, 0.0)
        usable = jnp.where(slot_row(hydrogen_ref) == 0.0, present, 0.0)
        line = lax.broadcasted_iota(jnp.int32, (128, slots), 0)
        marks = jnp.where(line.astype(f32) == slot_row(type_all_ref), 1.0, 0.0)
        marks = jnp.where(line == kinds, usable, jnp.where(line == kinds + 1, present, marks))
        columns = marks.T
        type_rows = marks[0:kinds].astype(bf16)
        type_t_ref[0] = type_rows
        type_columns = columns[:, 0:kinds].astype(bf16)
        valid = columns[:, kinds + 1 : kinds + 2]
        valid_ref[0] = valid
        bias_all[...] = mxu(table_ref[...], type_rows).astype(bf16)
        blank = jnp.zeros((slots, 256 - 2 * span - 2 * kinds), bf16)
        for index in range(groups):
            part = keys[:, span * index : span * (index + 1)]
            left_all[index] = jnp.concatenate([part, part, type_columns, type_columns, blank], axis=1)
            value_ref[0, index] = values[:, span * index : span * (index + 1)]
        row = lax.broadcasted_iota(jnp.int32, (slots, slots), 0)
        column = lax.broadcasted_iota(jnp.int32, (slots, slots), 1)
        cap[...] = jnp.where((columns[:, kinds : kinds + 1] > 0.0) | (row == column), 3e38, masked_score * log2_e)

    step = pl.program_id(0) * groups + group
    early = step < state_steps

    def keep_state(state):
        own_state_ref[...] = state
        leaving_ref[...] = state.astype(bf16)

    @pl.when(early & (core == 0))
    def _():
        keep_state(up_state_ref[...].T)

    @pl.when(early & (core == 1))
    def _():
        keep_state(down_state_ref[...])

    left = left_all[group]
    owner = lax.broadcasted_iota(jnp.int32, (span, slots), 0) // (span // heads)
    start = pl.multiple_of(group * span, span)
    high = query_high[pl.ds(start, span), :]
    low = query_low[pl.ds(start, span), :]
    zero = jnp.zeros_like(high)
    blank = jnp.zeros((256 - 2 * span - 2 * kinds, slots), bf16)

    def scores(head):
        mine = owner == head
        place = pl.multiple_of((group * heads + head) * 2 * kinds, 2 * kinds)
        bias = bias_all[pl.ds(place, 2 * kinds), :]
        parts = [jnp.where(mine, high, zero).astype(bf16), jnp.where(mine, low, zero).astype(bf16), bias, blank]
        return mxu(left, jnp.concatenate(parts, axis=0))

    def softmax(head, logits):
        logits = jnp.minimum(logits, cap[...])
        raised = jnp.exp2(logits - jnp.max(logits, axis=0, keepdims=True))
        low_probs = (raised * (1.0 / jnp.sum(raised, axis=0, keepdims=True))).astype(bf16)
        prob_ref[0, head] = low_probs
        return low_probs

    def weigh(head, low_probs):
        pair = value_t[pl.ds(pl.multiple_of(group * span + (head // 2) * 16, 16), 16), :]
        both = mxu(pair, low_probs)
        return both[0:8] if head % 2 == 0 else both[8:16]

    ahead = 3
    waiting = [scores(head) for head in range(ahead)]
    probs, results = [], []
    for head in range(heads):
        probs.append(softmax(head, waiting[head]))
        if head + ahead < heads:
            waiting.append(scores(head + ahead))
        if head:
            results.append(weigh(head - 1, probs[head - 1]))
    results.append(weigh(heads - 1, probs[heads - 1]))
    read = jnp.concatenate(results, axis=0)
    read_t_ref[0] = read
    read_all[pl.ds(start, span), :] = read.astype(bf16)

    @pl.when(group == groups - 1)
    def _():
        attended = read_all[...]
        attended_t_ref[0] = attended
        middle = load_rows() + valid_ref[0] * mxu(attended, out_w_ref[...].astype(bf16), TN)
        middle_ref[0] = middle
        unit, _ = norm_parts(middle)
        normed_two_ref[0] = (unit * norm_ref[2:3] + norm_ref[3:4]).astype(bf16)


def attend(scalars, atoms, other, qkv_w, norms, table, types, hydrogen, out_w, up_state, down_state):
    mols, half, width = other.shape
    slots = 2 * half
    groups = 8
    heads = width // 8 // groups
    kinds = 32
    span = width // groups
    whole = lambda a: pl.BlockSpec(a.shape, lambda m, g, s: (0,) * a.ndim)
    each = lambda *shape: pl.BlockSpec((1,) + shape, lambda m, g, s: (m,) + (0,) * len(shape))
    state_steps = mols * groups // 2
    state_rows = down_state.shape[0] // state_steps
    state_at = lambda m, g: jnp.minimum(m * groups + g, state_steps - 1)
    state_block = pl.BlockSpec((state_rows, width), lambda m, g, s: (state_at(m, g), 0))
    shape = jax.ShapeDtypeStruct
    rows = shape((mols, width, slots), bf16)
    return pl.pallas_call(
        functools.partial(attend_kernel, groups, state_steps),
        grid_spec=pltpu.PrefetchScalarGridSpec(
            num_scalar_prefetch=1,
            grid=(mols, groups),
            in_specs=[pl.BlockSpec((1, half, width), lambda m, g, s: (s[1] * mols + m, 0, 0)), each(half, width), whole(qkv_w),
                      whole(norms), whole(table), whole(types), whole(hydrogen), whole(out_w),
                      pl.BlockSpec((width, state_rows), lambda m, g, s: (0, state_at(m, g))), state_block],
            out_specs=[pl.BlockSpec((1, heads, slots, slots), lambda m, g, s: (m, g, 0, 0)),
                       pl.BlockSpec((1, span, slots), lambda m, g, s: (m, g, 0)),
                       each(width, slots), each(width, slots), each(groups, slots, span), each(width, slots), each(width, slots),
                       each(slots, width), each(slots, width), state_block, state_block, each(kinds, slots), each(slots, 1)],
            scratch_shapes=[pltpu.VMEM((groups, slots, 256), bf16), pltpu.VMEM((width, slots), f32), pltpu.VMEM((width, slots), f32),
                            pltpu.VMEM((width, slots), bf16), pltpu.VMEM((table.shape[0], slots), bf16), pltpu.VMEM((slots, slots), f32),
                            pltpu.VMEM((width, slots), bf16), pltpu.VMEM(qkv_w.shape, bf16)],
        ),
        out_shape=[shape((mols, groups * heads, slots, slots), bf16), shape((mols, width, slots), f32), rows, rows,
                   shape((mols, groups, slots, span), bf16), rows, rows, shape((mols, slots, width), f32),
                   shape((mols, slots, width), bf16), shape(down_state.shape, f32), shape(down_state.shape, bf16),
                   shape((mols, kinds, slots), bf16), shape((mols, slots, 1), f32)],
        compiler_params=pltpu.CompilerParams(vmem_limit_bytes=vmem_bytes),
        cost_estimate=pl.CostEstimate(flops=22 * 10**9, bytes_accessed=24 * 10**6, transcendentals=8 * 10**6),
        name="attend",
    )(scalars, atoms, other, qkv_w, norms, table, types, hydrogen, out_w, up_state, down_state)


def feed_kernel(
    piece_rows, out_rows,
    place_ref, normed_ref, middle_ref, own_grad_ref, other_grad_ref, valid_ref, attended_t_ref, norm_ref, out_w_ref,
    up_own_ref, down_own_ref, first_ref, second_ref, bias_ref,
    keep_ref, send_ref, bias_grad_ref, mixed_ref, middle_grad_ref, attended_grad_t_ref, out_grad_ref, norm_grad_ref,
    rows_grad, sum_out, sum_back, up_used, down_used, out_low, *ordered,
):
    step = pl.program_id(0)
    steps = pl.num_programs(0)
    core = place_ref[0]
    me = place_ref[4]
    mols, half, width = other_grad_ref.shape
    rows = mols * 2 * half

    def given():
        return jnp.concatenate([part for m in range(mols) for part in (own_grad_ref[m], other_grad_ref[m])], axis=0)

    @pl.when(step == 0)
    def _():
        rows_grad[...] = (valid_ref[...] * given().astype(f32)).astype(bf16)
        out_low[...] = out_w_ref[...].astype(bf16)
        sum_out[...] = jnp.zeros_like(sum_out)
        sum_back[...] = jnp.zeros_like(sum_back)

    is_own = step < steps // 2

    def choose(condition, up_ref, down_ref):
        @pl.when(condition)
        def _():
            up_used[...] = up_ref[...]
            down_used[...] = down_ref[...]

    choose(is_own, up_own_ref, down_own_ref)
    choose(jnp.logical_not(is_own) & (core == 0), first_ref, second_ref)
    choose(jnp.logical_not(is_own) & (core == 1), second_ref, first_ref)
    up = up_used[...]
    down = down_used[...]
    normed = normed_ref[...]
    grads = rows_grad[...]
    hidden = mxu(normed, up, NT) + bias_ref[...]
    back = mxu(grads, down, NT)
    cumulative = 0.5 * (1.0 + lax.erf(hidden * 0.7071067811865476))
    activated = (hidden * cumulative).astype(bf16)
    slope = cumulative + hidden * jnp.exp(-0.5 * hidden * hidden) * 0.3989422804014327
    hidden_grad = (back * slope).astype(bf16)
    sum_out[...] += mxu(activated, down)
    sum_back[...] += mxu(hidden_grad, up)
    up_grad = mxu(hidden_grad, normed, TN).astype(bf16)
    down_grad = mxu(activated, grads, TN).astype(bf16)
    bias_grad_ref[...] = jnp.sum(hidden_grad.astype(f32), axis=0, keepdims=True)
    place_half = step // (steps // 2)
    first_piece = step % (steps // 2) * (up.shape[0] // piece_rows)

    def place_rows(kept, sent):
        for piece in range(up.shape[0] // piece_rows):
            at = jnp.bitwise_xor(first_piece + piece, me)
            keep_ref[place_half, at, 0:piece_rows] = kept[piece * piece_rows : (piece + 1) * piece_rows]
            send_ref[place_half, at, 0:piece_rows] = sent[piece * piece_rows : (piece + 1) * piece_rows]

    @pl.when(core == 0)
    def _():
        place_rows(up_grad, down_grad)

    @pl.when(core == 1)
    def _():
        place_rows(down_grad, up_grad)

    @pl.when(step == steps - 1)
    def _():
        middle = middle_ref[...]
        valid = valid_ref[...]
        mixed_ref[...] = (middle + valid * sum_out[...]).astype(bf16)
        unit, inverse = norm_parts(middle)
        grad_two = sum_back[...]
        norm_grad_ref[0:1] = jnp.sum(grad_two * unit, axis=0, keepdims=True)
        norm_grad_ref[1:2] = jnp.sum(grad_two, axis=0, keepdims=True)
        middle_grad = given().astype(f32) + norm_back(grad_two, unit, inverse, norm_ref[2:3])
        middle_grad_ref[...] = middle_grad
        branch_grad = (valid * middle_grad).astype(bf16)
        total = None
        for m in range(mols):
            part = branch_grad[m * 2 * half : (m + 1) * 2 * half]
            attended_grad_t_ref[m] = mxu(out_low[...], part, NT).astype(bf16)
            term = mxu(attended_t_ref[m], part)
            total = term if total is None else total + term
        out_grad_ref[...] = total
        if out_rows:
            half_pieces = keep_ref.shape[1]
            count = 2 * half_pieces
            for piece in range(2 * count):
                ordered[0][piece] = total[piece * out_rows : (piece + 1) * out_rows]
            for piece in range(count):
                at = jnp.bitwise_xor(piece, place_ref[5])
                spot = (at // half_pieces, at % half_pieces, slice(piece_rows, piece_rows + out_rows))
                keep_ref[spot] = ordered[0][core * count + piece].astype(bf16)
                send_ref[spot] = ordered[0][(1 - core) * count + piece].astype(bf16)


def feed(place, normed, middle, own_grad, other_grad, valid, attended_t, norms, out_w, up_own, down_own, first, second, bias,
         half_pieces, out_rows):
    mols, half, width = other_grad.shape
    rows = mols * 2 * half
    held = up_own.shape[0]
    block = 256
    per_half = held // block
    steps = 2 * per_half
    piece_rows = held // half_pieces
    whole = lambda a: pl.BlockSpec(a.shape, lambda j, s: (0,) * a.ndim)
    fixed = lambda *s: pl.BlockSpec(s, lambda j, s_: (0,) * len(s))
    mine = pl.BlockSpec((block, width), lambda j, s: (jnp.minimum(j, per_half - 1), 0))
    theirs = pl.BlockSpec((block, width), lambda j, s: (jnp.maximum(j - per_half, 0), 0))
    shape = jax.ShapeDtypeStruct
    return pl.pallas_call(
        functools.partial(feed_kernel, piece_rows, out_rows),
        grid_spec=pltpu.PrefetchScalarGridSpec(
            num_scalar_prefetch=1,
            grid=(steps,),
            in_specs=[whole(normed), whole(middle), pl.BlockSpec((mols, half, width), lambda j, s: (s[1], 0, 0)), whole(other_grad), whole(valid), whole(attended_t),
                      whole(norms), whole(out_w), mine, mine, theirs, theirs, pl.BlockSpec((1, block), lambda j, s: (0, j))],
            out_specs=[fixed(2, half_pieces, piece_rows + out_rows, width), fixed(2, half_pieces, piece_rows + out_rows, width),
                       pl.BlockSpec((1, block), lambda j, s: (0, j)),
                       fixed(rows, width), fixed(rows, width), fixed(mols, width, 2 * half),
                       fixed(width, width), fixed(2, width)],
            scratch_shapes=[pltpu.VMEM((rows, width), bf16), pltpu.VMEM((rows, width), f32), pltpu.VMEM((rows, width), f32),
                            pltpu.VMEM((block, width), bf16), pltpu.VMEM((block, width), bf16), pltpu.VMEM(out_w.shape, bf16)]
                           + [pltpu.VMEM((4 * half_pieces, out_rows, width), f32)] * (out_rows > 0),
        ),
        out_shape=[shape((2, half_pieces, piece_rows + out_rows, width), bf16), shape((2, half_pieces, piece_rows + out_rows, width), bf16), shape((1, 2 * held), f32), shape((rows, width), bf16),
                   shape((rows, width), f32), shape((mols, width, 2 * half), bf16),
                   shape((width, width), f32), shape((2, width), f32)],
        compiler_params=pltpu.CompilerParams(vmem_limit_bytes=vmem_bytes),
        cost_estimate=pl.CostEstimate(flops=14 * 10**9, bytes_accessed=14 * 10**6, transcendentals=2 * 10**6),
        name="feed",
    )(place, normed, middle, own_grad, other_grad, valid, attended_t, norms, out_w, up_own, down_own, first, second, bias)


def score_kernel(
    prob_ref, grad_t_ref, read_t_ref, value_ref, key_t_ref, query_t_ref, type_t_ref, after_ref,
    query_grad_ref, key_grad_ref, value_grad_ref, pair_grad_ref,
):
    molecule = pl.program_id(1)
    heads, slots = prob_ref.shape[1], prob_ref.shape[2]
    span = grad_t_ref.shape[1]
    head_width = span // heads
    scale = head_width**-0.5
    values = value_ref[0, 0]
    grads = grad_t_ref[0]
    keys = key_t_ref[0]
    queries = query_t_ref[0]
    kinds = type_t_ref[0]
    count = kinds.shape[0]
    owner = lax.broadcasted_iota(jnp.int32, (span, slots), 0) // head_width
    wide_grads = grads.astype(f32)
    zero = jnp.zeros_like(wide_grads)
    dotted = wide_grads * read_t_ref[0]

    def pair_of(array, head):
        return array[(head // 2) * 16 : (head // 2) * 16 + 16]

    def own_half(both, head):
        return both[0:8] if head % 2 == 0 else both[8:16]

    def prob_grads(head):
        return mxu(values, jnp.where(owner == head, wide_grads, zero).astype(bf16))

    def score_grads(head, prob_grad):
        center = jnp.sum(dotted[head * head_width : (head + 1) * head_width], axis=0, keepdims=True)
        return (prob_ref[0, head].astype(f32) * (prob_grad - center)).astype(bf16)

    query_parts, key_parts, value_parts, type_parts = [], [], [], []

    def products(head, score_grad):
        left = jnp.concatenate([pair_of(keys, head), kinds], axis=0)
        both = mxu(left, score_grad)
        query_parts.append(own_half(both, head) * scale)
        type_parts.append(both[16:])
        key_parts.append(own_half(mxu(pair_of(queries, head), score_grad, NT), head) * scale)

    ahead = 3
    waiting = [prob_grads(head) for head in range(ahead)]
    done = []
    for head in range(heads):
        done.append(score_grads(head, waiting[head]))
        value_parts.append(own_half(mxu(pair_of(grads, head), prob_ref[0, head], NT), head))
        if head + ahead < heads:
            waiting.append(prob_grads(head + ahead))
        if head:
            products(head - 1, done[head - 1])
    products(heads - 1, done[heads - 1])
    query_grad_ref[0] = jnp.concatenate(query_parts, axis=0).astype(bf16)
    key_grad_ref[0] = jnp.concatenate(key_parts, axis=0).astype(bf16)
    value_grad_ref[0] = jnp.concatenate(value_parts, axis=0).astype(bf16)
    high, low = two_parts(jnp.concatenate(type_parts, axis=0))
    pairs = mxu(kinds, high, NT) + mxu(kinds, low, NT)

    @pl.when(molecule == 0)
    def _():
        pair_grad_ref[...] = pairs

    @pl.when(molecule > 0)
    def _():
        pair_grad_ref[...] += pairs


def attend_back(first, count, probs, grad_t, read_t, values, key_t, query_t, type_t, after):
    mols, all_heads, slots, _ = probs.shape
    groups = values.shape[1]
    heads = all_heads // groups
    width = grad_t.shape[1]
    span = width // groups
    kinds = type_t.shape[1]
    rows = pl.BlockSpec((1, span, slots), lambda g, m: (m, first + g, 0))
    new_rows = pl.BlockSpec((1, span, slots), lambda g, m: (m, g, 0))
    shape = jax.ShapeDtypeStruct
    part = shape((mols, count * span, slots), bf16)
    return pl.pallas_call(
        score_kernel,
        grid=(count, mols),
        in_specs=[pl.BlockSpec((1, heads, slots, slots), lambda g, m: (m, first + g, 0, 0)), rows, rows,
                  pl.BlockSpec((1, 1, slots, span), lambda g, m: (m, first + g, 0, 0)), rows, rows,
                  pl.BlockSpec((1, kinds, slots), lambda g, m: (m, 0, 0)), pl.BlockSpec(memory_space=pl.ANY)],
        out_specs=[new_rows, new_rows, new_rows, pl.BlockSpec((kinds, heads * kinds), lambda g, m: (0, g))],
        out_shape=[part, part, part, shape((kinds, count * heads * kinds), f32)],
        compiler_params=pltpu.CompilerParams(vmem_limit_bytes=vmem_bytes),
        cost_estimate=pl.CostEstimate(flops=5 * 10**9 * count, bytes_accessed=3 * 10**6 * count, transcendentals=0),
        name="attend_back",
    )(probs, grad_t, read_t, values, key_t, query_t, type_t, after)


def project_kernel(
    pieces, calls, place_ref, normed_t_ref, weight_ref, own_ref, other_ref, middle_grad_ref, norm_ref, tiny_ref, after_ref, *refs,
):
    part_refs, refs = refs[: 4 * calls], refs[4 * calls :]
    keep_ref, send_ref, own_out_ref, other_out_ref, ordered, grad_t_ref = refs
    part_rows = part_refs[0].shape[1]
    for call in range(calls):
        for kind in range(3):
            start = kind * part_rows * calls + call * part_rows
            grad_t_ref[:, start : start + part_rows] = part_refs[4 * call + kind][...]
    pair_refs = part_refs[3::4]
    per_pair = pair_refs[0].shape[1] // 128
    me = place_ref[2]
    mols, width, slots = normed_t_ref.shape
    half = slots // 2
    rows = width // pieces
    block = 256
    for start in range(0, width, block):
        total = sum(mxu(normed_t_ref[m, start : start + block], grad_t_ref[m], NT) for m in range(mols))
        for piece in range(block // rows):
            ordered[start // rows + piece, :, 0 : total.shape[1]] = total[piece * rows : (piece + 1) * rows]
    weight = weight_ref[...].astype(bf16)
    gain_grad, offset_grad = 0.0, 0.0
    for m in range(mols):
        normed_grad = mxu(weight, grad_t_ref[m]).T
        unit, inverse = norm_parts(jnp.concatenate([own_ref[place_ref[1] * mols + m], other_ref[m]], axis=0).astype(f32))
        gain_grad += jnp.sum(normed_grad * unit, axis=0, keepdims=True)
        offset_grad += jnp.sum(normed_grad, axis=0, keepdims=True)
        result = middle_grad_ref[m * slots : (m + 1) * slots] + norm_back(normed_grad, unit, inverse, norm_ref[0:1])
        own_out_ref[m] = result[:half]
        other_out_ref[m] = result[half:].astype(bf16)
    columns = weight_ref.shape[1]
    kinds = pair_refs[0].shape[0]
    for chunk in range(width // kinds):
        at = chunk % per_pair * 128
        ordered[:, chunk, columns : columns + 128] = pair_refs[chunk // per_pair][:, at : at + 128]
    vectors = jnp.concatenate([gain_grad, offset_grad, tiny_ref[...], jnp.zeros((128 - 8, width), f32)], axis=0)
    ordered[:, :, columns + 128 : columns + 256] = vectors.T.reshape(kinds, width // kinds, 128)
    core = place_ref[0]
    count = pieces // 2
    for piece in range(count):
        at = jnp.bitwise_xor(piece, me)
        keep_ref[at] = ordered[core * count + piece].astype(bf16)
        send_ref[at] = ordered[(1 - core) * count + piece].astype(bf16)


def project_back(place, parts, normed_t, weight, own, other, middle_grad, norms, tiny, after, pieces):
    mols, width, slots = normed_t.shape
    columns = weight.shape[1]
    shape = jax.ShapeDtypeStruct
    vmem = pl.BlockSpec(memory_space=pltpu.VMEM)
    return pl.pallas_call(
        functools.partial(project_kernel, pieces, len(parts)),
        in_specs=[pl.BlockSpec(memory_space=pltpu.SMEM)] + [vmem] * 7 + [pl.BlockSpec(memory_space=pl.ANY)] + [vmem] * 4 * len(parts),
        out_specs=[vmem] * 4,
        out_shape=[shape((pieces // 2, width // pieces, columns + 256), bf16), shape((pieces // 2, width // pieces, columns + 256), bf16),
                   shape((mols, slots // 2, width), f32),
                   shape((mols, slots // 2, width), bf16)],
        scratch_shapes=[pltpu.VMEM((pieces, width // pieces, columns + 256), f32), pltpu.VMEM((mols, columns, slots), bf16)],
        compiler_params=pltpu.CompilerParams(vmem_limit_bytes=vmem_bytes),
        cost_estimate=pl.CostEstimate(flops=4 * 10**9, bytes_accessed=10 * 10**6, transcendentals=0),
        name="project_back",
    )(place, normed_t, weight, own, other, middle_grad, norms, tiny, after, *[array for part in parts for array in part])


def swap(array, axis, bit, size):
    return lax.ppermute(array, axis, [(i, i ^ (1 << bit)) for i in range(size)])


def add_low(left, right):
    return (left.astype(f32) + right.astype(f32)).astype(bf16)


def tied(array, after):
    return array if after is None else lax.optimization_barrier((array, after))[0]


def halve(array, axes, digit, sizes, after=None):
    index = axes.index(digit)
    keep = lax.index_in_dim(array, 0, index, keepdims=False)
    send = lax.index_in_dim(array, 1, index, keepdims=False)
    return add_low(tied(keep, after), swap(send, *digit, sizes[digit[0]])), axes[:index] + axes[index + 1 :]


def jump(array, digits, sizes):
    axis = digits[0][0]
    mask = sum(1 << bit for _, bit in digits)
    return lax.ppermute(array, axis, [(i, i ^ mask) for i in range(sizes[axis])])


def quarter(array, axes, pair, sizes, after=None):
    first, second = axes.index(pair[0]), axes.index(pair[1])
    array = jnp.moveaxis(array, (first, second), (0, 1))
    total = tied(array[0, 0], after).astype(f32)
    for place, digits in (((1, 0), pair[:1]), ((0, 1), pair[1:]), ((1, 1), pair)):
        total = total + jump(array[place], digits, sizes).astype(f32)
    return total.astype(bf16), [digit for digit in axes if digit not in pair]


def double(array, digit, sizes, after=None):
    return jnp.stack([tied(array, after), swap(array, *digit, sizes[digit[0]])])


def quadruple(array, pair, sizes, after=None):
    pieces = [tied(array, after)] + [jump(array, digits, sizes) for digits in (pair[1:], pair[:1], pair)]
    return jnp.stack(pieces).reshape((2, 2) + array.shape)


def split_middle(digits):
    middle = digits[1:-1]
    return middle[: len(middle) % 2], [middle[i : i + 2] for i in range(len(middle) % 2, len(middle), 2)]


def scatter_first(array, digits, sizes, after=None):
    cut = array.shape[-1] // 2
    left, _ = halve(array[..., :cut], digits, digits[0], sizes, after)
    right, _ = halve(array[..., cut:], digits, digits[-1], sizes, after)
    return left, right


def scatter_second(parts, digits, sizes, after=None):
    left, _ = halve(parts[0], digits[1:], digits[-1], sizes, after)
    right, _ = halve(parts[1], digits[:-1], digits[0], sizes, after)
    return jnp.concatenate([left, right], axis=-1)


def scatter_middle(both, digits, sizes, after=None):
    single, pairs = split_middle(digits)
    axes = digits[1:-1]
    for pair in pairs[::-1]:
        both, axes = quarter(both, axes, pair, sizes, after)
    for digit in single:
        both, axes = halve(both, axes, digit, sizes)
    return both


def gather_middle(both, digits, sizes, after=None):
    single, pairs = split_middle(digits)
    for digit in single:
        both = double(both, digit, sizes)
    for pair in pairs:
        both = quadruple(both, pair, sizes, after)
    return both


def gather_second(both, digits, sizes, after=None):
    cut = both.shape[-1] // 2
    return double(both[..., :cut], digits[-1], sizes, after), double(both[..., cut:], digits[0], sizes, after)


def gather_first(parts, digits, sizes, after=None):
    left = double(parts[0], digits[0], sizes, after)
    right = double(parts[1], digits[-1], sizes, after)
    return left, jnp.swapaxes(right, 0, 1)


def beside(parts):
    return jnp.concatenate(parts, axis=-1)


def gather_order(digits):
    single, pairs = split_middle(digits)
    return [digits[0], digits[-1]] + [digit for pair in pairs[::-1] for digit in pair] + single


def place_list(order, digits):
    result = []
    for number in range(2 ** len(order)):
        bits = {digit: (number >> (len(order) - 1 - i)) & 1 for i, digit in enumerate(order)}
        result.append(sum(bits[digit] << (len(digits) - 1 - i) for i, digit in enumerate(digits)))
    return result


def absolute(array, digits, places):
    for index, (axis, bit) in enumerate(digits):
        flag = (places[axis] >> bit) & 1
        array = jnp.where(flag == 1, jnp.flip(array, index), array)
    return array


def muon_load(high_ref, low_ref, source_ref, scale, tall):
    block = 256
    for start in range(0, source_ref.shape[0], block):
        at = slice(start, start + block)
        high_ref[at], low_ref[at] = two_parts(source_ref[at] * scale)


def symmetric_product(left, right):
    half = left.shape[0] // 2
    left_high, left_low = two_parts(left)
    right_high, right_low = two_parts(right)
    rows = jnp.concatenate([left_high, left_low, left_high], axis=1)
    columns = jnp.concatenate([right_high, right_high, right_low], axis=0)
    top = mxu(rows[:half], columns)
    corner = mxu(rows[half:], columns[:, half:])
    return jnp.concatenate([top, jnp.concatenate([top[:, half:].T, corner], axis=1)], axis=0)


def muon_product(tall, steps, high_ref, low_ref, gram_ref, poly_ref, product_ref):
    size = gram_ref.shape[0]
    row = lax.broadcasted_iota(jnp.int32, (size, size), 0)
    column = lax.broadcasted_iota(jnp.int32, (size, size), 1)

    def polynomial():
        gram = gram_ref[...]
        poly_ref[...] = coef_second * gram + coef_third * symmetric_product(gram, gram)

    def inner(index, carry):
        poly = poly_ref[...]
        gram = gram_ref[...]
        step = coef_first * gram + symmetric_product(poly, gram)
        gram_ref[...] = coef_first * step + symmetric_product(poly, step)
        polynomial()
        product = product_ref[...]
        product_ref[...] = coef_first * product + symmetric_product(poly_ref[...], product)
        return carry

    if tall:
        both = mxu(high_ref[...], jnp.concatenate([high_ref[...], low_ref[...]], axis=1), TN)
    else:
        both = mxu(high_ref[...], jnp.concatenate([high_ref[...], low_ref[...]], axis=0), NT)
    crossing = both[:, size:]
    gram_ref[...] = both[:, :size] + crossing + crossing.T
    polynomial()
    product_ref[...] = poly_ref[...] + jnp.where(row == column, coef_first, 0.0)
    if not isinstance(steps, int) or steps > 1:
        lax.fori_loop(0, steps - 1, inner, 0)


def muon_blocks(tall, high_ref, low_ref, product_ref, length):
    high, low = two_parts(product_ref[...])
    block = 256
    if tall:
        right = jnp.concatenate([high, high, low], axis=0)
    else:
        left = jnp.concatenate([high, high, low], axis=1)
    for start in range(0, length, block):
        at = slice(start, start + block)
        if tall:
            left = jnp.concatenate([high_ref[at], low_ref[at], high_ref[at]], axis=1)
        else:
            right = jnp.concatenate([high_ref[:, at], low_ref[:, at], high_ref[:, at]], axis=0)
        yield at, mxu(left, right)


def inverse_norm(values):
    return 1.0 / (jnp.sqrt(jnp.full((1, 1), values, f32)) + 1e-07)


def muon_scratch(shape, size):
    return [pltpu.VMEM(shape, bf16), pltpu.VMEM(shape, bf16)] + [pltpu.VMEM((size, size), f32)] * 3


def copies_of(pairs, semaphores):
    copies = [pltpu.make_async_copy(source, target, semaphores.at[index]) for index, (source, target) in enumerate(pairs)]
    for copy in copies:
        copy.start()
    return copies


def muon_feed_kernel(
    numbers, place_ref, sum_ref, own_state_ref, other_state_ref, direction_ref,
    sums, own_state, other_state, direction, moment, high, low, gram, poly, product, semaphores, out_semaphores,
):
    me = place_ref[4]
    held, width = own_state.shape
    count = len(numbers) // 2
    rows = held // count
    incoming = copies_of(
        [(sum_ref.at[0:count], sums.at[0:count]), (own_state_ref, own_state),
         (sum_ref.at[count : 2 * count], sums.at[count : 2 * count]), (other_state_ref, other_state)],
        semaphores,
    )
    total = jnp.zeros((1, width), f32)
    for index, number in enumerate(numbers):
        if index % count == 0:
            incoming[2 * (index // count)].wait()
            incoming[2 * (index // count) + 1].wait()
        state_ref = own_state if index < count else other_state
        start = pl.multiple_of(jnp.bitwise_xor(number % count, me) * rows, rows)
        state = state_ref[pl.ds(start, rows), :].astype(f32)
        value = momentum_keep * state + sums[index, 0:rows].astype(f32)
        moment[pl.ds(start + (0 if index < count else held), rows), :] = value
        total += jnp.sum(value * value, axis=0, keepdims=True)
    muon_load(high, low, moment, inverse_norm(jnp.sum(total)), True)
    muon_product(True, 3, high, low, gram, poly, product)
    for at, value in muon_blocks(True, high, low, product, 2 * held):
        high[at], low[at] = two_parts(value)
    muon_product(True, 2, high, low, gram, poly, product)
    outgoing = []
    for at, value in muon_blocks(True, high, low, product, held):
        direction[at] = value.astype(bf16)
        outgoing += copies_of([(direction.at[at], direction_ref.at[at])], out_semaphores.at[pl.ds(len(outgoing), 1)])
    for copy in outgoing:
        copy.wait()


def muon_feed(place, sums, own_state, other_state, numbers):
    held, width = own_state.shape
    any_memory = pl.BlockSpec(memory_space=pl.ANY)
    return pl.pallas_call(
        functools.partial(muon_feed_kernel, numbers),
        in_specs=[pl.BlockSpec(memory_space=pltpu.SMEM)] + [any_memory] * 3,
        out_specs=any_memory,
        out_shape=jax.ShapeDtypeStruct((held, width), bf16),
        scratch_shapes=[pltpu.VMEM(sums.shape, bf16), pltpu.VMEM((held, width), f32), pltpu.VMEM((held, width), bf16),
                        pltpu.VMEM((held, width), bf16), pltpu.VMEM((2 * held, width), f32)]
                       + muon_scratch((2 * held, width), width)
                       + [pltpu.SemaphoreType.DMA((4,)), pltpu.SemaphoreType.DMA((held // 256,))],
        compiler_params=pltpu.CompilerParams(vmem_limit_bytes=vmem_bytes),
        cost_estimate=pl.CostEstimate(flops=26 * 10**9, bytes_accessed=8 * 10**6, transcendentals=0),
        name="muon_feed",
    )(place, sums, own_state, other_state)


def muon_whole_kernel(
    numbers, plan, rate, me_ref, sum_ref, swapped_ref, state_ref, weight_ref, moment_ref, updated_ref,
    sums, swapped, state, weight, high, low, gram, poly, product, semaphores, out_semaphores,
):
    me = me_ref[0]
    rows = sums.shape[1]
    columns = state.shape[1]
    incoming = copies_of([(state_ref, state), (sum_ref, sums), (swapped_ref, swapped), (weight_ref, weight)], semaphores)
    for copy in incoming[:3]:
        copy.wait()
    total = jnp.zeros((1, columns), f32)
    for core_place, ref in enumerate((sums, swapped)):
        for index, number in enumerate(numbers):
            number += core_place * len(numbers)
            start = pl.multiple_of(jnp.bitwise_xor(number, me) * rows, rows)
            value = momentum_keep * state[pl.ds(start, rows), :] + ref[index, :, 0:columns].astype(f32)
            state[pl.ds(start, rows), :] = value
            total += jnp.sum(value * value, axis=0, keepdims=True)
    moment_out = copies_of([(state, moment_ref)], out_semaphores.at[pl.ds(0, 1)])
    muon_load(high, low, state, inverse_norm(jnp.sum(total)), False)

    def outer(index, carry):
        muon_product(False, plan[0] if len(set(plan)) == 1 else plan[0] - index, high, low, gram, poly, product)
        for at, value in muon_blocks(False, high, low, product, columns):
            high[:, at], low[:, at] = two_parts(value)
        return carry

    lax.fori_loop(0, len(plan), outer, 0)
    incoming[3].wait()
    outgoing = moment_out
    for start in range(0, weight.shape[0], 64):
        at = slice(start, start + 64)
        weight[at] = weight[at] - rate * (high[at].astype(f32) + low[at].astype(f32))
        outgoing = outgoing + copies_of([(weight.at[at], updated_ref.at[at])], out_semaphores.at[pl.ds(len(outgoing), 1)])
    for copy in outgoing:
        copy.wait()


def muon_whole(me, sums, swapped, state, weight, numbers, plan, rate):
    any_memory = pl.BlockSpec(memory_space=pl.ANY)
    shape = jax.ShapeDtypeStruct(state.shape, f32)
    return pl.pallas_call(
        functools.partial(muon_whole_kernel, numbers, plan, rate),
        in_specs=[pl.BlockSpec(memory_space=pltpu.SMEM)] + [any_memory] * 4,
        out_specs=[any_memory] * 2,
        out_shape=[shape, shape],
        scratch_shapes=[pltpu.VMEM(sums.shape, bf16), pltpu.VMEM(sums.shape, bf16), pltpu.VMEM(state.shape, f32),
                        pltpu.VMEM(state.shape, f32)]
                       + muon_scratch(state.shape, state.shape[0])
                       + [pltpu.SemaphoreType.DMA((4,)), pltpu.SemaphoreType.DMA((1 + state.shape[0] // 64,))],
        compiler_params=pltpu.CompilerParams(vmem_limit_bytes=vmem_bytes),
        cost_estimate=pl.CostEstimate(flops=state.size * 25000, bytes_accessed=16 * 10**6, transcendentals=0),
        name="muon_whole",
    )(me, sums, swapped, state, weight)


def feed_moments_kernel(numbers, place_ref, own_ref, swapped_ref, up_state_ref, down_state_ref, up_ref, down_ref, up_sum):
    me = place_ref[4]
    core = place_ref[0]
    count, rows, _ = own_ref.shape

    def write(up_from, down_from):
        for index, number in enumerate(numbers):
            start = pl.multiple_of(jnp.bitwise_xor(number, me) * rows, rows)
            at = pl.ds(start, rows)
            up_sum[at, :] = up_from[index].astype(f32)
            down_ref[at, :] = momentum_keep * down_state_ref[at, :] + down_from[index].astype(f32)

    @pl.when(core == 0)
    def _():
        write(own_ref, swapped_ref)

    @pl.when(core == 1)
    def _():
        write(swapped_ref, own_ref)

    for start in range(0, up_sum.shape[0], 256):
        at = slice(start, start + 256)
        up_ref[:, at] = momentum_keep * up_state_ref[:, at] + up_sum[at].T


def feed_moments(place, own, swapped, up_state, down_state, numbers):
    vmem = pl.BlockSpec(memory_space=pltpu.VMEM)
    return pl.pallas_call(
        functools.partial(feed_moments_kernel, numbers),
        in_specs=[pl.BlockSpec(memory_space=pltpu.SMEM)] + [vmem] * 4,
        out_specs=[vmem] * 2,
        out_shape=[jax.ShapeDtypeStruct(up_state.shape, f32), jax.ShapeDtypeStruct(down_state.shape, f32)],
        scratch_shapes=[pltpu.VMEM(down_state.shape, f32)],
        compiler_params=pltpu.CompilerParams(vmem_limit_bytes=vmem_bytes),
        cost_estimate=pl.CostEstimate(flops=10**6, bytes_accessed=10 * 10**6, transcendentals=0),
        name="feed_moments",
    )(place, own, swapped, up_state, down_state)


def feed_update_kernel(rate_first, rate_second, place_ref, own_ref, swapped_ref, up_weight_ref, down_weight_ref, up_ref, down_ref):
    core = place_ref[0]

    def write(up_from, down_from):
        down_ref[...] = down_weight_ref[...] - rate_second * down_from[...].astype(f32)
        for start in range(0, up_from.shape[0], 256):
            at = slice(start, start + 256)
            up_ref[:, at] = up_weight_ref[:, at] - rate_first * up_from[at].astype(f32).T

    @pl.when(core == 0)
    def _():
        write(own_ref, swapped_ref)

    @pl.when(core == 1)
    def _():
        write(swapped_ref, own_ref)


def feed_update(place, own, swapped, up_weight, down_weight, rate_first, rate_second):
    vmem = pl.BlockSpec(memory_space=pltpu.VMEM)
    return pl.pallas_call(
        functools.partial(feed_update_kernel, rate_first, rate_second),
        in_specs=[pl.BlockSpec(memory_space=pltpu.SMEM)] + [vmem] * 4,
        out_specs=[vmem] * 2,
        out_shape=[jax.ShapeDtypeStruct(up_weight.shape, f32), jax.ShapeDtypeStruct(down_weight.shape, f32)],
        compiler_params=pltpu.CompilerParams(vmem_limit_bytes=vmem_bytes),
        cost_estimate=pl.CostEstimate(flops=10**6, bytes_accessed=10 * 10**6, transcendentals=0),
        name="feed_update",
    )(place, own, swapped, up_weight, down_weight)


def step_factor(rows, columns):
    return math.sqrt(max(1.0, rows / columns))


def on_device(
    dp_size, mp_size,
    atoms, atom_counts, hydrogen, atom_types, cotangent, qkv_weight, out_weight, up_weight, down_weight, ffn_bias, norm_params,
    pair_table, qkv_state, out_state, up_state, down_state, bias_state, norm_state, pair_state,
):
    sizes = {"dp": dp_size, "mp": mp_size}
    place_dp, place_mp = lax.axis_index("dp"), lax.axis_index("mp")
    places = {"dp": place_dp, "mp": place_mp}
    core = place_dp & 1
    dp_bits = dp_size.bit_length() - 1
    mols, half, width = atoms.shape
    mine = mols // 2
    slots = 2 * half
    types_count, _, head_count = pair_table.shape
    kinds = 32

    def other_slots(array):
        return swap(lax.dynamic_slice_in_dim(array, (1 - place_mp) * mine, mine, 0), "mp", 0, mp_size)

    atoms_other = other_slots(atoms)
    up_own = up_weight.T.astype(bf16)
    down_own = down_weight.astype(bf16)
    cot_other = other_slots(cotangent)
    bias_other = swap(ffn_bias, "mp", 0, mp_size)
    leaving, cot_other, bias_other = lax.optimization_barrier((jnp.where(core == 0, up_own, down_own), cot_other, bias_other))
    crossed = swap(leaving, "mp", 0, mp_size)
    bias_rel = jnp.concatenate([ffn_bias, bias_other])[None]

    table = jnp.pad(lax.reduce_precision(pair_table, 8, 7) * log2_e, ((0, kinds - types_count), (0, kinds - types_count), (0, 0)))
    table = table.transpose(2, 1, 0)
    table_high = lax.reduce_precision(table, 8, 7)
    table_rows = jnp.concatenate([table_high, table - table_high], axis=1).astype(bf16).reshape(head_count * 2 * kinds, kinds)
    scalars = jnp.concatenate([jnp.stack([core, place_mp]).astype(jnp.int32), atom_counts])
    (probs, read_t, query_t, key_t, values, normed_t, attended_t, middle, normed_two, own_state, leaving_state, type_t, valid) = attend(
        scalars, atoms, atoms_other, qkv_weight, norm_params, table_rows, atom_types, hydrogen, out_weight, up_state, down_state
    )
    crossed, normed_two = lax.optimization_barrier((crossed, normed_two))
    crossed_again = swap(crossed, "dp", 0, dp_size)
    other_state = swap(leaving_state, "mp", 0, mp_size)

    core_digit = ("dp", 0)
    half_digits = [("dp", bit) for bit in range(dp_bits - 1, 0, -1)]
    half_pieces = dp_size // 2
    chip_digits = [("mp", 0)] + half_digits
    some_digits = chip_digits[-4:]
    plain_digits = chip_digits[:-4]
    pieces = 2 ** (1 + len(some_digits))
    half_place = place_dp >> 1
    some_place = (place_mp * half_pieces + half_place) & (pieces // 2 - 1)
    piece_rows = up_own.shape[0] // half_pieces
    out_rows = width // (4 * half_pieces)
    aligned = out_rows % 16 == 0
    place = jnp.stack(
        [core, place_mp, some_place, core * (pieces // 2) + some_place, half_place, place_mp * half_pieces + half_place]
    ).astype(jnp.int32)

    rows = mine * slots
    (keep, send, bias_grad, mixed, middle_grad, attended_grad_t, out_grad, norm_grad_two) = feed(
        place, normed_two.reshape(rows, width), middle.reshape(rows, width), cotangent, cot_other, valid.reshape(rows, 1), attended_t,
        norm_params, out_weight, up_own, down_own, crossed, crossed_again, bias_rel, half_pieces, out_rows if aligned else 0,
    )

    digit_shape = (2,) * len(chip_digits)
    if not aligned:
        out_grad = out_grad.astype(bf16).reshape((2,) + digit_shape + (out_rows, width))
        out_grad = absolute(out_grad, [core_digit] + chip_digits, places).reshape((2, 2, half_pieces, out_rows, width))
        keep, send = jnp.concatenate([keep, out_grad[0]], axis=-2), jnp.concatenate([send, out_grad[1]], axis=-2)
    early = add_low(keep, swap(send, "dp", 0, dp_size)).reshape(digit_shape + (piece_rows + out_rows, width))
    early_ends = scatter_first(early, chip_digits, sizes)
    early_both = scatter_second(early_ends, chip_digits, sizes)

    def corner(*arrays):
        return jnp.stack([array[(0,) * (array.ndim - 2)][:16, :128] for array in arrays])

    groups = values.shape[1]
    calls = 4
    mixed = mixed.reshape(mine, slots, width)
    mixed_moved = swap(mixed[:, half:], "mp", 0, mp_size)
    waits = [place, corner(early), corner(early, other_state, mixed_moved), corner(*early_ends), corner(early_both)]
    parts = [
        attend_back(i * groups // calls, groups // calls, probs, attended_grad_t, read_t, values, key_t, query_t, type_t, waits[i])
        for i in range(calls)
    ]
    bias_grad = bias_grad.reshape(2, -1)
    bias_grad = jnp.where(place_mp == 0, bias_grad, bias_grad[::-1]).reshape(-1, width)
    tiny = jnp.concatenate([norm_grad_two, bias_grad], axis=0)
    late_keep, late_send, atoms_grad_own, atoms_grad_other = project_back(
        place, parts, normed_t, qkv_weight, atoms, atoms_other, middle_grad, norm_params, tiny, waits[4], pieces
    )

    def own_last(array):
        return swap(array, "dp", 0, dp_size)

    def back_slots(own, moved):
        moved = moved.astype(own.dtype)
        return jnp.where(place_mp == 0, jnp.concatenate([own, moved], 0), jnp.concatenate([moved, own], 0))

    atoms_moved = swap(atoms_grad_other, "mp", 0, mp_size)
    early_order, late_order = gather_order(chip_digits), gather_order(some_digits)
    late = add_low(late_keep, own_last(late_send))
    late_shape = late.shape
    late = late.reshape((2,) * len(some_digits) + late_shape[1:])
    early_both = scatter_middle(early_both, chip_digits, sizes, late)
    late_ends = scatter_first(late, some_digits, sizes)
    early_middle = gather_middle(early_both, chip_digits, sizes, late_ends)
    out_own = double(early_middle[..., piece_rows:, :], chip_digits[-1], sizes)
    late_both = scatter_second(late_ends, some_digits, sizes, out_own)
    early_half = gather_second(early_middle[..., :piece_rows, :], chip_digits, sizes, (late_both, atoms_moved))
    out_own = double(out_own, chip_digits[0], sizes, early_half).reshape((2 * half_pieces, out_rows, width))
    late_both = scatter_middle(late_both, some_digits, sizes, out_own)
    for axis, bit in plain_digits:
        late_both = add_low(late_both, swap(late_both, axis, bit, sizes[axis]))
    out_swapped = tied(own_last(out_own), late_both)
    out_numbers, out_me = place_list(early_order, chip_digits), core * 2 * half_pieces + place[5]
    if not aligned:
        out_sum = jnp.stack([out_own, out_swapped]).reshape((2,) + digit_shape + (out_rows, width))
        out_sum = absolute(out_sum, [core_digit] + early_order, places)
        spots = [0] + [1 + early_order.index(digit) for digit in chip_digits]
        out_sum = out_sum.transpose(spots + [len(spots), len(spots) + 1]).reshape(2, -1, 16, width)
        out_own, out_swapped = out_sum
        out_numbers, out_me = list(range(out_own.shape[0])), out_me * 0
    out_moment, out_updated = muon_whole(
        out_me[None].astype(jnp.int32), out_own, out_swapped, out_state, out_weight, out_numbers, (1, 1, 1, 1, 1),
        rate_out * step_factor(*out_weight.shape),
    )
    late_middle = gather_middle(late_both, some_digits, sizes, out_updated)
    mixed_out = back_slots(mixed[:, :half], mixed_moved)
    atoms_grad = back_slots(atoms_grad_own, atoms_moved)
    early_sum = beside(gather_first(early_half, chip_digits, sizes, (late_middle, mixed_out, atoms_grad)))
    early_sum = early_sum.reshape((2 * half_pieces, piece_rows, width))
    direction = muon_feed(place, early_sum, own_state, other_state, place_list(early_order, chip_digits))
    own_sum = early_sum[:half_pieces]
    own_numbers = place_list(early_order[1:], half_digits)
    late_half = gather_second(late_middle, some_digits, sizes, direction)
    up_moment, down_moment = feed_moments(place, tied(own_sum, late_half), own_last(own_sum), up_state, down_state, own_numbers)
    late_sum = beside(gather_first(late_half, some_digits, sizes, up_moment)).reshape(late_shape)
    hidden_units = mp_size * up_weight.shape[1]
    up_updated, down_updated = feed_update(
        place, tied(direction, late_sum), own_last(direction), up_weight, down_weight,
        rate_up * step_factor(width, hidden_units), rate_down * step_factor(hidden_units, width),
    )
    late_swapped = own_last(late_sum)
    late_sum = tied(late_sum, up_updated)
    qkv_moment, qkv_updated = muon_whole(
        place[3:4], late_sum, late_swapped, qkv_state, qkv_weight, place_list(late_order, some_digits), (3, 2),
        rate_qkv * step_factor(*qkv_weight.shape),
    )

    order = late_order
    small = jnp.stack([late_sum[..., 3 * width :], late_swapped[..., 3 * width :]])
    small = absolute(small.reshape((2,) * (1 + len(order)) + small.shape[2:]), [core_digit] + order, places)
    spots = (0,) + tuple(1 + order.index(digit) for digit in some_digits)
    small = small.transpose(spots + (len(spots), len(spots) + 1)).reshape(kinds, width // kinds, 256).astype(f32)
    pair_sum = small[..., :128].reshape(kinds, head_count, kinds).transpose(0, 2, 1)[:types_count, :types_count]
    pair_sum = lax.optimization_barrier(pair_sum)
    vectors = small[..., 128:136].reshape(width, 8).T
    norm_sum = vectors[:4]
    bias_sum = lax.dynamic_slice_in_dim(vectors[4:].reshape(-1), place_mp * ffn_bias.shape[0], ffn_bias.shape[0], 0)

    norm_moment = momentum_keep * norm_state + norm_sum
    norm_updated = norm_params - rate_norm * norm_moment
    bias_moment = momentum_keep * bias_state + bias_sum
    bias_updated = ffn_bias - rate_bias * bias_moment
    pair_moment = momentum_keep * pair_state + pair_sum
    pair_updated = pair_table - rate_pair * pair_moment

    return (
        mixed_out,
        atoms_grad,
        qkv_moment,
        qkv_updated,
        out_moment,
        out_updated,
        up_moment,
        up_updated,
        down_moment,
        down_updated,
        bias_moment,
        bias_updated,
        norm_moment,
        norm_updated,
        pair_moment,
        pair_updated,
    )


def solution(mesh):
    rows = P("dp", "mp", None)
    in_specs = (
        rows, P("dp"), P("dp", None), P("dp", None), rows, P(), P(), P(None, "mp"), P("mp", None), P("mp"), P(), P(),
        P(), P(), P(None, "mp"), P("mp", None), P("mp"), P(), P(),
    )
    out_specs = (
        rows, rows, P(), P(), P(), P(), P(None, "mp"), P(None, "mp"), P("mp", None), P("mp", None), P("mp"), P("mp"),
        P(), P(), P(), P(),
    )
    body = functools.partial(on_device, mesh.shape["dp"], mesh.shape["mp"])
    return jax.shard_map(body, mesh=mesh, in_specs=in_specs, out_specs=out_specs, check_vma=False)
```

```python
import functools
import math

import jax
import jax.numpy as jnp
from jax import lax
from jax.experimental import pallas as pl
from jax.experimental.pallas import tpu as pltpu
from jax.sharding import PartitionSpec as P

norm_eps = 1e-05
masked_score = -1000000000.0
coef_first = 3.4445
coef_second = -4.775
coef_third = 2.0315
momentum_keep = 0.5
rate_qkv = 1.0
rate_out = 4.0
rate_up = 1.0
rate_down = 1.0
rate_norm = 0.001
rate_bias = 0.01
rate_pair = 0.05

bf16 = jnp.bfloat16
f32 = jnp.float32
log2_e = 1.4426950408889634
NN = (((1,), (0,)), ((), ()))
NT = (((1,), (1,)), ((), ()))
TN = (((0,), (0,)), ((), ()))
vmem_bytes = 56 * 2**20


def mxu(left, right, dims=NN):
    return lax.dot_general(left, right, dims, preferred_element_type=f32)


def norm_parts(values):
    center = values - jnp.mean(values, axis=-1, keepdims=True)
    inverse = lax.rsqrt(jnp.mean(center * center, axis=-1, keepdims=True) + norm_eps)
    return center * inverse, inverse


def norm_back(grad_rows, unit_rows, inverse, gain_vec):
    scaled = grad_rows * gain_vec
    mean_one = jnp.mean(scaled, axis=-1, keepdims=True)
    mean_two = jnp.mean(scaled * unit_rows, axis=-1, keepdims=True)
    return inverse * (scaled - mean_one - unit_rows * mean_two)


def two_parts(values):
    high = values.astype(bf16)
    return high, (values - high.astype(f32)).astype(bf16)


def attend_kernel(
    groups, state_steps, scalar_ref, own_ref, other_ref, qkv_w_ref, norm_ref, table_ref, type_all_ref, hydrogen_ref, out_w_ref,
    up_state_ref, down_state_ref,
    prob_ref, read_t_ref, query_t_ref, key_t_ref, value_ref, normed_t_ref, attended_t_ref, middle_ref, normed_two_ref,
    own_state_ref, leaving_ref, type_t_ref, valid_ref,
    left_all, query_high, query_low, value_t, table_wide, table_rows, bias_all, cap, read_all, qkv_low,
):
    step_index = pl.program_id(1)
    steps = pl.num_programs(1)
    core, side = scalar_ref[0], scalar_ref[1]
    molecule = side * pl.num_programs(0) + pl.program_id(0)
    count = scalar_ref[2 + molecule]
    slots = prob_ref.shape[2]
    width = own_ref.shape[2]
    half = slots // 2
    span = width // groups
    at_once = groups // steps
    heads = prob_ref.shape[1] // at_once
    kinds = type_t_ref.shape[1]

    def slot_row(ref):
        row = ref[pl.ds(molecule, 1), :].astype(f32)
        turned = jnp.concatenate([row[:, half:], row[:, :half]], axis=1)
        second = side.astype(f32)
        return row * (1.0 - second) + turned * second

    def load_rows():
        return jnp.concatenate([own_ref[0], other_ref[0]], axis=0).astype(f32)

    @pl.when((step_index == 0) & (pl.program_id(0) == 0))
    def _():
        qkv_low[...] = qkv_w_ref[...].astype(bf16)
        types, _, all_heads = table_ref.shape
        table_wide[...] = jnp.zeros_like(table_wide)
        for other in range(types):
            entries = jnp.concatenate([table_ref[:, other, :], jnp.zeros((kinds - types, all_heads), f32)], axis=0)
            entries = (entries.astype(bf16).astype(f32) * log2_e).T
            rounded = entries.astype(bf16).astype(f32)
            table_wide[:, other, :] = rounded
            table_wide[:, kinds + other, :] = entries - rounded
        for head in range(0, all_heads, 8):
            rows = table_wide[head : head + 8].reshape(16 * kinds, kinds)
            table_rows[head * 2 * kinds : (head + 8) * 2 * kinds] = rows.astype(bf16)

    @pl.when(step_index == 0)
    def _():
        unit, _ = norm_parts(load_rows())
        normed = unit * norm_ref[0:1] + norm_ref[1:2]
        normed_t_ref[0] = normed.T.astype(bf16)
        normed = normed.astype(bf16)
        query = mxu(normed, qkv_low[:, 0:width]).T.astype(bf16)
        query_t_ref[0] = query
        keys = mxu(normed, qkv_low[:, width : 2 * width])
        key_t_ref[0] = keys.T.astype(bf16)
        keys = keys.astype(bf16)
        values = mxu(normed, qkv_low[:, 2 * width :])
        value_t[...] = values.T.astype(bf16)
        values = values.astype(bf16)
        head_width = span // heads
        scaled = query.astype(f32) * (head_width**-0.5 * log2_e)
        high = scaled.astype(bf16).astype(f32)
        query_high[...] = high
        query_low[...] = scaled - high
        slot = lax.broadcasted_iota(jnp.int32, (1, slots), 1) + side * half
        slot = jnp.where(slot >= slots, slot - slots, slot)
        present = jnp.where(slot < count, 1.0, 0.0)
        usable = jnp.where(slot_row(hydrogen_ref) == 0.0, present, 0.0)
        line = lax.broadcasted_iota(jnp.int32, (128, slots), 0)
        marks = jnp.where(line.astype(f32) == slot_row(type_all_ref), 1.0, 0.0)
        marks = jnp.where(line == kinds, usable, jnp.where(line == kinds + 1, present, marks))
        columns = marks.T
        type_rows = marks[0:kinds].astype(bf16)
        type_t_ref[0] = type_rows
        type_columns = columns[:, 0:kinds].astype(bf16)
        valid = columns[:, kinds + 1 : kinds + 2]
        valid_ref[0] = valid
        bias_all[...] = mxu(table_rows[...], type_rows).astype(bf16)
        blank = jnp.zeros((slots, 256 - 2 * span - 2 * kinds), bf16)
        for index in range(groups):
            part = keys[:, span * index : span * (index + 1)]
            left_all[index] = jnp.concatenate([part, part, type_columns, type_columns, blank], axis=1)
            value_ref[0, index] = values[:, span * index : span * (index + 1)]
        row = lax.broadcasted_iota(jnp.int32, (slots, slots), 0)
        column = lax.broadcasted_iota(jnp.int32, (slots, slots), 1)
        cap[...] = jnp.where((columns[:, kinds : kinds + 1] > 0.0) | (row == column), 3e38, masked_score * log2_e)

    early = pl.program_id(0) * steps + step_index < state_steps

    def keep_state(state):
        own_state_ref[...] = state
        leaving_ref[...] = state.astype(bf16)

    @pl.when(early & (core == 0))
    def _():
        keep_state(up_state_ref[...].T)

    @pl.when(early & (core == 1))
    def _():
        keep_state(down_state_ref[...])

    for part in range(at_once):
        group = step_index * at_once + part
        left = left_all[group]
        owner = lax.broadcasted_iota(jnp.int32, (span, slots), 0) // (span // heads)
        start = pl.multiple_of(group * span, span)
        high = query_high[pl.ds(start, span), :]
        low = query_low[pl.ds(start, span), :]
        zero = jnp.zeros_like(high)
        blank = jnp.zeros((256 - 2 * span - 2 * kinds, slots), bf16)

        def scores(head):
            mine = owner == head
            place = pl.multiple_of((group * heads + head) * 2 * kinds, 2 * kinds)
            bias = bias_all[pl.ds(place, 2 * kinds), :]
            parts = [jnp.where(mine, high, zero).astype(bf16), jnp.where(mine, low, zero).astype(bf16), bias, blank]
            return mxu(left, jnp.concatenate(parts, axis=0))

        def softmax(head, logits):
            logits = jnp.minimum(logits, cap[...])
            raised = jnp.exp2(logits - jnp.max(logits, axis=0, keepdims=True))
            low_probs = (raised * (1.0 / jnp.sum(raised, axis=0, keepdims=True))).astype(bf16)
            prob_ref[0, heads * part + head] = low_probs
            return low_probs

        def weigh(head, low_probs):
            pair = value_t[pl.ds(pl.multiple_of(group * span + (head // 2) * 16, 16), 16), :]
            both = mxu(pair, low_probs)
            return both[0:8] if head % 2 == 0 else both[8:16]

        ahead = heads
        waiting = [scores(head) for head in range(ahead)]
        probs, results = [], []
        for head in range(heads):
            probs.append(softmax(head, waiting[head]))
            if head + ahead < heads:
                waiting.append(scores(head + ahead))
            if head:
                results.append(weigh(head - 1, probs[head - 1]))
        results.append(weigh(heads - 1, probs[heads - 1]))
        read = jnp.concatenate(results, axis=0)
        read_t_ref[0, span * part : span * (part + 1)] = read
        read_all[pl.ds(start, span), :] = read.astype(bf16)

    @pl.when(step_index == steps - 1)
    def _():
        attended = read_all[...]
        attended_t_ref[0] = attended
        middle = load_rows() + valid_ref[0] * mxu(attended, out_w_ref[...].astype(bf16), TN)
        middle_ref[0] = middle
        unit, _ = norm_parts(middle)
        normed_two_ref[0] = (unit * norm_ref[2:3] + norm_ref[3:4]).astype(bf16)


def attend(scalars, atoms, other, qkv_w, norms, table, types, hydrogen, out_w, up_state, down_state):
    mols, half, width = other.shape
    slots = 2 * half
    groups = 8
    heads = width // 8 // groups
    kinds = 32
    span = width // groups
    whole = lambda a: pl.BlockSpec(a.shape, lambda m, g, s: (0,) * a.ndim)
    each = lambda *shape: pl.BlockSpec((1,) + shape, lambda m, g, s: (m,) + (0,) * len(shape))
    at_once = 2
    steps = groups // at_once
    state_steps = mols * steps // 2
    state_rows = down_state.shape[0] // state_steps
    state_at = lambda m, g: jnp.minimum(m * steps + g, state_steps - 1)
    state_block = pl.BlockSpec((state_rows, width), lambda m, g, s: (state_at(m, g), 0))
    shape = jax.ShapeDtypeStruct
    rows = shape((mols, width, slots), bf16)
    return pl.pallas_call(
        functools.partial(attend_kernel, groups, state_steps),
        grid_spec=pltpu.PrefetchScalarGridSpec(
            num_scalar_prefetch=1,
            grid=(mols, steps),
            in_specs=[pl.BlockSpec((1, half, width), lambda m, g, s: (s[1] * mols + m, 0, 0)), each(half, width), whole(qkv_w),
                      whole(norms), whole(table), whole(types), whole(hydrogen), whole(out_w),
                      pl.BlockSpec((width, state_rows), lambda m, g, s: (0, state_at(m, g))), state_block],
            out_specs=[pl.BlockSpec((1, heads * at_once, slots, slots), lambda m, g, s: (m, g, 0, 0)),
                       pl.BlockSpec((1, span * at_once, slots), lambda m, g, s: (m, g, 0)),
                       each(width, slots), each(width, slots), each(groups, slots, span), each(width, slots), each(width, slots),
                       each(slots, width), each(slots, width), state_block, state_block, each(kinds, slots), each(slots, 1)],
            scratch_shapes=[pltpu.VMEM((groups, slots, 256), bf16), pltpu.VMEM((width, slots), f32), pltpu.VMEM((width, slots), f32),
                            pltpu.VMEM((width, slots), bf16), pltpu.VMEM((groups * heads, 2 * kinds, kinds), f32),
                            pltpu.VMEM((groups * heads * 2 * kinds, kinds), bf16),
                            pltpu.VMEM((groups * heads * 2 * kinds, slots), bf16), pltpu.VMEM((slots, slots), f32),
                            pltpu.VMEM((width, slots), bf16), pltpu.VMEM(qkv_w.shape, bf16)],
        ),
        out_shape=[shape((mols, groups * heads, slots, slots), bf16), shape((mols, width, slots), f32), rows, rows,
                   shape((mols, groups, slots, span), bf16), rows, rows, shape((mols, slots, width), f32),
                   shape((mols, slots, width), bf16), shape(down_state.shape, f32), shape(down_state.shape, bf16),
                   shape((mols, kinds, slots), bf16), shape((mols, slots, 1), f32)],
        compiler_params=pltpu.CompilerParams(vmem_limit_bytes=vmem_bytes),
        cost_estimate=pl.CostEstimate(flops=22 * 10**9, bytes_accessed=24 * 10**6, transcendentals=8 * 10**6),
        name="attend",
    )(scalars, atoms, other, qkv_w, norms, table, types, hydrogen, out_w, up_state, down_state)


def feed_kernel(
    piece_rows, out_rows, block_count,
    place_ref, normed_ref, middle_ref, own_grad_ref, other_grad_ref, valid_ref, attended_t_ref, norm_ref, out_w_ref,
    up_own_ref, down_own_ref, first_ref, second_ref, bias_ref,
    keep_out, send_out, bias_grad_ref, mixed_ref, middle_grad_ref, attended_grad_t_ref, out_grad_ref, norm_grad_ref,
    rows_grad, sum_out, sum_back, up_used, down_used, out_low, keep_ref, send_ref, semaphores, *ordered,
):
    step = pl.program_id(0)
    steps = pl.num_programs(0)
    core = place_ref[0]
    me = place_ref[4]
    mols, half, width = other_grad_ref.shape
    rows = mols * 2 * half

    def given():
        return jnp.concatenate([part for m in range(mols) for part in (own_grad_ref[m], other_grad_ref[m])], axis=0)

    @pl.when(step == 0)
    def _():
        rows_grad[...] = (valid_ref[...] * given().astype(f32)).astype(bf16)
        out_low[...] = out_w_ref[...].astype(bf16)
        sum_out[...] = jnp.zeros_like(sum_out)
        sum_back[...] = jnp.zeros_like(sum_back)

    is_own = step < steps // 2

    def choose(condition, up_ref, down_ref):
        @pl.when(condition)
        def _():
            up_used[...] = up_ref[...]
            down_used[...] = down_ref[...]

    choose(is_own, up_own_ref, down_own_ref)
    choose(jnp.logical_not(is_own) & (core == 0), first_ref, second_ref)
    choose(jnp.logical_not(is_own) & (core == 1), second_ref, first_ref)
    up = up_used[...]
    down = down_used[...]
    normed = normed_ref[...]
    grads = rows_grad[...]
    chunks = [slice(start, start + rows // 2) for start in (0, rows // 2)]
    firsts = [(mxu(normed[chunk], up, NT) + bias_ref[...], mxu(grads[chunk], down, NT)) for chunk in chunks]
    actives, hidden_grads = [], []
    for chunk, (hidden, back) in zip(chunks, firsts):
        cumulative = 0.5 * (1.0 + lax.erf(hidden * 0.7071067811865476))
        active = (hidden * cumulative).astype(bf16)
        slope = cumulative + hidden * jnp.exp(-0.5 * hidden * hidden) * 0.3989422804014327
        back = (back * slope).astype(bf16)
        sum_out[chunk] += mxu(active, down)
        sum_back[chunk] += mxu(back, up)
        actives.append(active)
        hidden_grads.append(back)
    activated = jnp.concatenate(actives, axis=0)
    hidden_grad = jnp.concatenate(hidden_grads, axis=0)
    up_grad = mxu(hidden_grad, normed, TN).astype(bf16)
    down_grad = mxu(activated, grads, TN).astype(bf16)
    bias_grad_ref[...] = jnp.sum(hidden_grad.astype(f32), axis=0, keepdims=True)
    block_rows = up.shape[0]
    place_half = step // (steps // 2)
    first_piece = step % (steps // 2) * (up.shape[0] // piece_rows)

    def place_rows(kept, sent):
        for piece in range(up.shape[0] // piece_rows):
            at = jnp.bitwise_xor(first_piece + piece, me)
            keep_ref[place_half, at, 0:piece_rows] = kept[piece * piece_rows : (piece + 1) * piece_rows]
            send_ref[place_half, at, 0:piece_rows] = sent[piece * piece_rows : (piece + 1) * piece_rows]

    @pl.when(core == 0)
    def _():
        place_rows(up_grad, down_grad)

    @pl.when(core == 1)
    def _():
        place_rows(down_grad, up_grad)

    def leaving(spot, number):
        pairs = [(keep_ref.at[spot], keep_out.at[spot]), (send_ref.at[spot], send_out.at[spot])]
        return [pltpu.make_async_copy(source, target, semaphores.at[number, index]) for index, (source, target) in enumerate(pairs)]

    def step_pieces(number):
        first = number % (steps // 2) * (block_rows // piece_rows)
        spots = [(number // (steps // 2), jnp.bitwise_xor(first + piece, me), slice(0, piece_rows)) for piece in range(block_rows // piece_rows)]
        return [copy for index, spot in enumerate(spots) for copy in leaving(spot, number * (block_rows // piece_rows) + index)]

    for copy in step_pieces(step):
        copy.start()

    @pl.when(step == steps - 1)
    def _():
        middle = middle_ref[...]
        valid = valid_ref[...]
        mixed_ref[...] = (middle + valid * sum_out[...]).astype(bf16)
        unit, inverse = norm_parts(middle)
        grad_two = sum_back[...]
        norm_grad_ref[0:1] = jnp.sum(grad_two * unit, axis=0, keepdims=True)
        norm_grad_ref[1:2] = jnp.sum(grad_two, axis=0, keepdims=True)
        middle_grad = given().astype(f32) + norm_back(grad_two, unit, inverse, norm_ref[2:3])
        middle_grad_ref[...] = middle_grad
        branch_grad = (valid * middle_grad).astype(bf16)
        total = None
        for m in range(mols):
            part = branch_grad[m * 2 * half : (m + 1) * 2 * half]
            attended_grad_t_ref[m] = mxu(out_low[...], part, NT).astype(bf16)
            term = mxu(attended_t_ref[m], part)
            total = term if total is None else total + term
        out_grad_ref[...] = total
        if out_rows:
            half_pieces = keep_ref.shape[1]
            count = 2 * half_pieces
            for piece in range(2 * count):
                ordered[0][piece] = total[piece * out_rows : (piece + 1) * out_rows]
            for piece in range(count):
                at = jnp.bitwise_xor(piece, place_ref[5])
                spot = (at // half_pieces, at % half_pieces, slice(piece_rows, piece_rows + out_rows))
                keep_ref[spot] = ordered[0][core * count + piece].astype(bf16)
                send_ref[spot] = ordered[0][(1 - core) * count + piece].astype(bf16)
            rest = slice(piece_rows, piece_rows + out_rows)
            pairs = [(keep_ref.at[:, :, rest], keep_out.at[:, :, rest]), (send_ref.at[:, :, rest], send_out.at[:, :, rest])]
            tail = [pltpu.make_async_copy(source, target, ordered[1].at[index]) for index, (source, target) in enumerate(pairs)]
            for copy in tail:
                copy.start()
            for copy in tail:
                copy.wait()
        for number in range(block_count):
            for copy in step_pieces(number):
                copy.wait()


def feed(place, normed, middle, own_grad, other_grad, valid, attended_t, norms, out_w, up_own, down_own, first, second, bias,
         half_pieces, out_rows):
    mols, half, width = other_grad.shape
    rows = mols * 2 * half
    held = up_own.shape[0]
    block = 512
    per_half = held // block
    steps = 2 * per_half
    piece_rows = held // half_pieces
    whole = lambda a: pl.BlockSpec(a.shape, lambda j, s: (0,) * a.ndim)
    fixed = lambda *s: pl.BlockSpec(s, lambda j, s_: (0,) * len(s))
    mine = pl.BlockSpec((block, width), lambda j, s: (jnp.minimum(j, per_half - 1), 0))
    theirs = pl.BlockSpec((block, width), lambda j, s: (jnp.maximum(j - per_half, 0), 0))
    shape = jax.ShapeDtypeStruct
    return pl.pallas_call(
        functools.partial(feed_kernel, piece_rows, out_rows, steps),
        grid_spec=pltpu.PrefetchScalarGridSpec(
            num_scalar_prefetch=1,
            grid=(steps,),
            in_specs=[whole(normed), whole(middle), pl.BlockSpec((mols, half, width), lambda j, s: (s[1], 0, 0)), whole(other_grad), whole(valid), whole(attended_t),
                      whole(norms), whole(out_w), mine, mine, theirs, theirs, pl.BlockSpec((1, block), lambda j, s: (0, j))],
            out_specs=[pl.BlockSpec(memory_space=pl.ANY), pl.BlockSpec(memory_space=pl.ANY),
                       pl.BlockSpec((1, block), lambda j, s: (0, j)),
                       fixed(rows, width), fixed(rows, width), fixed(mols, width, 2 * half),
                       fixed(width, width), fixed(2, width)],
            scratch_shapes=[pltpu.VMEM((rows, width), bf16), pltpu.VMEM((rows, width), f32), pltpu.VMEM((rows, width), f32),
                            pltpu.VMEM((block, width), bf16), pltpu.VMEM((block, width), bf16), pltpu.VMEM(out_w.shape, bf16),
                            pltpu.VMEM((2, half_pieces, piece_rows + out_rows, width), bf16),
                            pltpu.VMEM((2, half_pieces, piece_rows + out_rows, width), bf16),
                            pltpu.SemaphoreType.DMA((2 * half_pieces, 2))]
                           + [pltpu.VMEM((4 * half_pieces, out_rows, width), f32), pltpu.SemaphoreType.DMA((2,))] * (out_rows > 0),
        ),
        out_shape=[shape((2, half_pieces, piece_rows + out_rows, width), bf16), shape((2, half_pieces, piece_rows + out_rows, width), bf16), shape((1, 2 * held), f32), shape((rows, width), bf16),
                   shape((rows, width), f32), shape((mols, width, 2 * half), bf16),
                   shape((width, width), f32), shape((2, width), f32)],
        compiler_params=pltpu.CompilerParams(vmem_limit_bytes=vmem_bytes),
        cost_estimate=pl.CostEstimate(flops=14 * 10**9, bytes_accessed=14 * 10**6, transcendentals=2 * 10**6),
        name="feed",
    )(place, normed, middle, own_grad, other_grad, valid, attended_t, norms, out_w, up_own, down_own, first, second, bias)


def score_kernel(
    prob_ref, grad_t_ref, read_t_ref, value_ref, key_t_ref, query_t_ref, type_t_ref, after_ref,
    query_grad_ref, key_grad_ref, value_grad_ref, pair_grad_ref,
):
    molecule = pl.program_id(1)
    heads, slots = prob_ref.shape[1], prob_ref.shape[2]
    span = grad_t_ref.shape[1]
    head_width = span // heads
    scale = head_width**-0.5
    values = value_ref[0, 0]
    grads = grad_t_ref[0]
    keys = key_t_ref[0]
    queries = query_t_ref[0]
    kinds = type_t_ref[0]
    count = kinds.shape[0]
    owner = lax.broadcasted_iota(jnp.int32, (span, slots), 0) // head_width
    wide_grads = grads.astype(f32)
    zero = jnp.zeros_like(wide_grads)
    dotted = wide_grads * read_t_ref[0]

    def pair_of(array, head):
        return array[(head // 2) * 16 : (head // 2) * 16 + 16]

    def own_half(both, head):
        return both[0:8] if head % 2 == 0 else both[8:16]

    def prob_grads(head):
        return mxu(values, jnp.where(owner == head, wide_grads, zero).astype(bf16))

    def score_grads(head, prob_grad):
        center = jnp.sum(dotted[head * head_width : (head + 1) * head_width], axis=0, keepdims=True)
        return (prob_ref[0, head].astype(f32) * (prob_grad - center)).astype(bf16)

    query_parts, key_parts, value_parts, type_parts = [], [], [], []

    def products(head, score_grad):
        left = jnp.concatenate([pair_of(keys, head), kinds], axis=0)
        both = mxu(left, score_grad)
        query_parts.append(own_half(both, head) * scale)
        type_parts.append(both[16:])
        key_parts.append(own_half(mxu(pair_of(queries, head), score_grad, NT), head) * scale)

    ahead = 3
    waiting = [prob_grads(head) for head in range(ahead)]
    done = []
    for head in range(heads):
        done.append(score_grads(head, waiting[head]))
        value_parts.append(own_half(mxu(pair_of(grads, head), prob_ref[0, head], NT), head))
        if head + ahead < heads:
            waiting.append(prob_grads(head + ahead))
        if head:
            products(head - 1, done[head - 1])
    products(heads - 1, done[heads - 1])
    query_grad_ref[0] = jnp.concatenate(query_parts, axis=0).astype(bf16)
    key_grad_ref[0] = jnp.concatenate(key_parts, axis=0).astype(bf16)
    value_grad_ref[0] = jnp.concatenate(value_parts, axis=0).astype(bf16)
    high, low = two_parts(jnp.concatenate(type_parts, axis=0))
    pairs = mxu(kinds, high, NT) + mxu(kinds, low, NT)

    @pl.when(molecule == 0)
    def _():
        pair_grad_ref[...] = pairs

    @pl.when(molecule > 0)
    def _():
        pair_grad_ref[...] += pairs


def attend_back(first, count, probs, grad_t, read_t, values, key_t, query_t, type_t, after):
    mols, all_heads, slots, _ = probs.shape
    groups = values.shape[1]
    heads = all_heads // groups
    width = grad_t.shape[1]
    span = width // groups
    kinds = type_t.shape[1]
    rows = pl.BlockSpec((1, span, slots), lambda g, m: (m, first + g, 0))
    new_rows = pl.BlockSpec((1, span, slots), lambda g, m: (m, g, 0))
    shape = jax.ShapeDtypeStruct
    part = shape((mols, count * span, slots), bf16)
    return pl.pallas_call(
        score_kernel,
        grid=(count, mols),
        in_specs=[pl.BlockSpec((1, heads, slots, slots), lambda g, m: (m, first + g, 0, 0)), rows, rows,
                  pl.BlockSpec((1, 1, slots, span), lambda g, m: (m, first + g, 0, 0)), rows, rows,
                  pl.BlockSpec((1, kinds, slots), lambda g, m: (m, 0, 0)), pl.BlockSpec(memory_space=pl.ANY)],
        out_specs=[new_rows, new_rows, new_rows, pl.BlockSpec((kinds, heads * kinds), lambda g, m: (0, g))],
        out_shape=[part, part, part, shape((kinds, count * heads * kinds), f32)],
        compiler_params=pltpu.CompilerParams(vmem_limit_bytes=vmem_bytes),
        cost_estimate=pl.CostEstimate(flops=5 * 10**9 * count, bytes_accessed=3 * 10**6 * count, transcendentals=0),
        name="attend_back",
    )(probs, grad_t, read_t, values, key_t, query_t, type_t, after)


def project_kernel(
    pieces, calls, place_ref, normed_t_ref, weight_ref, own_ref, other_ref, middle_grad_ref, norm_ref, norm_two_ref, bias_grad_ref, after_ref, *refs,
):
    part_refs, refs = refs[: 4 * calls], refs[4 * calls :]
    keep_ref, send_ref, own_out_ref, other_out_ref, ordered, grad_t_ref = refs
    part_rows = part_refs[0].shape[1]
    for call in range(calls):
        for kind in range(3):
            start = kind * part_rows * calls + call * part_rows
            grad_t_ref[:, start : start + part_rows] = part_refs[4 * call + kind][...]
    pair_refs = part_refs[3::4]
    per_pair = pair_refs[0].shape[1] // 128
    me = place_ref[2]
    mols, width, slots = normed_t_ref.shape
    half = slots // 2
    rows = width // pieces
    block = 256
    for start in range(0, width, block):
        total = sum(mxu(normed_t_ref[m, start : start + block], grad_t_ref[m], NT) for m in range(mols))
        for piece in range(block // rows):
            ordered[start // rows + piece, :, 0 : total.shape[1]] = total[piece * rows : (piece + 1) * rows]
    weight = weight_ref[...].astype(bf16)
    gain_grad, offset_grad = 0.0, 0.0
    for m in range(mols):
        normed_grad = mxu(weight, grad_t_ref[m]).T
        unit, inverse = norm_parts(jnp.concatenate([own_ref[place_ref[1] * mols + m], other_ref[m]], axis=0).astype(f32))
        gain_grad += jnp.sum(normed_grad * unit, axis=0, keepdims=True)
        offset_grad += jnp.sum(normed_grad, axis=0, keepdims=True)
        result = middle_grad_ref[m * slots : (m + 1) * slots] + norm_back(normed_grad, unit, inverse, norm_ref[0:1])
        own_out_ref[m] = result[:half]
        other_out_ref[m] = result[half:].astype(bf16)
    columns = weight_ref.shape[1]
    kinds = pair_refs[0].shape[0]
    for chunk in range(width // kinds):
        at = chunk % per_pair * 128
        ordered[:, chunk, columns : columns + 128] = pair_refs[chunk // per_pair][:, at : at + 128]
    bias = bias_grad_ref[...]
    held = bias.shape[1] // 2
    side = place_ref[1].astype(f32)
    turned = jnp.concatenate([bias[:, held:], bias[:, :held]], axis=1)
    bias = bias * (1.0 - side) + turned * side
    rest = [bias[:, start : start + width] for start in range(0, 2 * held, width)]
    vectors = [gain_grad, offset_grad, norm_two_ref[...]] + rest + [jnp.zeros((128 - 4 - len(rest), width), f32)]
    vectors = jnp.concatenate(vectors, axis=0)
    ordered[:, :, columns + 128 : columns + 256] = vectors.T.reshape(kinds, width // kinds, 128)
    core = place_ref[0]
    count = pieces // 2
    for piece in range(count):
        at = jnp.bitwise_xor(piece, me)
        keep_ref[at] = ordered[core * count + piece].astype(bf16)
        send_ref[at] = ordered[(1 - core) * count + piece].astype(bf16)


def project_back(place, parts, normed_t, weight, own, other, middle_grad, norms, norm_two, bias_grad, after, pieces):
    mols, width, slots = normed_t.shape
    columns = weight.shape[1]
    shape = jax.ShapeDtypeStruct
    vmem = pl.BlockSpec(memory_space=pltpu.VMEM)
    return pl.pallas_call(
        functools.partial(project_kernel, pieces, len(parts)),
        in_specs=[pl.BlockSpec(memory_space=pltpu.SMEM)] + [vmem] * 8 + [pl.BlockSpec(memory_space=pl.ANY)] + [vmem] * 4 * len(parts),
        out_specs=[vmem] * 4,
        out_shape=[shape((pieces // 2, width // pieces, columns + 256), bf16), shape((pieces // 2, width // pieces, columns + 256), bf16),
                   shape((mols, slots // 2, width), f32),
                   shape((mols, slots // 2, width), bf16)],
        scratch_shapes=[pltpu.VMEM((pieces, width // pieces, columns + 256), f32), pltpu.VMEM((mols, columns, slots), bf16)],
        compiler_params=pltpu.CompilerParams(vmem_limit_bytes=vmem_bytes),
        cost_estimate=pl.CostEstimate(flops=4 * 10**9, bytes_accessed=10 * 10**6, transcendentals=0),
        name="project_back",
    )(place, normed_t, weight, own, other, middle_grad, norms, norm_two, bias_grad, after, *[array for part in parts for array in part])


def swap(array, axis, bit, size):
    return lax.ppermute(array, axis, [(i, i ^ (1 << bit)) for i in range(size)])


def add_low(left, right):
    return (left.astype(f32) + right.astype(f32)).astype(bf16)


def tied(array, after):
    return array if after is None else lax.optimization_barrier((array, after))[0]


def halve(array, axes, digit, sizes, after=None):
    index = axes.index(digit)
    keep = lax.index_in_dim(array, 0, index, keepdims=False)
    send = lax.index_in_dim(array, 1, index, keepdims=False)
    return add_low(tied(keep, after), swap(send, *digit, sizes[digit[0]])), axes[:index] + axes[index + 1 :]


def jump(array, digits, sizes):
    axis = digits[0][0]
    mask = sum(1 << bit for _, bit in digits)
    return lax.ppermute(array, axis, [(i, i ^ mask) for i in range(sizes[axis])])


def quarter(array, axes, pair, sizes, after=None):
    first, second = axes.index(pair[0]), axes.index(pair[1])
    array = jnp.moveaxis(array, (first, second), (0, 1))
    total = tied(array[0, 0], after).astype(f32)
    for place, digits in (((1, 0), pair[:1]), ((0, 1), pair[1:]), ((1, 1), pair)):
        total = total + jump(array[place], digits, sizes).astype(f32)
    return total.astype(bf16), [digit for digit in axes if digit not in pair]


def double(array, digit, sizes, after=None):
    return jnp.stack([tied(array, after), swap(array, *digit, sizes[digit[0]])])


def quadruple(array, pair, sizes, after=None):
    pieces = [tied(array, after)] + [jump(array, digits, sizes) for digits in (pair[1:], pair[:1], pair)]
    return jnp.stack(pieces).reshape((2, 2) + array.shape)


def split_middle(digits):
    middle = digits[1:-1]
    return middle[: len(middle) % 2], [middle[i : i + 2] for i in range(len(middle) % 2, len(middle), 2)]


def scatter_first(array, digits, sizes, after=None):
    cut = array.shape[-1] // 2
    left, _ = halve(array[..., :cut], digits, digits[0], sizes, after)
    right, _ = halve(array[..., cut:], digits, digits[-1], sizes, after)
    return left, right


def scatter_second(parts, digits, sizes, after=None):
    left, _ = halve(parts[0], digits[1:], digits[-1], sizes, after)
    right, _ = halve(parts[1], digits[:-1], digits[0], sizes, after)
    return jnp.concatenate([left, right], axis=-1)


def scatter_middle(both, digits, sizes, after=None):
    single, pairs = split_middle(digits)
    axes = digits[1:-1]
    for pair in pairs[::-1]:
        both, axes = quarter(both, axes, pair, sizes, after)
    for digit in single:
        both, axes = halve(both, axes, digit, sizes)
    return both


def gather_middle(both, digits, sizes, after=None):
    single, pairs = split_middle(digits)
    for digit in single:
        both = double(both, digit, sizes)
    for pair in pairs:
        both = quadruple(both, pair, sizes, after)
    return both


def gather_second(both, digits, sizes, after=None):
    cut = both.shape[-1] // 2
    return double(both[..., :cut], digits[-1], sizes, after), double(both[..., cut:], digits[0], sizes, after)


def gather_first(parts, digits, sizes, after=None):
    left = double(parts[0], digits[0], sizes, after)
    right = double(parts[1], digits[-1], sizes, after)
    return left, jnp.swapaxes(right, 0, 1)


def beside(parts):
    return jnp.concatenate(parts, axis=-1)


def gather_order(digits):
    single, pairs = split_middle(digits)
    return [digits[0], digits[-1]] + [digit for pair in pairs[::-1] for digit in pair] + single


def place_list(order, digits):
    result = []
    for number in range(2 ** len(order)):
        bits = {digit: (number >> (len(order) - 1 - i)) & 1 for i, digit in enumerate(order)}
        result.append(sum(bits[digit] << (len(digits) - 1 - i) for i, digit in enumerate(digits)))
    return result


def absolute(array, digits, places):
    for index, (axis, bit) in enumerate(digits):
        flag = (places[axis] >> bit) & 1
        array = jnp.where(flag == 1, jnp.flip(array, index), array)
    return array


def muon_load(high_ref, low_ref, source_ref, scale, tall):
    block = 256
    for start in range(0, source_ref.shape[0], block):
        at = slice(start, start + block)
        high_ref[at], low_ref[at] = two_parts(source_ref[at] * scale)


def symmetric_product(left, right):
    half = left.shape[0] // 2
    left_high, left_low = two_parts(left)
    right_high, right_low = two_parts(right)
    rows = jnp.concatenate([left_high, left_low, left_high], axis=1)
    columns = jnp.concatenate([right_high, right_high, right_low], axis=0)
    top = mxu(rows[:half], columns)
    corner = mxu(rows[half:], columns[:, half:])
    return jnp.concatenate([top, jnp.concatenate([top[:, half:].T, corner], axis=1)], axis=0)


def muon_product(tall, steps, high_ref, low_ref, gram_ref, poly_ref, product_ref):
    size = gram_ref.shape[0]
    row = lax.broadcasted_iota(jnp.int32, (size, size), 0)
    column = lax.broadcasted_iota(jnp.int32, (size, size), 1)

    def polynomial():
        gram = gram_ref[...]
        poly_ref[...] = coef_second * gram + coef_third * symmetric_product(gram, gram)

    def inner(index, carry):
        poly = poly_ref[...]
        gram = gram_ref[...]
        step = coef_first * gram + symmetric_product(poly, gram)
        gram_ref[...] = coef_first * step + symmetric_product(poly, step)
        polynomial()
        product = product_ref[...]
        product_ref[...] = coef_first * product + symmetric_product(poly_ref[...], product)
        return carry

    if tall:
        both = mxu(high_ref[...], jnp.concatenate([high_ref[...], low_ref[...]], axis=1), TN)
    else:
        both = mxu(high_ref[...], jnp.concatenate([high_ref[...], low_ref[...]], axis=0), NT)
    crossing = both[:, size:]
    gram_ref[...] = both[:, :size] + crossing + crossing.T
    polynomial()
    product_ref[...] = poly_ref[...] + jnp.where(row == column, coef_first, 0.0)
    if not isinstance(steps, int) or steps > 1:
        lax.fori_loop(0, steps - 1, inner, 0)


def muon_blocks(tall, high_ref, low_ref, product_ref, length):
    high, low = two_parts(product_ref[...])
    block = 256
    if tall:
        right = jnp.concatenate([high, high, low], axis=0)
    else:
        left = jnp.concatenate([high, high, low], axis=1)
    for start in range(0, length, block):
        at = slice(start, start + block)
        if tall:
            left = jnp.concatenate([high_ref[at], low_ref[at], high_ref[at]], axis=1)
        else:
            right = jnp.concatenate([high_ref[:, at], low_ref[:, at], high_ref[:, at]], axis=0)
        yield at, mxu(left, right)


def inverse_norm(values):
    return 1.0 / (jnp.sqrt(jnp.full((1, 1), values, f32)) + 1e-07)


def muon_scratch(shape, size):
    return [pltpu.VMEM(shape, bf16), pltpu.VMEM(shape, bf16)] + [pltpu.VMEM((size, size), f32)] * 3


def copies_of(pairs, semaphores):
    copies = [pltpu.make_async_copy(source, target, semaphores.at[index]) for index, (source, target) in enumerate(pairs)]
    for copy in copies:
        copy.start()
    return copies


def muon_feed_kernel(
    numbers, place_ref, sum_ref, own_state_ref, other_state_ref, direction_ref,
    sums, own_state, other_state, direction, moment, high, low, gram, poly, product, semaphores, out_semaphores,
):
    me = place_ref[4]
    held, width = own_state.shape
    count = len(numbers) // 2
    rows = held // count
    incoming = copies_of(
        [(sum_ref.at[0:count], sums.at[0:count]), (own_state_ref, own_state),
         (sum_ref.at[count : 2 * count], sums.at[count : 2 * count]), (other_state_ref, other_state)],
        semaphores,
    )
    total = jnp.zeros((1, width), f32)
    for index, number in enumerate(numbers):
        if index % count == 0:
            incoming[2 * (index // count)].wait()
            incoming[2 * (index // count) + 1].wait()
        state_ref = own_state if index < count else other_state
        start = pl.multiple_of(jnp.bitwise_xor(number % count, me) * rows, rows)
        state = state_ref[pl.ds(start, rows), :].astype(f32)
        value = momentum_keep * state + sums[index, 0:rows].astype(f32)
        moment[pl.ds(start + (0 if index < count else held), rows), :] = value
        total += jnp.sum(value * value, axis=0, keepdims=True)
    muon_load(high, low, moment, inverse_norm(jnp.sum(total)), True)
    muon_product(True, 3, high, low, gram, poly, product)
    for at, value in muon_blocks(True, high, low, product, 2 * held):
        high[at], low[at] = two_parts(value)
    muon_product(True, 2, high, low, gram, poly, product)
    outgoing = []
    for at, value in muon_blocks(True, high, low, product, held):
        direction[at] = value.astype(bf16)
        outgoing += copies_of([(direction.at[at], direction_ref.at[at])], out_semaphores.at[pl.ds(len(outgoing), 1)])
    for copy in outgoing:
        copy.wait()


def muon_feed(place, sums, own_state, other_state, numbers):
    held, width = own_state.shape
    any_memory = pl.BlockSpec(memory_space=pl.ANY)
    return pl.pallas_call(
        functools.partial(muon_feed_kernel, numbers),
        in_specs=[pl.BlockSpec(memory_space=pltpu.SMEM)] + [any_memory] * 3,
        out_specs=any_memory,
        out_shape=jax.ShapeDtypeStruct((held, width), bf16),
        scratch_shapes=[pltpu.VMEM(sums.shape, bf16), pltpu.VMEM((held, width), f32), pltpu.VMEM((held, width), bf16),
                        pltpu.VMEM((held, width), bf16), pltpu.VMEM((2 * held, width), f32)]
                       + muon_scratch((2 * held, width), width)
                       + [pltpu.SemaphoreType.DMA((4,)), pltpu.SemaphoreType.DMA((held // 256,))],
        compiler_params=pltpu.CompilerParams(vmem_limit_bytes=vmem_bytes),
        cost_estimate=pl.CostEstimate(flops=26 * 10**9, bytes_accessed=8 * 10**6, transcendentals=0),
        name="muon_feed",
    )(place, sums, own_state, other_state)


def muon_whole_kernel(
    numbers, plan, rate, me_ref, sum_ref, swapped_ref, state_ref, weight_ref, moment_ref, updated_ref,
    sums, swapped, state, weight, high, low, gram, poly, product, semaphores, out_semaphores,
):
    me = me_ref[0]
    rows = sums.shape[1]
    columns = state.shape[1]
    incoming = copies_of([(state_ref, state), (sum_ref, sums), (swapped_ref, swapped), (weight_ref, weight)], semaphores)
    for copy in incoming[:3]:
        copy.wait()
    total = jnp.zeros((1, columns), f32)
    for core_place, ref in enumerate((sums, swapped)):
        for index, number in enumerate(numbers):
            number += core_place * len(numbers)
            start = pl.multiple_of(jnp.bitwise_xor(number, me) * rows, rows)
            value = momentum_keep * state[pl.ds(start, rows), :] + ref[index, :, 0:columns].astype(f32)
            state[pl.ds(start, rows), :] = value
            total += jnp.sum(value * value, axis=0, keepdims=True)
    moment_out = copies_of([(state, moment_ref)], out_semaphores.at[pl.ds(0, 1)])
    muon_load(high, low, state, inverse_norm(jnp.sum(total)), False)

    def outer(index, carry):
        muon_product(False, plan[0] if len(set(plan)) == 1 else plan[0] - index, high, low, gram, poly, product)
        for at, value in muon_blocks(False, high, low, product, columns):
            high[:, at], low[:, at] = two_parts(value)
        return carry

    lax.fori_loop(0, len(plan), outer, 0)
    incoming[3].wait()
    outgoing = moment_out
    for start in range(0, weight.shape[0], 64):
        at = slice(start, start + 64)
        weight[at] = weight[at] - rate * (high[at].astype(f32) + low[at].astype(f32))
        outgoing = outgoing + copies_of([(weight.at[at], updated_ref.at[at])], out_semaphores.at[pl.ds(len(outgoing), 1)])
    for copy in outgoing:
        copy.wait()


def muon_whole(me, sums, swapped, state, weight, numbers, plan, rate):
    any_memory = pl.BlockSpec(memory_space=pl.ANY)
    shape = jax.ShapeDtypeStruct(state.shape, f32)
    return pl.pallas_call(
        functools.partial(muon_whole_kernel, numbers, plan, rate),
        in_specs=[pl.BlockSpec(memory_space=pltpu.SMEM)] + [any_memory] * 4,
        out_specs=[any_memory] * 2,
        out_shape=[shape, shape],
        scratch_shapes=[pltpu.VMEM(sums.shape, bf16), pltpu.VMEM(sums.shape, bf16), pltpu.VMEM(state.shape, f32),
                        pltpu.VMEM(state.shape, f32)]
                       + muon_scratch(state.shape, state.shape[0])
                       + [pltpu.SemaphoreType.DMA((4,)), pltpu.SemaphoreType.DMA((1 + state.shape[0] // 64,))],
        compiler_params=pltpu.CompilerParams(vmem_limit_bytes=vmem_bytes),
        cost_estimate=pl.CostEstimate(flops=state.size * 25000, bytes_accessed=16 * 10**6, transcendentals=0),
        name="muon_whole",
    )(me, sums, swapped, state, weight)


def feed_moments_kernel(
    numbers, place_ref, own_ref, swapped_ref, up_state_ref, down_state_ref, up_ref, down_ref,
    own, swapped, up_state, down_state, up_sum, down_sum, in_semaphores, out_semaphores,
):
    me = place_ref[4]
    core = place_ref[0]
    _, rows, _ = own.shape
    block = 256
    blocks = [slice(start, start + block) for start in range(0, up_sum.shape[0], block)]
    sums = copies_of([(own_ref, own), (swapped_ref, swapped)], in_semaphores.at[pl.ds(0, 2)])
    states = []
    for at in blocks:
        pairs = [(up_state_ref.at[:, at], up_state.at[:, at]), (down_state_ref.at[at], down_state.at[at])]
        states.append(copies_of(pairs, in_semaphores.at[pl.ds(2 + 2 * len(states), 2)]))
    for copy in sums:
        copy.wait()

    def write(up_from, down_from):
        for index, number in enumerate(numbers):
            start = pl.multiple_of(jnp.bitwise_xor(number, me) * rows, rows)
            up_sum[pl.ds(start, rows), :] = up_from[index].astype(f32)
            down_sum[pl.ds(start, rows), :] = down_from[index].astype(f32)

    @pl.when(core == 0)
    def _():
        write(own, swapped)

    @pl.when(core == 1)
    def _():
        write(swapped, own)

    results = []
    for index, at in enumerate(blocks):
        for copy in states[index]:
            copy.wait()
        up_state[:, at] = momentum_keep * up_state[:, at] + up_sum[at].T
        down_state[at] = momentum_keep * down_state[at] + down_sum[at]
        pairs = [(up_state.at[:, at], up_ref.at[:, at]), (down_state.at[at], down_ref.at[at])]
        results += copies_of(pairs, out_semaphores.at[pl.ds(2 * index, 2)])
    for copy in results:
        copy.wait()


def feed_moments(place, own, swapped, up_state, down_state, numbers):
    any_memory = pl.BlockSpec(memory_space=pl.ANY)
    blocks = down_state.shape[0] // 256
    return pl.pallas_call(
        functools.partial(feed_moments_kernel, numbers),
        in_specs=[pl.BlockSpec(memory_space=pltpu.SMEM)] + [any_memory] * 4,
        out_specs=[any_memory] * 2,
        out_shape=[jax.ShapeDtypeStruct(up_state.shape, f32), jax.ShapeDtypeStruct(down_state.shape, f32)],
        scratch_shapes=[pltpu.VMEM(own.shape, bf16), pltpu.VMEM(own.shape, bf16), pltpu.VMEM(up_state.shape, f32)]
                       + [pltpu.VMEM(down_state.shape, f32)] * 3
                       + [pltpu.SemaphoreType.DMA((2 + 2 * blocks,)), pltpu.SemaphoreType.DMA((2 * blocks,))],
        compiler_params=pltpu.CompilerParams(vmem_limit_bytes=vmem_bytes),
        cost_estimate=pl.CostEstimate(flops=10**6, bytes_accessed=10 * 10**6, transcendentals=0),
        name="feed_moments",
    )(place, own, swapped, up_state, down_state)


def feed_update_kernel(
    rate_first, rate_second, place_ref, own_ref, swapped_ref, up_weight_ref, down_weight_ref, up_ref, down_ref,
    both, up_weight, down_weight, in_semaphores, out_semaphores,
):
    core = place_ref[0]
    block = 256
    blocks = [slice(start, start + block) for start in range(0, down_weight.shape[0], block)]
    incoming = []
    for at in blocks:
        pairs = [(own_ref.at[at], both.at[core, at]), (swapped_ref.at[at], both.at[1 - core, at]),
                 (up_weight_ref.at[:, at], up_weight.at[:, at]), (down_weight_ref.at[at], down_weight.at[at])]
        incoming.append(copies_of(pairs, in_semaphores.at[pl.ds(4 * len(incoming), 4)]))
    results = []
    for index, at in enumerate(blocks):
        for copy in incoming[index]:
            copy.wait()
        up_weight[:, at] = up_weight[:, at] - rate_first * both[0, at].astype(f32).T
        down_weight[at] = down_weight[at] - rate_second * both[1, at].astype(f32)
        pairs = [(up_weight.at[:, at], up_ref.at[:, at]), (down_weight.at[at], down_ref.at[at])]
        results += copies_of(pairs, out_semaphores.at[pl.ds(2 * index, 2)])
    for copy in results:
        copy.wait()


def feed_update(place, own, swapped, up_weight, down_weight, rate_first, rate_second):
    any_memory = pl.BlockSpec(memory_space=pl.ANY)
    blocks = down_weight.shape[0] // 256
    return pl.pallas_call(
        functools.partial(feed_update_kernel, rate_first, rate_second),
        in_specs=[pl.BlockSpec(memory_space=pltpu.SMEM)] + [any_memory] * 4,
        out_specs=[any_memory] * 2,
        out_shape=[jax.ShapeDtypeStruct(up_weight.shape, f32), jax.ShapeDtypeStruct(down_weight.shape, f32)],
        scratch_shapes=[pltpu.VMEM((2,) + own.shape, bf16), pltpu.VMEM(up_weight.shape, f32), pltpu.VMEM(down_weight.shape, f32),
                        pltpu.SemaphoreType.DMA((4 * blocks,)), pltpu.SemaphoreType.DMA((2 * blocks,))],
        compiler_params=pltpu.CompilerParams(vmem_limit_bytes=vmem_bytes),
        cost_estimate=pl.CostEstimate(flops=10**6, bytes_accessed=10 * 10**6, transcendentals=0),
        name="feed_update",
    )(place, own, swapped, up_weight, down_weight)


def step_factor(rows, columns):
    return math.sqrt(max(1.0, rows / columns))


def on_device(
    dp_size, mp_size,
    atoms, atom_counts, hydrogen, atom_types, cotangent, qkv_weight, out_weight, up_weight, down_weight, ffn_bias, norm_params,
    pair_table, qkv_state, out_state, up_state, down_state, bias_state, norm_state, pair_state,
):
    sizes = {"dp": dp_size, "mp": mp_size}
    place_dp, place_mp = lax.axis_index("dp"), lax.axis_index("mp")
    places = {"dp": place_dp, "mp": place_mp}
    core = place_dp & 1
    dp_bits = dp_size.bit_length() - 1
    mols, half, width = atoms.shape
    mine = mols // 2
    slots = 2 * half
    types_count, _, head_count = pair_table.shape
    kinds = 32

    def other_slots(array):
        return swap(lax.dynamic_slice_in_dim(array, (1 - place_mp) * mine, mine, 0), "mp", 0, mp_size)

    atoms_other = other_slots(atoms)
    up_own = up_weight.T.astype(bf16)
    down_own = down_weight.astype(bf16)
    bias_other = swap(ffn_bias, "mp", 0, mp_size)
    leaving_grad = lax.dynamic_slice_in_dim(cotangent, (1 - place_mp) * mine, mine, 0).reshape(-1, width)
    leaving = jnp.concatenate([jnp.where(core == 0, up_own, down_own), leaving_grad], axis=0)
    leaving, atoms_other, bias_other = lax.optimization_barrier((leaving, atoms_other, bias_other))
    crossed = swap(leaving, "mp", 0, mp_size)
    cot_other = crossed[up_own.shape[0] :].reshape(mine, half, width)
    bias_rel = jnp.concatenate([ffn_bias, bias_other])[None]

    scalars = jnp.concatenate([jnp.stack([core, place_mp]).astype(jnp.int32), atom_counts])
    (probs, read_t, query_t, key_t, values, normed_t, attended_t, middle, normed_two, own_state, leaving_state, type_t, valid) = attend(
        scalars, atoms, atoms_other, qkv_weight, norm_params, pair_table, atom_types, hydrogen, out_weight, up_state, down_state
    )
    crossed, normed_two = lax.optimization_barrier((crossed, normed_two))
    crossed_again = swap(crossed, "dp", 0, dp_size)
    other_state = swap(leaving_state, "mp", 0, mp_size)

    core_digit = ("dp", 0)
    half_digits = [("dp", bit) for bit in range(dp_bits - 1, 0, -1)]
    half_pieces = dp_size // 2
    chip_digits = [("mp", 0)] + half_digits
    some_digits = chip_digits[-4:]
    plain_digits = chip_digits[:-4]
    pieces = 2 ** (1 + len(some_digits))
    half_place = place_dp >> 1
    some_place = (place_mp * half_pieces + half_place) & (pieces // 2 - 1)
    piece_rows = up_own.shape[0] // half_pieces
    out_rows = width // (4 * half_pieces)
    aligned = out_rows % 16 == 0
    place = jnp.stack(
        [core, place_mp, some_place, core * (pieces // 2) + some_place, half_place, place_mp * half_pieces + half_place]
    ).astype(jnp.int32)

    rows = mine * slots
    (keep, send, bias_grad, mixed, middle_grad, attended_grad_t, out_grad, norm_grad_two) = feed(
        place, normed_two.reshape(rows, width), middle.reshape(rows, width), cotangent, cot_other, valid.reshape(rows, 1), attended_t,
        norm_params, out_weight, up_own, down_own, crossed, crossed_again, bias_rel, half_pieces, out_rows if aligned else 0,
    )

    digit_shape = (2,) * len(chip_digits)
    if not aligned:
        out_grad = out_grad.astype(bf16).reshape((2,) + digit_shape + (out_rows, width))
        out_grad = absolute(out_grad, [core_digit] + chip_digits, places).reshape((2, 2, half_pieces, out_rows, width))
        keep, send = jnp.concatenate([keep, out_grad[0]], axis=-2), jnp.concatenate([send, out_grad[1]], axis=-2)
    early = add_low(keep, swap(send, "dp", 0, dp_size)).reshape(digit_shape + (piece_rows + out_rows, width))
    early_ends = scatter_first(early, chip_digits, sizes)
    early_both = scatter_second(early_ends, chip_digits, sizes)

    def corner(*arrays):
        return jnp.stack([array[(0,) * (array.ndim - 2)][:16, :128] for array in arrays])

    groups = values.shape[1]
    calls = 4
    mixed = mixed.reshape(mine, slots, width)
    mixed_moved = swap(mixed[:, half:], "mp", 0, mp_size)
    waits = [place, corner(early), corner(early, mixed_moved), corner(*early_ends, other_state), corner(early_both)]
    parts = [
        attend_back(i * groups // calls, groups // calls, probs, attended_grad_t, read_t, values, key_t, query_t, type_t, waits[i])
        for i in range(calls)
    ]
    late_keep, late_send, atoms_grad_own, atoms_grad_other = project_back(
        place, parts, normed_t, qkv_weight, atoms, atoms_other, middle_grad, norm_params, norm_grad_two, bias_grad, waits[4], pieces
    )

    def own_last(array):
        return swap(array, "dp", 0, dp_size)

    def back_slots(own, moved):
        moved = moved.astype(own.dtype)
        return jnp.where(place_mp == 0, jnp.concatenate([own, moved], 0), jnp.concatenate([moved, own], 0))

    atoms_moved = swap(atoms_grad_other, "mp", 0, mp_size)
    early_order, late_order = gather_order(chip_digits), gather_order(some_digits)
    late = add_low(late_keep, own_last(late_send))
    late_shape = late.shape
    late = late.reshape((2,) * len(some_digits) + late_shape[1:])
    early_both = scatter_middle(early_both, chip_digits, sizes, late_keep)
    late_ends = scatter_first(late, some_digits, sizes)
    early_middle = gather_middle(early_both, chip_digits, sizes, late_ends)
    out_own = double(early_middle[..., piece_rows:, :], chip_digits[-1], sizes)
    late_both = scatter_second(late_ends, some_digits, sizes, out_own)
    early_half = gather_second(early_middle[..., :piece_rows, :], chip_digits, sizes, (late_both, atoms_moved))
    out_own = double(out_own, chip_digits[0], sizes, early_half).reshape((2 * half_pieces, out_rows, width))
    late_both = scatter_middle(late_both, some_digits, sizes, out_own)
    for axis, bit in plain_digits:
        late_both = add_low(late_both, swap(late_both, axis, bit, sizes[axis]))
    out_swapped = tied(own_last(out_own), late_both)
    out_numbers, out_me = place_list(early_order, chip_digits), core * 2 * half_pieces + place[5]
    if not aligned:
        out_sum = jnp.stack([out_own, out_swapped]).reshape((2,) + digit_shape + (out_rows, width))
        out_sum = absolute(out_sum, [core_digit] + early_order, places)
        spots = [0] + [1 + early_order.index(digit) for digit in chip_digits]
        out_sum = out_sum.transpose(spots + [len(spots), len(spots) + 1]).reshape(2, -1, 16, width)
        out_own, out_swapped = out_sum
        out_numbers, out_me = list(range(out_own.shape[0])), out_me * 0
    out_moment, out_updated = muon_whole(
        out_me[None].astype(jnp.int32), out_own, out_swapped, out_state, out_weight, out_numbers, (1, 1, 1, 1, 1),
        rate_out * step_factor(*out_weight.shape),
    )
    late_middle = gather_middle(late_both, some_digits, sizes, out_updated)
    mixed_out = back_slots(mixed[:, :half], mixed_moved)
    atoms_grad = back_slots(atoms_grad_own, atoms_moved)
    early_sum = beside(gather_first(early_half, chip_digits, sizes, (late_middle, mixed_out, atoms_grad)))
    early_sum = early_sum.reshape((2 * half_pieces, piece_rows, width))
    direction = muon_feed(place, early_sum, own_state, other_state, place_list(early_order, chip_digits))
    own_sum = early_sum[:half_pieces]
    own_numbers = place_list(early_order[1:], half_digits)
    late_half = gather_second(late_middle, some_digits, sizes, direction)
    up_moment, down_moment = feed_moments(place, tied(own_sum, late_half), own_last(own_sum), up_state, down_state, own_numbers)
    late_sum = beside(gather_first(late_half, some_digits, sizes, up_moment)).reshape(late_shape)
    hidden_units = mp_size * up_weight.shape[1]
    up_updated, down_updated = feed_update(
        place, tied(direction, late_sum), own_last(direction), up_weight, down_weight,
        rate_up * step_factor(width, hidden_units), rate_down * step_factor(hidden_units, width),
    )
    late_swapped = own_last(late_sum)
    late_sum = tied(late_sum, up_updated)
    qkv_moment, qkv_updated = muon_whole(
        place[3:4], late_sum, late_swapped, qkv_state, qkv_weight, place_list(late_order, some_digits), (3, 2),
        rate_qkv * step_factor(*qkv_weight.shape),
    )

    order = late_order
    small = jnp.stack([late_sum[..., 3 * width :], late_swapped[..., 3 * width :]])
    small = absolute(small.reshape((2,) * (1 + len(order)) + small.shape[2:]), [core_digit] + order, places)
    spots = (0,) + tuple(1 + order.index(digit) for digit in some_digits)
    small = small.transpose(spots + (len(spots), len(spots) + 1)).reshape(kinds, width // kinds, 256).astype(f32)
    pair_sum = small[..., :128].reshape(kinds, head_count, kinds).transpose(0, 2, 1)[:types_count, :types_count]
    pair_sum = lax.optimization_barrier(pair_sum)
    vectors = small[..., 128:136].reshape(width, 8).T
    norm_sum = vectors[:4]
    bias_sum = lax.dynamic_slice_in_dim(vectors[4:].reshape(-1), place_mp * ffn_bias.shape[0], ffn_bias.shape[0], 0)

    norm_moment = momentum_keep * norm_state + norm_sum
    norm_updated = norm_params - rate_norm * norm_moment
    bias_moment = momentum_keep * bias_state + bias_sum
    bias_updated = ffn_bias - rate_bias * bias_moment
    pair_moment = momentum_keep * pair_state + pair_sum
    pair_updated = pair_table - rate_pair * pair_moment

    return (
        mixed_out,
        atoms_grad,
        qkv_moment,
        qkv_updated,
        out_moment,
        out_updated,
        up_moment,
        up_updated,
        down_moment,
        down_updated,
        bias_moment,
        bias_updated,
        norm_moment,
        norm_updated,
        pair_moment,
        pair_updated,
    )


def solution(mesh):
    rows = P("dp", "mp", None)
    in_specs = (
        rows, P("dp"), P("dp", None), P("dp", None), rows, P(), P(), P(None, "mp"), P("mp", None), P("mp"), P(), P(),
        P(), P(), P(None, "mp"), P("mp", None), P("mp"), P(), P(),
    )
    out_specs = (
        rows, rows, P(), P(), P(), P(), P(None, "mp"), P(None, "mp"), P("mp", None), P("mp", None), P("mp"), P("mp"),
        P(), P(), P(), P(),
    )
    body = functools.partial(on_device, mesh.shape["dp"], mesh.shape["mp"])
    return jax.shard_map(body, mesh=mesh, in_specs=in_specs, out_specs=out_specs, check_vma=False)
```

```python
import functools
import math

import jax
import jax.numpy as jnp
from jax import lax
from jax.experimental import pallas as pl
from jax.experimental.pallas import tpu as pltpu
from jax.sharding import PartitionSpec as P

norm_eps = 1e-05
masked_score = -1000000000.0
coef_first = 3.4445
coef_second = -4.775
coef_third = 2.0315
momentum_keep = 0.5
rate_qkv = 1.0
rate_out = 4.0
rate_up = 1.0
rate_down = 1.0
rate_norm = 0.001
rate_bias = 0.01
rate_pair = 0.05

bf16 = jnp.bfloat16
f32 = jnp.float32
log2_e = 1.4426950408889634
NN = (((1,), (0,)), ((), ()))
NT = (((1,), (1,)), ((), ()))
TN = (((0,), (0,)), ((), ()))
vmem_bytes = 56 * 2**20
vmem_less = 50 * 2**20


def mxu(left, right, dims=NN):
    return lax.dot_general(left, right, dims, preferred_element_type=f32)


def norm_parts(values):
    center = values - jnp.mean(values, axis=-1, keepdims=True)
    inverse = lax.rsqrt(jnp.mean(center * center, axis=-1, keepdims=True) + norm_eps)
    return center * inverse, inverse


def norm_back(grad_rows, unit_rows, inverse, gain_vec):
    scaled = grad_rows * gain_vec
    mean_one = jnp.mean(scaled, axis=-1, keepdims=True)
    mean_two = jnp.mean(scaled * unit_rows, axis=-1, keepdims=True)
    return inverse * (scaled - mean_one - unit_rows * mean_two)


def two_parts(values):
    high = values.astype(bf16)
    return high, (values - high.astype(f32)).astype(bf16)


def attend_kernel(
    groups, state_steps, scalar_ref, own_ref, other_ref, qkv_w_ref, norm_ref, table_ref, type_all_ref, hydrogen_ref, out_w_ref,
    up_state_ref, down_state_ref,
    prob_ref, read_t_ref, query_t_ref, key_t_ref, value_ref, normed_t_ref, attended_t_ref, middle_ref, normed_two_ref,
    own_state_ref, leaving_ref, type_t_ref, valid_ref,
    left_all, query_high, query_low, value_t, table_wide, table_rows, bias_all, cap, read_all, qkv_low,
):
    step_index = pl.program_id(1)
    steps = pl.num_programs(1)
    core, side = scalar_ref[0], scalar_ref[1]
    molecule = side * pl.num_programs(0) + pl.program_id(0)
    count = scalar_ref[2 + molecule]
    slots = prob_ref.shape[2]
    width = own_ref.shape[2]
    half = slots // 2
    span = width // groups
    at_once = groups // steps
    heads = prob_ref.shape[1] // at_once
    kinds = type_t_ref.shape[1]

    def slot_row(ref):
        row = ref[pl.ds(molecule, 1), :].astype(f32)
        turned = jnp.concatenate([row[:, half:], row[:, :half]], axis=1)
        second = side.astype(f32)
        return row * (1.0 - second) + turned * second

    def load_rows():
        return jnp.concatenate([own_ref[0], other_ref[0]], axis=0).astype(f32)

    @pl.when((step_index == 0) & (pl.program_id(0) == 0))
    def _():
        qkv_low[...] = qkv_w_ref[...].astype(bf16)
        types, _, all_heads = table_ref.shape
        table_wide[...] = jnp.zeros_like(table_wide)
        for other in range(types):
            entries = jnp.concatenate([table_ref[:, other, :], jnp.zeros((kinds - types, all_heads), f32)], axis=0)
            entries = (entries.astype(bf16).astype(f32) * log2_e).T
            rounded = entries.astype(bf16).astype(f32)
            table_wide[:, other, :] = rounded
            table_wide[:, kinds + other, :] = entries - rounded
        for head in range(0, all_heads, 8):
            rows = table_wide[head : head + 8].reshape(16 * kinds, kinds)
            table_rows[head * 2 * kinds : (head + 8) * 2 * kinds] = rows.astype(bf16)

    @pl.when(step_index == 0)
    def _():
        unit, _ = norm_parts(load_rows())
        normed = unit * norm_ref[0:1] + norm_ref[1:2]
        normed_t_ref[0] = normed.T.astype(bf16)
        normed = normed.astype(bf16)
        query = mxu(normed, qkv_low[:, 0:width]).T.astype(bf16)
        query_t_ref[0] = query
        keys = mxu(normed, qkv_low[:, width : 2 * width])
        key_t_ref[0] = keys.T.astype(bf16)
        keys = keys.astype(bf16)
        values = mxu(normed, qkv_low[:, 2 * width :])
        value_t[...] = values.T.astype(bf16)
        values = values.astype(bf16)
        head_width = span // heads
        scaled = query.astype(f32) * (head_width**-0.5 * log2_e)
        high = scaled.astype(bf16).astype(f32)
        query_high[...] = high
        query_low[...] = scaled - high
        slot = lax.broadcasted_iota(jnp.int32, (1, slots), 1) + side * half
        slot = jnp.where(slot >= slots, slot - slots, slot)
        present = jnp.where(slot < count, 1.0, 0.0)
        usable = jnp.where(slot_row(hydrogen_ref) == 0.0, present, 0.0)
        line = lax.broadcasted_iota(jnp.int32, (128, slots), 0)
        marks = jnp.where(line.astype(f32) == slot_row(type_all_ref), 1.0, 0.0)
        marks = jnp.where(line == kinds, usable, jnp.where(line == kinds + 1, present, marks))
        columns = marks.T
        type_rows = marks[0:kinds].astype(bf16)
        type_t_ref[0] = type_rows
        type_columns = columns[:, 0:kinds].astype(bf16)
        valid = columns[:, kinds + 1 : kinds + 2]
        valid_ref[0] = valid
        bias_all[...] = mxu(table_rows[...], type_rows).astype(bf16)
        blank = jnp.zeros((slots, 256 - 2 * span - 2 * kinds), bf16)
        for index in range(groups):
            part = keys[:, span * index : span * (index + 1)]
            left_all[index] = jnp.concatenate([part, part, type_columns, type_columns, blank], axis=1)
            value_ref[0, index] = values[:, span * index : span * (index + 1)]
        row = lax.broadcasted_iota(jnp.int32, (slots, slots), 0)
        column = lax.broadcasted_iota(jnp.int32, (slots, slots), 1)
        cap[...] = jnp.where((columns[:, kinds : kinds + 1] > 0.0) | (row == column), 3e38, masked_score * log2_e)

    early = pl.program_id(0) * steps + step_index < state_steps

    def keep_state(state):
        own_state_ref[...] = state
        leaving_ref[...] = state.astype(bf16)

    @pl.when(early & (core == 0))
    def _():
        keep_state(up_state_ref[...].T)

    @pl.when(early & (core == 1))
    def _():
        keep_state(down_state_ref[...])

    for part in range(at_once):
        group = step_index * at_once + part
        left = left_all[group]
        owner = lax.broadcasted_iota(jnp.int32, (span, slots), 0) // (span // heads)
        start = pl.multiple_of(group * span, span)
        high = query_high[pl.ds(start, span), :]
        low = query_low[pl.ds(start, span), :]
        zero = jnp.zeros_like(high)
        blank = jnp.zeros((256 - 2 * span - 2 * kinds, slots), bf16)

        def scores(head):
            mine = owner == head
            place = pl.multiple_of((group * heads + head) * 2 * kinds, 2 * kinds)
            bias = bias_all[pl.ds(place, 2 * kinds), :]
            parts = [jnp.where(mine, high, zero).astype(bf16), jnp.where(mine, low, zero).astype(bf16), bias, blank]
            return mxu(left, jnp.concatenate(parts, axis=0))

        def softmax(head, logits):
            logits = jnp.minimum(logits, cap[...])
            raised = jnp.exp2(logits - jnp.max(logits, axis=0, keepdims=True))
            low_probs = (raised * (1.0 / jnp.sum(raised, axis=0, keepdims=True))).astype(bf16)
            prob_ref[0, heads * part + head] = low_probs
            return low_probs

        def weigh(head, low_probs):
            pair = value_t[pl.ds(pl.multiple_of(group * span + (head // 2) * 16, 16), 16), :]
            both = mxu(pair, low_probs)
            return both[0:8] if head % 2 == 0 else both[8:16]

        ahead = heads
        waiting = [scores(head) for head in range(ahead)]
        probs, results = [], []
        for head in range(heads):
            probs.append(softmax(head, waiting[head]))
            if head + ahead < heads:
                waiting.append(scores(head + ahead))
            if head:
                results.append(weigh(head - 1, probs[head - 1]))
        results.append(weigh(heads - 1, probs[heads - 1]))
        read = jnp.concatenate(results, axis=0)
        read_t_ref[0, span * part : span * (part + 1)] = read
        read_all[pl.ds(start, span), :] = read.astype(bf16)

    @pl.when(step_index == steps - 1)
    def _():
        attended = read_all[...]
        attended_t_ref[0] = attended
        middle = load_rows() + valid_ref[0] * mxu(attended, out_w_ref[...].astype(bf16), TN)
        middle_ref[0] = middle
        unit, _ = norm_parts(middle)
        normed_two_ref[0] = (unit * norm_ref[2:3] + norm_ref[3:4]).astype(bf16)


def attend(scalars, atoms, other, qkv_w, norms, table, types, hydrogen, out_w, up_state, down_state):
    mols, half, width = other.shape
    slots = 2 * half
    groups = 8
    heads = width // 8 // groups
    kinds = 32
    span = width // groups
    whole = lambda a: pl.BlockSpec(a.shape, lambda m, g, s: (0,) * a.ndim)
    each = lambda *shape: pl.BlockSpec((1,) + shape, lambda m, g, s: (m,) + (0,) * len(shape))
    at_once = 2
    steps = groups // at_once
    state_steps = mols * steps // 2
    state_rows = down_state.shape[0] // state_steps
    state_at = lambda m, g: jnp.minimum(m * steps + g, state_steps - 1)
    state_block = pl.BlockSpec((state_rows, width), lambda m, g, s: (state_at(m, g), 0))
    shape = jax.ShapeDtypeStruct
    rows = shape((mols, width, slots), bf16)
    return pl.pallas_call(
        functools.partial(attend_kernel, groups, state_steps),
        grid_spec=pltpu.PrefetchScalarGridSpec(
            num_scalar_prefetch=1,
            grid=(mols, steps),
            in_specs=[pl.BlockSpec((1, half, width), lambda m, g, s: (s[1] * mols + m, 0, 0)), each(half, width), whole(qkv_w),
                      whole(norms), whole(table), whole(types), whole(hydrogen), whole(out_w),
                      pl.BlockSpec((width, state_rows), lambda m, g, s: (0, state_at(m, g))), state_block],
            out_specs=[pl.BlockSpec((1, heads * at_once, slots, slots), lambda m, g, s: (m, g, 0, 0)),
                       pl.BlockSpec((1, span * at_once, slots), lambda m, g, s: (m, g, 0)),
                       each(width, slots), each(width, slots), each(groups, slots, span), each(width, slots), each(width, slots),
                       each(slots, width), each(slots, width), state_block, state_block, each(kinds, slots), each(slots, 1)],
            scratch_shapes=[pltpu.VMEM((groups, slots, 256), bf16), pltpu.VMEM((width, slots), f32), pltpu.VMEM((width, slots), f32),
                            pltpu.VMEM((width, slots), bf16), pltpu.VMEM((groups * heads, 2 * kinds, kinds), f32),
                            pltpu.VMEM((groups * heads * 2 * kinds, kinds), bf16),
                            pltpu.VMEM((groups * heads * 2 * kinds, slots), bf16), pltpu.VMEM((slots, slots), f32),
                            pltpu.VMEM((width, slots), bf16), pltpu.VMEM(qkv_w.shape, bf16)],
        ),
        out_shape=[shape((mols, groups * heads, slots, slots), bf16), shape((mols, width, slots), f32), rows, rows,
                   shape((mols, groups, slots, span), bf16), rows, rows, shape((mols, slots, width), f32),
                   shape((mols, slots, width), bf16), shape(down_state.shape, f32), shape(down_state.shape, bf16),
                   shape((mols, kinds, slots), bf16), shape((mols, slots, 1), f32)],
        compiler_params=pltpu.CompilerParams(vmem_limit_bytes=vmem_bytes),
        cost_estimate=pl.CostEstimate(flops=22 * 10**9, bytes_accessed=24 * 10**6, transcendentals=8 * 10**6),
        name="attend",
    )(scalars, atoms, other, qkv_w, norms, table, types, hydrogen, out_w, up_state, down_state)


def feed_kernel(
    piece_rows, out_rows, block_count,
    place_ref, normed_ref, middle_ref, own_grad_ref, other_grad_ref, valid_ref, attended_t_ref, norm_ref, out_w_ref,
    up_own_ref, down_own_ref, first_ref, second_ref, bias_ref,
    keep_out, send_out, bias_grad_ref, mixed_ref, middle_grad_ref, attended_grad_t_ref, out_grad_ref, norm_grad_ref,
    rows_grad, sum_out, sum_back, up_used, down_used, out_low, keep_ref, send_ref, semaphores, *ordered,
):
    step = pl.program_id(0)
    steps = pl.num_programs(0)
    core = place_ref[0]
    me = place_ref[4]
    mols, half, width = other_grad_ref.shape
    rows = mols * 2 * half

    def given():
        return jnp.concatenate([part for m in range(mols) for part in (own_grad_ref[m], other_grad_ref[m])], axis=0)

    @pl.when(step == 0)
    def _():
        rows_grad[...] = (valid_ref[...] * given().astype(f32)).astype(bf16)
        out_low[...] = out_w_ref[...].astype(bf16)
        sum_out[...] = jnp.zeros_like(sum_out)
        sum_back[...] = jnp.zeros_like(sum_back)

    is_own = step < steps // 2

    def choose(condition, up_ref, down_ref):
        @pl.when(condition)
        def _():
            up_used[...] = up_ref[...]
            down_used[...] = down_ref[...]

    choose(is_own, up_own_ref, down_own_ref)
    choose(jnp.logical_not(is_own) & (core == 0), first_ref, second_ref)
    choose(jnp.logical_not(is_own) & (core == 1), second_ref, first_ref)
    up = up_used[...]
    down = down_used[...]
    normed = normed_ref[...]
    grads = rows_grad[...]
    chunks = [slice(start, start + rows // 2) for start in (0, rows // 2)]
    firsts = [(mxu(normed[chunk], up, NT) + bias_ref[...], mxu(grads[chunk], down, NT)) for chunk in chunks]
    actives, hidden_grads = [], []
    for chunk, (hidden, back) in zip(chunks, firsts):
        cumulative = 0.5 * (1.0 + lax.erf(hidden * 0.7071067811865476))
        active = (hidden * cumulative).astype(bf16)
        slope = cumulative + hidden * jnp.exp(-0.5 * hidden * hidden) * 0.3989422804014327
        back = (back * slope).astype(bf16)
        sum_out[chunk] += mxu(active, down)
        sum_back[chunk] += mxu(back, up)
        actives.append(active)
        hidden_grads.append(back)
    activated = jnp.concatenate(actives, axis=0)
    hidden_grad = jnp.concatenate(hidden_grads, axis=0)
    up_grad = mxu(hidden_grad, normed, TN).astype(bf16)
    down_grad = mxu(activated, grads, TN).astype(bf16)
    bias_grad_ref[...] = jnp.sum(hidden_grad.astype(f32), axis=0, keepdims=True)
    block_rows = up.shape[0]
    place_half = step // (steps // 2)
    first_piece = step % (steps // 2) * (up.shape[0] // piece_rows)

    def place_rows(kept, sent):
        for piece in range(up.shape[0] // piece_rows):
            at = jnp.bitwise_xor(first_piece + piece, me)
            keep_ref[place_half, at, 0:piece_rows] = kept[piece * piece_rows : (piece + 1) * piece_rows]
            send_ref[place_half, at, 0:piece_rows] = sent[piece * piece_rows : (piece + 1) * piece_rows]

    @pl.when(core == 0)
    def _():
        place_rows(up_grad, down_grad)

    @pl.when(core == 1)
    def _():
        place_rows(down_grad, up_grad)

    def leaving(spot, number):
        pairs = [(keep_ref.at[spot], keep_out.at[spot]), (send_ref.at[spot], send_out.at[spot])]
        return [pltpu.make_async_copy(source, target, semaphores.at[number, index]) for index, (source, target) in enumerate(pairs)]

    def step_pieces(number):
        first = number % (steps // 2) * (block_rows // piece_rows)
        spots = [(number // (steps // 2), jnp.bitwise_xor(first + piece, me), slice(0, piece_rows)) for piece in range(block_rows // piece_rows)]
        return [copy for index, spot in enumerate(spots) for copy in leaving(spot, number * (block_rows // piece_rows) + index)]

    for copy in step_pieces(step):
        copy.start()

    @pl.when(step == steps - 1)
    def _():
        middle = middle_ref[...]
        valid = valid_ref[...]
        mixed_ref[...] = (middle + valid * sum_out[...]).astype(bf16)
        unit, inverse = norm_parts(middle)
        grad_two = sum_back[...]
        norm_grad_ref[0:1] = jnp.sum(grad_two * unit, axis=0, keepdims=True)
        norm_grad_ref[1:2] = jnp.sum(grad_two, axis=0, keepdims=True)
        middle_grad = given().astype(f32) + norm_back(grad_two, unit, inverse, norm_ref[2:3])
        middle_grad_ref[...] = middle_grad
        branch_grad = (valid * middle_grad).astype(bf16)
        total = None
        for m in range(mols):
            part = branch_grad[m * 2 * half : (m + 1) * 2 * half]
            attended_grad_t_ref[m] = mxu(out_low[...], part, NT).astype(bf16)
            term = mxu(attended_t_ref[m], part)
            total = term if total is None else total + term
        out_grad_ref[...] = total
        if out_rows:
            half_pieces = keep_ref.shape[1]
            count = 2 * half_pieces
            for piece in range(2 * count):
                ordered[0][piece] = total[piece * out_rows : (piece + 1) * out_rows]
            for piece in range(count):
                at = jnp.bitwise_xor(piece, place_ref[5])
                spot = (at // half_pieces, at % half_pieces, slice(piece_rows, piece_rows + out_rows))
                keep_ref[spot] = ordered[0][core * count + piece].astype(bf16)
                send_ref[spot] = ordered[0][(1 - core) * count + piece].astype(bf16)
            rest = slice(piece_rows, piece_rows + out_rows)
            pairs = [(keep_ref.at[:, :, rest], keep_out.at[:, :, rest]), (send_ref.at[:, :, rest], send_out.at[:, :, rest])]
            tail = [pltpu.make_async_copy(source, target, ordered[1].at[index]) for index, (source, target) in enumerate(pairs)]
            for copy in tail:
                copy.start()
            for copy in tail:
                copy.wait()
        for number in range(block_count):
            for copy in step_pieces(number):
                copy.wait()


def feed(place, normed, middle, own_grad, other_grad, valid, attended_t, norms, out_w, up_own, down_own, first, second, bias,
         half_pieces, out_rows):
    mols, half, width = other_grad.shape
    rows = mols * 2 * half
    held = up_own.shape[0]
    block = 512
    per_half = held // block
    steps = 2 * per_half
    piece_rows = held // half_pieces
    whole = lambda a: pl.BlockSpec(a.shape, lambda j, s: (0,) * a.ndim)
    fixed = lambda *s: pl.BlockSpec(s, lambda j, s_: (0,) * len(s))
    mine = pl.BlockSpec((block, width), lambda j, s: (jnp.minimum(j, per_half - 1), 0))
    theirs = pl.BlockSpec((block, width), lambda j, s: (jnp.maximum(j - per_half, 0), 0))
    shape = jax.ShapeDtypeStruct
    return pl.pallas_call(
        functools.partial(feed_kernel, piece_rows, out_rows, steps),
        grid_spec=pltpu.PrefetchScalarGridSpec(
            num_scalar_prefetch=1,
            grid=(steps,),
            in_specs=[whole(normed), whole(middle), pl.BlockSpec((mols, half, width), lambda j, s: (s[1], 0, 0)), whole(other_grad), whole(valid), whole(attended_t),
                      whole(norms), whole(out_w), mine, mine, theirs, theirs, pl.BlockSpec((1, block), lambda j, s: (0, j))],
            out_specs=[pl.BlockSpec(memory_space=pl.ANY), pl.BlockSpec(memory_space=pl.ANY),
                       pl.BlockSpec((1, block), lambda j, s: (0, j)),
                       fixed(rows, width), fixed(rows, width), fixed(mols, width, 2 * half),
                       fixed(width, width), fixed(2, width)],
            scratch_shapes=[pltpu.VMEM((rows, width), bf16), pltpu.VMEM((rows, width), f32), pltpu.VMEM((rows, width), f32),
                            pltpu.VMEM((block, width), bf16), pltpu.VMEM((block, width), bf16), pltpu.VMEM(out_w.shape, bf16),
                            pltpu.VMEM((2, half_pieces, piece_rows + out_rows, width), bf16),
                            pltpu.VMEM((2, half_pieces, piece_rows + out_rows, width), bf16),
                            pltpu.SemaphoreType.DMA((2 * half_pieces, 2))]
                           + [pltpu.VMEM((4 * half_pieces, out_rows, width), f32), pltpu.SemaphoreType.DMA((2,))] * (out_rows > 0),
        ),
        out_shape=[shape((2, half_pieces, piece_rows + out_rows, width), bf16), shape((2, half_pieces, piece_rows + out_rows, width), bf16), shape((1, 2 * held), f32), shape((rows, width), bf16),
                   shape((rows, width), f32), shape((mols, width, 2 * half), bf16),
                   shape((width, width), f32), shape((2, width), f32)],
        compiler_params=pltpu.CompilerParams(vmem_limit_bytes=vmem_bytes),
        cost_estimate=pl.CostEstimate(flops=14 * 10**9, bytes_accessed=14 * 10**6, transcendentals=2 * 10**6),
        name="feed",
    )(place, normed, middle, own_grad, other_grad, valid, attended_t, norms, out_w, up_own, down_own, first, second, bias)


def score_kernel(
    prob_ref, grad_t_ref, read_t_ref, value_ref, key_t_ref, query_t_ref, type_t_ref, after_ref,
    query_grad_ref, key_grad_ref, value_grad_ref, pair_grad_ref,
):
    molecule = pl.program_id(1)
    heads, slots = prob_ref.shape[1], prob_ref.shape[2]
    span = grad_t_ref.shape[1]
    head_width = span // heads
    scale = head_width**-0.5
    values = value_ref[0, 0]
    grads = grad_t_ref[0]
    keys = key_t_ref[0]
    queries = query_t_ref[0]
    kinds = type_t_ref[0]
    count = kinds.shape[0]
    owner = lax.broadcasted_iota(jnp.int32, (span, slots), 0) // head_width
    wide_grads = grads.astype(f32)
    zero = jnp.zeros_like(wide_grads)
    dotted = wide_grads * read_t_ref[0]

    def pair_of(array, head):
        return array[(head // 2) * 16 : (head // 2) * 16 + 16]

    def own_half(both, head):
        return both[0:8] if head % 2 == 0 else both[8:16]

    def prob_grads(head):
        return mxu(values, jnp.where(owner == head, wide_grads, zero).astype(bf16))

    def score_grads(head, prob_grad):
        center = jnp.sum(dotted[head * head_width : (head + 1) * head_width], axis=0, keepdims=True)
        return (prob_ref[0, head].astype(f32) * (prob_grad - center)).astype(bf16)

    query_parts, key_parts, value_parts, type_parts = [], [], [], []

    def products(head, score_grad):
        left = jnp.concatenate([pair_of(keys, head), kinds], axis=0)
        both = mxu(left, score_grad)
        query_parts.append(own_half(both, head) * scale)
        type_parts.append(both[16:])
        key_parts.append(own_half(mxu(pair_of(queries, head), score_grad, NT), head) * scale)

    ahead = 3
    waiting = [prob_grads(head) for head in range(ahead)]
    done = []
    for head in range(heads):
        done.append(score_grads(head, waiting[head]))
        value_parts.append(own_half(mxu(pair_of(grads, head), prob_ref[0, head], NT), head))
        if head + ahead < heads:
            waiting.append(prob_grads(head + ahead))
        if head:
            products(head - 1, done[head - 1])
    products(heads - 1, done[heads - 1])
    query_grad_ref[0] = jnp.concatenate(query_parts, axis=0).astype(bf16)
    key_grad_ref[0] = jnp.concatenate(key_parts, axis=0).astype(bf16)
    value_grad_ref[0] = jnp.concatenate(value_parts, axis=0).astype(bf16)
    high, low = two_parts(jnp.concatenate(type_parts, axis=0))
    pairs = mxu(kinds, high, NT) + mxu(kinds, low, NT)

    @pl.when(molecule == 0)
    def _():
        pair_grad_ref[...] = pairs

    @pl.when(molecule > 0)
    def _():
        pair_grad_ref[...] += pairs


def attend_back(first, count, probs, grad_t, read_t, values, key_t, query_t, type_t, after):
    mols, all_heads, slots, _ = probs.shape
    groups = values.shape[1]
    heads = all_heads // groups
    width = grad_t.shape[1]
    span = width // groups
    kinds = type_t.shape[1]
    rows = pl.BlockSpec((1, span, slots), lambda g, m: (m, first + g, 0))
    new_rows = pl.BlockSpec((1, span, slots), lambda g, m: (m, g, 0))
    shape = jax.ShapeDtypeStruct
    part = shape((mols, count * span, slots), bf16)
    return pl.pallas_call(
        score_kernel,
        grid=(count, mols),
        in_specs=[pl.BlockSpec((1, heads, slots, slots), lambda g, m: (m, first + g, 0, 0)), rows, rows,
                  pl.BlockSpec((1, 1, slots, span), lambda g, m: (m, first + g, 0, 0)), rows, rows,
                  pl.BlockSpec((1, kinds, slots), lambda g, m: (m, 0, 0)), pl.BlockSpec(memory_space=pl.ANY)],
        out_specs=[new_rows, new_rows, new_rows, pl.BlockSpec((kinds, heads * kinds), lambda g, m: (0, g))],
        out_shape=[part, part, part, shape((kinds, count * heads * kinds), f32)],
        compiler_params=pltpu.CompilerParams(vmem_limit_bytes=vmem_less),
        cost_estimate=pl.CostEstimate(flops=5 * 10**9 * count, bytes_accessed=3 * 10**6 * count, transcendentals=0),
        name="attend_back",
    )(probs, grad_t, read_t, values, key_t, query_t, type_t, after)


def project_kernel(
    pieces, calls, place_ref, normed_t_ref, weight_ref, own_ref, other_ref, middle_grad_ref, norm_ref, norm_two_ref, bias_grad_ref, after_ref, *refs,
):
    part_refs, refs = refs[: 4 * calls], refs[4 * calls :]
    keep_ref, send_ref, own_out_ref, other_out_ref, ordered, grad_t_ref = refs
    part_rows = part_refs[0].shape[1]
    for call in range(calls):
        for kind in range(3):
            start = kind * part_rows * calls + call * part_rows
            grad_t_ref[:, start : start + part_rows] = part_refs[4 * call + kind][...]
    pair_refs = part_refs[3::4]
    per_pair = pair_refs[0].shape[1] // 128
    me = place_ref[2]
    mols, width, slots = normed_t_ref.shape
    half = slots // 2
    rows = width // pieces
    block = 256
    for start in range(0, width, block):
        total = sum(mxu(normed_t_ref[m, start : start + block], grad_t_ref[m], NT) for m in range(mols))
        for piece in range(block // rows):
            ordered[start // rows + piece, :, 0 : total.shape[1]] = total[piece * rows : (piece + 1) * rows]
    weight = weight_ref[...].astype(bf16)
    gain_grad, offset_grad = 0.0, 0.0
    for m in range(mols):
        normed_grad = mxu(weight, grad_t_ref[m]).T
        unit, inverse = norm_parts(jnp.concatenate([own_ref[place_ref[1] * mols + m], other_ref[m]], axis=0).astype(f32))
        gain_grad += jnp.sum(normed_grad * unit, axis=0, keepdims=True)
        offset_grad += jnp.sum(normed_grad, axis=0, keepdims=True)
        result = middle_grad_ref[m * slots : (m + 1) * slots] + norm_back(normed_grad, unit, inverse, norm_ref[0:1])
        own_out_ref[m] = result[:half]
        other_out_ref[m] = result[half:].astype(bf16)
    columns = weight_ref.shape[1]
    kinds = pair_refs[0].shape[0]
    for chunk in range(width // kinds):
        at = chunk % per_pair * 128
        ordered[:, chunk, columns : columns + 128] = pair_refs[chunk // per_pair][:, at : at + 128]
    bias = bias_grad_ref[...]
    held = bias.shape[1] // 2
    side = place_ref[1].astype(f32)
    turned = jnp.concatenate([bias[:, held:], bias[:, :held]], axis=1)
    bias = bias * (1.0 - side) + turned * side
    rest = [bias[:, start : start + width] for start in range(0, 2 * held, width)]
    vectors = [gain_grad, offset_grad, norm_two_ref[...]] + rest + [jnp.zeros((128 - 4 - len(rest), width), f32)]
    vectors = jnp.concatenate(vectors, axis=0)
    ordered[:, :, columns + 128 : columns + 256] = vectors.T.reshape(kinds, width // kinds, 128)
    core = place_ref[0]
    count = pieces // 2
    for piece in range(count):
        at = jnp.bitwise_xor(piece, me)
        keep_ref[at] = ordered[core * count + piece].astype(bf16)
        send_ref[at] = ordered[(1 - core) * count + piece].astype(bf16)


def project_back(place, parts, normed_t, weight, own, other, middle_grad, norms, norm_two, bias_grad, after, pieces):
    mols, width, slots = normed_t.shape
    columns = weight.shape[1]
    shape = jax.ShapeDtypeStruct
    vmem = pl.BlockSpec(memory_space=pltpu.VMEM)
    return pl.pallas_call(
        functools.partial(project_kernel, pieces, len(parts)),
        in_specs=[pl.BlockSpec(memory_space=pltpu.SMEM)] + [vmem] * 8 + [pl.BlockSpec(memory_space=pl.ANY)] + [vmem] * 4 * len(parts),
        out_specs=[vmem] * 4,
        out_shape=[shape((pieces // 2, width // pieces, columns + 256), bf16), shape((pieces // 2, width // pieces, columns + 256), bf16),
                   shape((mols, slots // 2, width), f32),
                   shape((mols, slots // 2, width), bf16)],
        scratch_shapes=[pltpu.VMEM((pieces, width // pieces, columns + 256), f32), pltpu.VMEM((mols, columns, slots), bf16)],
        compiler_params=pltpu.CompilerParams(vmem_limit_bytes=vmem_less),
        cost_estimate=pl.CostEstimate(flops=4 * 10**9, bytes_accessed=10 * 10**6, transcendentals=0),
        name="project_back",
    )(place, normed_t, weight, own, other, middle_grad, norms, norm_two, bias_grad, after, *[array for part in parts for array in part])


def swap(array, axis, bit, size):
    return lax.ppermute(array, axis, [(i, i ^ (1 << bit)) for i in range(size)])


def add_low(left, right):
    return (left.astype(f32) + right.astype(f32)).astype(bf16)


def tied(array, after):
    return array if after is None else lax.optimization_barrier((array, after))[0]


def halve(array, axes, digit, sizes, after=None):
    index = axes.index(digit)
    keep = lax.index_in_dim(array, 0, index, keepdims=False)
    send = lax.index_in_dim(array, 1, index, keepdims=False)
    return add_low(tied(keep, after), swap(send, *digit, sizes[digit[0]])), axes[:index] + axes[index + 1 :]


def jump(array, digits, sizes):
    axis = digits[0][0]
    mask = sum(1 << bit for _, bit in digits)
    return lax.ppermute(array, axis, [(i, i ^ mask) for i in range(sizes[axis])])


def quarter(array, axes, pair, sizes, after=None):
    first, second = axes.index(pair[0]), axes.index(pair[1])
    array = jnp.moveaxis(array, (first, second), (0, 1))
    total = tied(array[0, 0], after).astype(f32)
    for place, digits in (((1, 0), pair[:1]), ((0, 1), pair[1:]), ((1, 1), pair)):
        total = total + jump(array[place], digits, sizes).astype(f32)
    return total.astype(bf16), [digit for digit in axes if digit not in pair]


def double(array, digit, sizes, after=None):
    return jnp.stack([tied(array, after), swap(array, *digit, sizes[digit[0]])])


def quadruple(array, pair, sizes, after=None):
    pieces = [tied(array, after)] + [jump(array, digits, sizes) for digits in (pair[1:], pair[:1], pair)]
    return jnp.stack(pieces).reshape((2, 2) + array.shape)


def split_middle(digits):
    middle = digits[1:-1]
    return middle[: len(middle) % 2], [middle[i : i + 2] for i in range(len(middle) % 2, len(middle), 2)]


def scatter_first(array, digits, sizes, after=None):
    cut = array.shape[-1] // 2
    left, _ = halve(array[..., :cut], digits, digits[0], sizes, after)
    right, _ = halve(array[..., cut:], digits, digits[-1], sizes, after)
    return left, right


def scatter_second(parts, digits, sizes, after=None):
    left, _ = halve(parts[0], digits[1:], digits[-1], sizes, after)
    right, _ = halve(parts[1], digits[:-1], digits[0], sizes, after)
    return jnp.concatenate([left, right], axis=-1)


def scatter_middle(both, digits, sizes, after=None):
    single, pairs = split_middle(digits)
    axes = digits[1:-1]
    for pair in pairs[::-1]:
        both, axes = quarter(both, axes, pair, sizes, after)
    for digit in single:
        both, axes = halve(both, axes, digit, sizes)
    return both


def gather_middle(both, digits, sizes, after=None):
    single, pairs = split_middle(digits)
    for digit in single:
        both = double(both, digit, sizes)
    for pair in pairs:
        both = quadruple(both, pair, sizes, after)
    return both


def gather_second(both, digits, sizes, after=None):
    cut = both.shape[-1] // 2
    return double(both[..., :cut], digits[-1], sizes, after), double(both[..., cut:], digits[0], sizes, after)


def gather_first(parts, digits, sizes, after=None):
    left = double(parts[0], digits[0], sizes, after)
    right = double(parts[1], digits[-1], sizes, after)
    return left, jnp.swapaxes(right, 0, 1)


def beside(parts):
    return jnp.concatenate(parts, axis=-1)


def gather_order(digits):
    single, pairs = split_middle(digits)
    return [digits[0], digits[-1]] + [digit for pair in pairs[::-1] for digit in pair] + single


def place_list(order, digits):
    result = []
    for number in range(2 ** len(order)):
        bits = {digit: (number >> (len(order) - 1 - i)) & 1 for i, digit in enumerate(order)}
        result.append(sum(bits[digit] << (len(digits) - 1 - i) for i, digit in enumerate(digits)))
    return result


def absolute(array, digits, places):
    for index, (axis, bit) in enumerate(digits):
        flag = (places[axis] >> bit) & 1
        array = jnp.where(flag == 1, jnp.flip(array, index), array)
    return array


def muon_load(high_ref, low_ref, source_ref, scale, tall):
    block = 256
    for start in range(0, source_ref.shape[0], block):
        at = slice(start, start + block)
        high_ref[at], low_ref[at] = two_parts(source_ref[at] * scale)


def symmetric_product(left, right):
    half = left.shape[0] // 2
    left_high, left_low = two_parts(left)
    right_high, right_low = two_parts(right)
    rows = jnp.concatenate([left_high, left_low, left_high], axis=1)
    columns = jnp.concatenate([right_high, right_high, right_low], axis=0)
    top = mxu(rows[:half], columns)
    corner = mxu(rows[half:], columns[:, half:])
    return jnp.concatenate([top, jnp.concatenate([top[:, half:].T, corner], axis=1)], axis=0)


def muon_product(tall, steps, high_ref, low_ref, gram_ref, poly_ref, product_ref):
    size = gram_ref.shape[0]
    row = lax.broadcasted_iota(jnp.int32, (size, size), 0)
    column = lax.broadcasted_iota(jnp.int32, (size, size), 1)

    def polynomial():
        gram = gram_ref[...]
        poly_ref[...] = coef_second * gram + coef_third * symmetric_product(gram, gram)

    def inner(index, carry):
        poly = poly_ref[...]
        gram = gram_ref[...]
        step = coef_first * gram + symmetric_product(poly, gram)
        gram_ref[...] = coef_first * step + symmetric_product(poly, step)
        polynomial()
        product = product_ref[...]
        product_ref[...] = coef_first * product + symmetric_product(poly_ref[...], product)
        return carry

    if tall:
        both = mxu(high_ref[...], jnp.concatenate([high_ref[...], low_ref[...]], axis=1), TN)
    else:
        both = mxu(high_ref[...], jnp.concatenate([high_ref[...], low_ref[...]], axis=0), NT)
    crossing = both[:, size:]
    gram_ref[...] = both[:, :size] + crossing + crossing.T
    polynomial()
    product_ref[...] = poly_ref[...] + jnp.where(row == column, coef_first, 0.0)
    if not isinstance(steps, int) or steps > 1:
        lax.fori_loop(0, steps - 1, inner, 0)


def muon_blocks(tall, high_ref, low_ref, product_ref, length):
    high, low = two_parts(product_ref[...])
    block = 256
    if tall:
        right = jnp.concatenate([high, high, low], axis=0)
    else:
        left = jnp.concatenate([high, high, low], axis=1)
    for start in range(0, length, block):
        at = slice(start, start + block)
        if tall:
            left = jnp.concatenate([high_ref[at], low_ref[at], high_ref[at]], axis=1)
        else:
            right = jnp.concatenate([high_ref[:, at], low_ref[:, at], high_ref[:, at]], axis=0)
        yield at, mxu(left, right)


def inverse_norm(values):
    return 1.0 / (jnp.sqrt(jnp.full((1, 1), values, f32)) + 1e-07)


def muon_scratch(shape, size):
    return [pltpu.VMEM(shape, bf16), pltpu.VMEM(shape, bf16)] + [pltpu.VMEM((size, size), f32)] * 3


def copies_of(pairs, semaphores):
    copies = [pltpu.make_async_copy(source, target, semaphores.at[index]) for index, (source, target) in enumerate(pairs)]
    for copy in copies:
        copy.start()
    return copies


def muon_feed_kernel(
    numbers, place_ref, sum_ref, own_state_ref, other_state_ref, direction_ref,
    sums, own_state, other_state, direction, moment, high, low, gram, poly, product, semaphores, out_semaphores,
):
    me = place_ref[4]
    held, width = own_state.shape
    count = len(numbers) // 2
    rows = held // count
    incoming = copies_of(
        [(sum_ref.at[0:count], sums.at[0:count]), (own_state_ref, own_state),
         (sum_ref.at[count : 2 * count], sums.at[count : 2 * count]), (other_state_ref, other_state)],
        semaphores,
    )
    total = jnp.zeros((1, width), f32)
    for index, number in enumerate(numbers):
        if index % count == 0:
            incoming[2 * (index // count)].wait()
            incoming[2 * (index // count) + 1].wait()
        state_ref = own_state if index < count else other_state
        start = pl.multiple_of(jnp.bitwise_xor(number % count, me) * rows, rows)
        state = state_ref[pl.ds(start, rows), :].astype(f32)
        value = momentum_keep * state + sums[index, 0:rows].astype(f32)
        moment[pl.ds(start + (0 if index < count else held), rows), :] = value
        total += jnp.sum(value * value, axis=0, keepdims=True)
    muon_load(high, low, moment, inverse_norm(jnp.sum(total)), True)
    muon_product(True, 3, high, low, gram, poly, product)
    for at, value in muon_blocks(True, high, low, product, 2 * held):
        high[at], low[at] = two_parts(value)
    muon_product(True, 2, high, low, gram, poly, product)
    outgoing = []
    for at, value in muon_blocks(True, high, low, product, held):
        direction[at] = value.astype(bf16)
        outgoing += copies_of([(direction.at[at], direction_ref.at[at])], out_semaphores.at[pl.ds(len(outgoing), 1)])
    for copy in outgoing:
        copy.wait()


def muon_feed(place, sums, own_state, other_state, numbers):
    held, width = own_state.shape
    any_memory = pl.BlockSpec(memory_space=pl.ANY)
    return pl.pallas_call(
        functools.partial(muon_feed_kernel, numbers),
        in_specs=[pl.BlockSpec(memory_space=pltpu.SMEM)] + [any_memory] * 3,
        out_specs=any_memory,
        out_shape=jax.ShapeDtypeStruct((held, width), bf16),
        scratch_shapes=[pltpu.VMEM(sums.shape, bf16), pltpu.VMEM((held, width), f32), pltpu.VMEM((held, width), bf16),
                        pltpu.VMEM((held, width), bf16), pltpu.VMEM((2 * held, width), f32)]
                       + muon_scratch((2 * held, width), width)
                       + [pltpu.SemaphoreType.DMA((4,)), pltpu.SemaphoreType.DMA((held // 256,))],
        compiler_params=pltpu.CompilerParams(vmem_limit_bytes=vmem_less),
        cost_estimate=pl.CostEstimate(flops=26 * 10**9, bytes_accessed=8 * 10**6, transcendentals=0),
        name="muon_feed",
    )(place, sums, own_state, other_state)


def muon_whole_kernel(
    numbers, plan, rate, me_ref, sum_ref, swapped_ref, state_ref, weight_ref, moment_ref, updated_ref,
    sums, swapped, state, weight, high, low, gram, poly, product, semaphores, out_semaphores,
):
    me = me_ref[0]
    rows = sums.shape[1]
    columns = state.shape[1]
    incoming = copies_of([(state_ref, state), (sum_ref, sums), (swapped_ref, swapped), (weight_ref, weight)], semaphores)
    for copy in incoming[:3]:
        copy.wait()
    total = jnp.zeros((1, columns), f32)
    for core_place, ref in enumerate((sums, swapped)):
        for index, number in enumerate(numbers):
            number += core_place * len(numbers)
            start = pl.multiple_of(jnp.bitwise_xor(number, me) * rows, rows)
            value = momentum_keep * state[pl.ds(start, rows), :] + ref[index, :, 0:columns].astype(f32)
            state[pl.ds(start, rows), :] = value
            total += jnp.sum(value * value, axis=0, keepdims=True)
    moment_out = copies_of([(state, moment_ref)], out_semaphores.at[pl.ds(0, 1)])
    muon_load(high, low, state, inverse_norm(jnp.sum(total)), False)

    def outer(index, carry):
        muon_product(False, plan[0] if len(set(plan)) == 1 else plan[0] - index, high, low, gram, poly, product)
        for at, value in muon_blocks(False, high, low, product, columns):
            high[:, at], low[:, at] = two_parts(value)
        return carry

    lax.fori_loop(0, len(plan), outer, 0)
    incoming[3].wait()
    outgoing = moment_out
    for start in range(0, weight.shape[0], 64):
        at = slice(start, start + 64)
        weight[at] = weight[at] - rate * (high[at].astype(f32) + low[at].astype(f32))
        outgoing = outgoing + copies_of([(weight.at[at], updated_ref.at[at])], out_semaphores.at[pl.ds(len(outgoing), 1)])
    for copy in outgoing:
        copy.wait()


def muon_whole(me, sums, swapped, state, weight, numbers, plan, rate):
    any_memory = pl.BlockSpec(memory_space=pl.ANY)
    shape = jax.ShapeDtypeStruct(state.shape, f32)
    return pl.pallas_call(
        functools.partial(muon_whole_kernel, numbers, plan, rate),
        in_specs=[pl.BlockSpec(memory_space=pltpu.SMEM)] + [any_memory] * 4,
        out_specs=[any_memory] * 2,
        out_shape=[shape, shape],
        scratch_shapes=[pltpu.VMEM(sums.shape, bf16), pltpu.VMEM(sums.shape, bf16), pltpu.VMEM(state.shape, f32),
                        pltpu.VMEM(state.shape, f32)]
                       + muon_scratch(state.shape, state.shape[0])
                       + [pltpu.SemaphoreType.DMA((4,)), pltpu.SemaphoreType.DMA((1 + state.shape[0] // 64,))],
        compiler_params=pltpu.CompilerParams(vmem_limit_bytes=vmem_less),
        cost_estimate=pl.CostEstimate(flops=state.size * 25000, bytes_accessed=16 * 10**6, transcendentals=0),
        name="muon_whole",
    )(me, sums, swapped, state, weight)


def feed_moments_kernel(
    numbers, place_ref, own_ref, swapped_ref, up_state_ref, down_state_ref, up_ref, down_ref,
    own, swapped, up_state, down_state, up_sum, down_sum, in_semaphores, out_semaphores,
):
    me = place_ref[4]
    core = place_ref[0]
    _, rows, _ = own.shape
    block = 256
    blocks = [slice(start, start + block) for start in range(0, up_sum.shape[0], block)]
    sums = copies_of([(own_ref, own), (swapped_ref, swapped)], in_semaphores.at[pl.ds(0, 2)])
    states = []
    for at in blocks:
        pairs = [(up_state_ref.at[:, at], up_state.at[:, at]), (down_state_ref.at[at], down_state.at[at])]
        states.append(copies_of(pairs, in_semaphores.at[pl.ds(2 + 2 * len(states), 2)]))
    for copy in sums:
        copy.wait()

    def write(up_from, down_from):
        for index, number in enumerate(numbers):
            start = pl.multiple_of(jnp.bitwise_xor(number, me) * rows, rows)
            up_sum[pl.ds(start, rows), :] = up_from[index].astype(f32)
            down_sum[pl.ds(start, rows), :] = down_from[index].astype(f32)

    @pl.when(core == 0)
    def _():
        write(own, swapped)

    @pl.when(core == 1)
    def _():
        write(swapped, own)

    results = []
    for index, at in enumerate(blocks):
        for copy in states[index]:
            copy.wait()
        up_state[:, at] = momentum_keep * up_state[:, at] + up_sum[at].T
        down_state[at] = momentum_keep * down_state[at] + down_sum[at]
        pairs = [(up_state.at[:, at], up_ref.at[:, at]), (down_state.at[at], down_ref.at[at])]
        results += copies_of(pairs, out_semaphores.at[pl.ds(2 * index, 2)])
    for copy in results:
        copy.wait()


def feed_moments(place, own, swapped, up_state, down_state, numbers):
    any_memory = pl.BlockSpec(memory_space=pl.ANY)
    blocks = down_state.shape[0] // 256
    return pl.pallas_call(
        functools.partial(feed_moments_kernel, numbers),
        in_specs=[pl.BlockSpec(memory_space=pltpu.SMEM)] + [any_memory] * 4,
        out_specs=[any_memory] * 2,
        out_shape=[jax.ShapeDtypeStruct(up_state.shape, f32), jax.ShapeDtypeStruct(down_state.shape, f32)],
        scratch_shapes=[pltpu.VMEM(own.shape, bf16), pltpu.VMEM(own.shape, bf16), pltpu.VMEM(up_state.shape, f32)]
                       + [pltpu.VMEM(down_state.shape, f32)] * 3
                       + [pltpu.SemaphoreType.DMA((2 + 2 * blocks,)), pltpu.SemaphoreType.DMA((2 * blocks,))],
        compiler_params=pltpu.CompilerParams(vmem_limit_bytes=vmem_less),
        cost_estimate=pl.CostEstimate(flops=10**6, bytes_accessed=10 * 10**6, transcendentals=0),
        name="feed_moments",
    )(place, own, swapped, up_state, down_state)


def feed_update_kernel(
    rate_first, rate_second, place_ref, own_ref, swapped_ref, up_weight_ref, down_weight_ref, up_ref, down_ref,
    both, up_weight, down_weight, in_semaphores, out_semaphores,
):
    core = place_ref[0]
    block = 256
    blocks = [slice(start, start + block) for start in range(0, down_weight.shape[0], block)]
    incoming = []
    for at in blocks:
        pairs = [(own_ref.at[at], both.at[core, at]), (swapped_ref.at[at], both.at[1 - core, at]),
                 (up_weight_ref.at[:, at], up_weight.at[:, at]), (down_weight_ref.at[at], down_weight.at[at])]
        incoming.append(copies_of(pairs, in_semaphores.at[pl.ds(4 * len(incoming), 4)]))
    results = []
    for index, at in enumerate(blocks):
        for copy in incoming[index]:
            copy.wait()
        up_weight[:, at] = up_weight[:, at] - rate_first * both[0, at].astype(f32).T
        down_weight[at] = down_weight[at] - rate_second * both[1, at].astype(f32)
        pairs = [(up_weight.at[:, at], up_ref.at[:, at]), (down_weight.at[at], down_ref.at[at])]
        results += copies_of(pairs, out_semaphores.at[pl.ds(2 * index, 2)])
    for copy in results:
        copy.wait()


def feed_update(place, own, swapped, up_weight, down_weight, rate_first, rate_second):
    any_memory = pl.BlockSpec(memory_space=pl.ANY)
    blocks = down_weight.shape[0] // 256
    return pl.pallas_call(
        functools.partial(feed_update_kernel, rate_first, rate_second),
        in_specs=[pl.BlockSpec(memory_space=pltpu.SMEM)] + [any_memory] * 4,
        out_specs=[any_memory] * 2,
        out_shape=[jax.ShapeDtypeStruct(up_weight.shape, f32), jax.ShapeDtypeStruct(down_weight.shape, f32)],
        scratch_shapes=[pltpu.VMEM((2,) + own.shape, bf16), pltpu.VMEM(up_weight.shape, f32), pltpu.VMEM(down_weight.shape, f32),
                        pltpu.SemaphoreType.DMA((4 * blocks,)), pltpu.SemaphoreType.DMA((2 * blocks,))],
        compiler_params=pltpu.CompilerParams(vmem_limit_bytes=vmem_less),
        cost_estimate=pl.CostEstimate(flops=10**6, bytes_accessed=10 * 10**6, transcendentals=0),
        name="feed_update",
    )(place, own, swapped, up_weight, down_weight)


def plain_update_kernel(rate, sum_ref, state_ref, weight_ref, moment_ref, updated_ref):
    moment = momentum_keep * state_ref[...] + sum_ref[...]
    moment_ref[...] = moment
    updated_ref[...] = weight_ref[...] - rate * moment


def plain_update(total, state, weight, rate):
    vmem = pl.BlockSpec(memory_space=pltpu.VMEM)
    shape = jax.ShapeDtypeStruct(state.shape, f32)
    return pl.pallas_call(
        functools.partial(plain_update_kernel, rate),
        in_specs=[vmem] * 3,
        out_specs=[vmem] * 2,
        out_shape=[shape, shape],
        compiler_params=pltpu.CompilerParams(vmem_limit_bytes=16 * 2**20),
        cost_estimate=pl.CostEstimate(flops=10**5, bytes_accessed=2 * 10**6, transcendentals=0),
        name="plain_update",
    )(total, state, weight)


def step_factor(rows, columns):
    return math.sqrt(max(1.0, rows / columns))


def on_device(
    dp_size, mp_size,
    atoms, atom_counts, hydrogen, atom_types, cotangent, qkv_weight, out_weight, up_weight, down_weight, ffn_bias, norm_params,
    pair_table, qkv_state, out_state, up_state, down_state, bias_state, norm_state, pair_state,
):
    sizes = {"dp": dp_size, "mp": mp_size}
    place_dp, place_mp = lax.axis_index("dp"), lax.axis_index("mp")
    places = {"dp": place_dp, "mp": place_mp}
    core = place_dp & 1
    dp_bits = dp_size.bit_length() - 1
    mols, half, width = atoms.shape
    mine = mols // 2
    slots = 2 * half
    types_count, _, head_count = pair_table.shape
    kinds = 32

    def other_slots(array):
        return swap(lax.dynamic_slice_in_dim(array, (1 - place_mp) * mine, mine, 0), "mp", 0, mp_size)

    atoms_other = other_slots(atoms)
    up_own = up_weight.T.astype(bf16)
    down_own = down_weight.astype(bf16)
    bias_other = swap(ffn_bias, "mp", 0, mp_size)
    leaving_grad = lax.dynamic_slice_in_dim(cotangent, (1 - place_mp) * mine, mine, 0).reshape(-1, width)
    leaving = jnp.concatenate([jnp.where(core == 0, up_own, down_own), leaving_grad], axis=0)
    leaving, atoms_other, bias_other = lax.optimization_barrier((leaving, atoms_other, bias_other))
    crossed = swap(leaving, "mp", 0, mp_size)
    cot_other = crossed[up_own.shape[0] :].reshape(mine, half, width)
    bias_rel = jnp.concatenate([ffn_bias, bias_other])[None]

    scalars = jnp.concatenate([jnp.stack([core, place_mp]).astype(jnp.int32), atom_counts])
    (probs, read_t, query_t, key_t, values, normed_t, attended_t, middle, normed_two, own_state, leaving_state, type_t, valid) = attend(
        scalars, atoms, atoms_other, qkv_weight, norm_params, pair_table, atom_types, hydrogen, out_weight, up_state, down_state
    )
    crossed, normed_two = lax.optimization_barrier((crossed, normed_two))
    crossed_again = swap(crossed, "dp", 0, dp_size)
    other_state = swap(leaving_state, "mp", 0, mp_size)

    core_digit = ("dp", 0)
    half_digits = [("dp", bit) for bit in range(dp_bits - 1, 0, -1)]
    half_pieces = dp_size // 2
    chip_digits = [("mp", 0)] + half_digits
    some_digits = chip_digits[-4:]
    plain_digits = chip_digits[:-4]
    pieces = 2 ** (1 + len(some_digits))
    half_place = place_dp >> 1
    some_place = (place_mp * half_pieces + half_place) & (pieces // 2 - 1)
    piece_rows = up_own.shape[0] // half_pieces
    out_rows = width // (4 * half_pieces)
    aligned = out_rows % 16 == 0
    place = jnp.stack(
        [core, place_mp, some_place, core * (pieces // 2) + some_place, half_place, place_mp * half_pieces + half_place]
    ).astype(jnp.int32)

    rows = mine * slots
    (keep, send, bias_grad, mixed, middle_grad, attended_grad_t, out_grad, norm_grad_two) = feed(
        place, normed_two.reshape(rows, width), middle.reshape(rows, width), cotangent, cot_other, valid.reshape(rows, 1), attended_t,
        norm_params, out_weight, up_own, down_own, crossed, crossed_again, bias_rel, half_pieces, out_rows if aligned else 0,
    )

    digit_shape = (2,) * len(chip_digits)
    if not aligned:
        out_grad = out_grad.astype(bf16).reshape((2,) + digit_shape + (out_rows, width))
        out_grad = absolute(out_grad, [core_digit] + chip_digits, places).reshape((2, 2, half_pieces, out_rows, width))
        keep, send = jnp.concatenate([keep, out_grad[0]], axis=-2), jnp.concatenate([send, out_grad[1]], axis=-2)
    early = add_low(keep, swap(send, "dp", 0, dp_size)).reshape(digit_shape + (piece_rows + out_rows, width))
    early_ends = scatter_first(early, chip_digits, sizes)
    early_both = scatter_second(early_ends, chip_digits, sizes)

    def corner(*arrays):
        return jnp.stack([array[(0,) * (array.ndim - 2)][:16, :128] for array in arrays])

    groups = values.shape[1]
    calls = 4
    mixed = mixed.reshape(mine, slots, width)
    mixed_moved = swap(mixed[:, half:], "mp", 0, mp_size)
    waits = [place, corner(early), corner(early, mixed_moved), corner(*early_ends, other_state), corner(early_both)]
    parts = [
        attend_back(i * groups // calls, groups // calls, probs, attended_grad_t, read_t, values, key_t, query_t, type_t, waits[i])
        for i in range(calls)
    ]
    late_keep, late_send, atoms_grad_own, atoms_grad_other = project_back(
        place, parts, normed_t, qkv_weight, atoms, atoms_other, middle_grad, norm_params, norm_grad_two, bias_grad, waits[4], pieces
    )

    def own_last(array):
        return swap(array, "dp", 0, dp_size)

    def back_slots(own, moved):
        moved = moved.astype(own.dtype)
        return jnp.where(place_mp == 0, jnp.concatenate([own, moved], 0), jnp.concatenate([moved, own], 0))

    atoms_moved = swap(atoms_grad_other, "mp", 0, mp_size)
    early_order, late_order = gather_order(chip_digits), gather_order(some_digits)
    late = add_low(late_keep, own_last(late_send))
    late_shape = late.shape
    late = late.reshape((2,) * len(some_digits) + late_shape[1:])
    early_both = scatter_middle(early_both, chip_digits, sizes, late_keep)
    late_ends = scatter_first(late, some_digits, sizes)
    early_middle = gather_middle(early_both, chip_digits, sizes, late_ends)
    out_own = double(early_middle[..., piece_rows:, :], chip_digits[-1], sizes)
    late_both = scatter_second(late_ends, some_digits, sizes, out_own)
    early_half = gather_second(early_middle[..., :piece_rows, :], chip_digits, sizes, (late_both, atoms_moved))
    out_own = double(out_own, chip_digits[0], sizes, early_half).reshape((2 * half_pieces, out_rows, width))
    late_both = scatter_middle(late_both, some_digits, sizes, out_own)
    for axis, bit in plain_digits:
        late_both = add_low(late_both, swap(late_both, axis, bit, sizes[axis]))
    out_swapped = tied(own_last(out_own), late_both)
    out_numbers, out_me = place_list(early_order, chip_digits), core * 2 * half_pieces + place[5]
    if not aligned:
        out_sum = jnp.stack([out_own, out_swapped]).reshape((2,) + digit_shape + (out_rows, width))
        out_sum = absolute(out_sum, [core_digit] + early_order, places)
        spots = [0] + [1 + early_order.index(digit) for digit in chip_digits]
        out_sum = out_sum.transpose(spots + [len(spots), len(spots) + 1]).reshape(2, -1, 16, width)
        out_own, out_swapped = out_sum
        out_numbers, out_me = list(range(out_own.shape[0])), out_me * 0
    out_moment, out_updated = muon_whole(
        out_me[None].astype(jnp.int32), out_own, out_swapped, out_state, out_weight, out_numbers, (1, 1, 1, 1, 1),
        rate_out * step_factor(*out_weight.shape),
    )
    late_middle = gather_middle(late_both, some_digits, sizes, out_updated)
    mixed_out = back_slots(mixed[:, :half], mixed_moved)
    atoms_grad = back_slots(atoms_grad_own, atoms_moved)
    early_sum = beside(gather_first(early_half, chip_digits, sizes, (late_middle, mixed_out, atoms_grad)))
    early_sum = early_sum.reshape((2 * half_pieces, piece_rows, width))
    direction = muon_feed(place, early_sum, own_state, other_state, place_list(early_order, chip_digits))
    own_sum = early_sum[:half_pieces]
    own_numbers = place_list(early_order[1:], half_digits)
    late_half = gather_second(late_middle, some_digits, sizes, direction)
    up_moment, down_moment = feed_moments(place, tied(own_sum, late_half), own_last(own_sum), up_state, down_state, own_numbers)
    late_sum = beside(gather_first(late_half, some_digits, sizes, up_moment)).reshape(late_shape)
    hidden_units = mp_size * up_weight.shape[1]
    up_updated, down_updated = feed_update(
        place, tied(direction, late_sum), own_last(direction), up_weight, down_weight,
        rate_up * step_factor(width, hidden_units), rate_down * step_factor(hidden_units, width),
    )
    late_swapped = own_last(late_sum)
    late_sum = tied(late_sum, up_updated)
    qkv_moment, qkv_updated = muon_whole(
        place[3:4], late_sum, late_swapped, qkv_state, qkv_weight, place_list(late_order, some_digits), (3, 2),
        rate_qkv * step_factor(*qkv_weight.shape),
    )

    order = late_order
    small = jnp.stack([late_sum[..., 3 * width :], late_swapped[..., 3 * width :]])
    small = absolute(small.reshape((2,) * (1 + len(order)) + small.shape[2:]), [core_digit] + order, places)
    spots = (0,) + tuple(1 + order.index(digit) for digit in some_digits)
    small = small.transpose(spots + (len(spots), len(spots) + 1)).reshape(kinds, width // kinds, 256).astype(f32)
    pair_sum = small[..., :128].reshape(kinds, head_count, kinds).transpose(0, 2, 1)[:types_count, :types_count]
    vectors = small[..., 128:136].reshape(width, 8).T
    norm_sum = vectors[:4]
    bias_sum = lax.dynamic_slice_in_dim(vectors[4:].reshape(-1), place_mp * ffn_bias.shape[0], ffn_bias.shape[0], 0)

    norm_moment = momentum_keep * norm_state + norm_sum
    norm_updated = norm_params - rate_norm * norm_moment
    bias_moment = momentum_keep * bias_state + bias_sum
    bias_updated = ffn_bias - rate_bias * bias_moment
    pair_moment, pair_updated = plain_update(pair_sum, pair_state, pair_table, rate_pair)

    return (
        mixed_out,
        atoms_grad,
        qkv_moment,
        qkv_updated,
        out_moment,
        out_updated,
        up_moment,
        up_updated,
        down_moment,
        down_updated,
        bias_moment,
        bias_updated,
        norm_moment,
        norm_updated,
        pair_moment,
        pair_updated,
    )


def solution(mesh):
    rows = P("dp", "mp", None)
    in_specs = (
        rows, P("dp"), P("dp", None), P("dp", None), rows, P(), P(), P(None, "mp"), P("mp", None), P("mp"), P(), P(),
        P(), P(), P(None, "mp"), P("mp", None), P("mp"), P(), P(),
    )
    out_specs = (
        rows, rows, P(), P(), P(), P(), P(None, "mp"), P(None, "mp"), P("mp", None), P("mp", None), P("mp"), P("mp"),
        P(), P(), P(), P(),
    )
    body = functools.partial(on_device, mesh.shape["dp"], mesh.shape["mp"])
    return jax.shard_map(body, mesh=mesh, in_specs=in_specs, out_specs=out_specs, check_vma=False)
```

```python
import functools
import math

import jax
import jax.numpy as jnp
from jax import lax
from jax.experimental import pallas as pl
from jax.experimental.pallas import tpu as pltpu
from jax.sharding import PartitionSpec as P

norm_eps = 1e-05
masked_score = -1000000000.0
coef_first = 3.4445
coef_second = -4.775
coef_third = 2.0315
momentum_keep = 0.5
rate_qkv = 1.0
rate_out = 4.0
rate_up = 1.0
rate_down = 1.0
rate_norm = 0.001
rate_bias = 0.01
rate_pair = 0.05

bf16 = jnp.bfloat16
f32 = jnp.float32
log2_e = 1.4426950408889634
NN = (((1,), (0,)), ((), ()))
NT = (((1,), (1,)), ((), ()))
TN = (((0,), (0,)), ((), ()))
vmem_bytes = 56 * 2**20
vmem_less = 50 * 2**20


def mxu(left, right, dims=NN):
    return lax.dot_general(left, right, dims, preferred_element_type=f32)


def norm_parts(values):
    center = values - jnp.mean(values, axis=-1, keepdims=True)
    inverse = lax.rsqrt(jnp.mean(center * center, axis=-1, keepdims=True) + norm_eps)
    return center * inverse, inverse


def norm_back(grad_rows, unit_rows, inverse, gain_vec):
    scaled = grad_rows * gain_vec
    mean_one = jnp.mean(scaled, axis=-1, keepdims=True)
    mean_two = jnp.mean(scaled * unit_rows, axis=-1, keepdims=True)
    return inverse * (scaled - mean_one - unit_rows * mean_two)


def two_parts(values):
    high = values.astype(bf16)
    return high, (values - high.astype(f32)).astype(bf16)


def attend_kernel(
    groups, state_steps, scalar_ref, own_ref, other_ref, qkv_w_ref, norm_ref, table_ref, type_all_ref, hydrogen_ref, out_w_ref,
    up_state_ref, down_state_ref,
    prob_ref, read_t_ref, query_t_ref, key_t_ref, value_ref, normed_t_ref, attended_t_ref, middle_ref, normed_two_ref,
    own_state_ref, leaving_ref, type_t_ref, valid_ref,
    left_all, query_high, query_low, value_t, table_wide, table_rows, bias_all, cap, read_all, qkv_low,
):
    step_index = pl.program_id(1)
    steps = pl.num_programs(1)
    core, side = scalar_ref[0], scalar_ref[1]
    molecule = side * pl.num_programs(0) + pl.program_id(0)
    count = scalar_ref[2 + molecule]
    slots = prob_ref.shape[2]
    width = own_ref.shape[2]
    half = slots // 2
    span = width // groups
    at_once = groups // steps
    heads = prob_ref.shape[1] // at_once
    kinds = type_t_ref.shape[1]

    def slot_row(ref):
        row = ref[pl.ds(molecule, 1), :].astype(f32)
        turned = jnp.concatenate([row[:, half:], row[:, :half]], axis=1)
        second = side.astype(f32)
        return row * (1.0 - second) + turned * second

    def load_rows():
        return jnp.concatenate([own_ref[0], other_ref[0]], axis=0).astype(f32)

    @pl.when((step_index == 0) & (pl.program_id(0) == 0))
    def _():
        qkv_low[...] = qkv_w_ref[...].astype(bf16)
        types, _, all_heads = table_ref.shape
        table_wide[...] = jnp.zeros_like(table_wide)
        for other in range(types):
            entries = jnp.concatenate([table_ref[:, other, :], jnp.zeros((kinds - types, all_heads), f32)], axis=0)
            entries = (entries.astype(bf16).astype(f32) * log2_e).T
            rounded = entries.astype(bf16).astype(f32)
            table_wide[:, other, :] = rounded
            table_wide[:, kinds + other, :] = entries - rounded
        for head in range(0, all_heads, 8):
            rows = table_wide[head : head + 8].reshape(16 * kinds, kinds)
            table_rows[head * 2 * kinds : (head + 8) * 2 * kinds] = rows.astype(bf16)

    @pl.when(step_index == 0)
    def _():
        unit, _ = norm_parts(load_rows())
        normed = unit * norm_ref[0:1] + norm_ref[1:2]
        normed_t_ref[0] = normed.T.astype(bf16)
        normed = normed.astype(bf16)
        query = mxu(normed, qkv_low[:, 0:width]).T.astype(bf16)
        query_t_ref[0] = query
        keys = mxu(normed, qkv_low[:, width : 2 * width])
        key_t_ref[0] = keys.T.astype(bf16)
        keys = keys.astype(bf16)
        values = mxu(normed, qkv_low[:, 2 * width :])
        value_t[...] = values.T.astype(bf16)
        values = values.astype(bf16)
        head_width = span // heads
        scaled = query.astype(f32) * (head_width**-0.5 * log2_e)
        high = scaled.astype(bf16).astype(f32)
        query_high[...] = high
        query_low[...] = scaled - high
        slot = lax.broadcasted_iota(jnp.int32, (1, slots), 1) + side * half
        slot = jnp.where(slot >= slots, slot - slots, slot)
        present = jnp.where(slot < count, 1.0, 0.0)
        usable = jnp.where(slot_row(hydrogen_ref) == 0.0, present, 0.0)
        line = lax.broadcasted_iota(jnp.int32, (128, slots), 0)
        marks = jnp.where(line.astype(f32) == slot_row(type_all_ref), 1.0, 0.0)
        marks = jnp.where(line == kinds, usable, jnp.where(line == kinds + 1, present, marks))
        columns = marks.T
        type_rows = marks[0:kinds].astype(bf16)
        type_t_ref[0] = type_rows
        type_columns = columns[:, 0:kinds].astype(bf16)
        valid = columns[:, kinds + 1 : kinds + 2]
        valid_ref[0] = valid
        bias_all[...] = mxu(table_rows[...], type_rows).astype(bf16)
        blank = jnp.zeros((slots, 256 - 2 * span - 2 * kinds), bf16)
        for index in range(groups):
            part = keys[:, span * index : span * (index + 1)]
            left_all[index] = jnp.concatenate([part, part, type_columns, type_columns, blank], axis=1)
            value_ref[0, index] = values[:, span * index : span * (index + 1)]
        row = lax.broadcasted_iota(jnp.int32, (slots, slots), 0)
        column = lax.broadcasted_iota(jnp.int32, (slots, slots), 1)
        cap[...] = jnp.where((columns[:, kinds : kinds + 1] > 0.0) | (row == column), 3e38, masked_score * log2_e)

    early = pl.program_id(0) * steps + step_index < state_steps

    def keep_state(state):
        own_state_ref[...] = state
        leaving_ref[...] = state.astype(bf16)

    @pl.when(early & (core == 0))
    def _():
        keep_state(up_state_ref[...].T)

    @pl.when(early & (core == 1))
    def _():
        keep_state(down_state_ref[...])

    for part in range(at_once):
        group = step_index * at_once + part
        left = left_all[group]
        owner = lax.broadcasted_iota(jnp.int32, (span, slots), 0) // (span // heads)
        start = pl.multiple_of(group * span, span)
        high = query_high[pl.ds(start, span), :]
        low = query_low[pl.ds(start, span), :]
        zero = jnp.zeros_like(high)
        blank = jnp.zeros((256 - 2 * span - 2 * kinds, slots), bf16)

        def scores(head):
            mine = owner == head
            place = pl.multiple_of((group * heads + head) * 2 * kinds, 2 * kinds)
            bias = bias_all[pl.ds(place, 2 * kinds), :]
            parts = [jnp.where(mine, high, zero).astype(bf16), jnp.where(mine, low, zero).astype(bf16), bias, blank]
            return mxu(left, jnp.concatenate(parts, axis=0))

        def softmax(head, logits):
            logits = jnp.minimum(logits, cap[...])
            raised = jnp.exp2(logits - jnp.max(logits, axis=0, keepdims=True))
            low_probs = (raised * (1.0 / jnp.sum(raised, axis=0, keepdims=True))).astype(bf16)
            prob_ref[0, heads * part + head] = low_probs
            return low_probs

        def weigh(head, low_probs):
            pair = value_t[pl.ds(pl.multiple_of(group * span + (head // 2) * 16, 16), 16), :]
            both = mxu(pair, low_probs)
            return both[0:8] if head % 2 == 0 else both[8:16]

        ahead = heads
        waiting = [scores(head) for head in range(ahead)]
        probs, results = [], []
        for head in range(heads):
            probs.append(softmax(head, waiting[head]))
            if head + ahead < heads:
                waiting.append(scores(head + ahead))
            if head:
                results.append(weigh(head - 1, probs[head - 1]))
        results.append(weigh(heads - 1, probs[heads - 1]))
        read = jnp.concatenate(results, axis=0)
        read_t_ref[0, span * part : span * (part + 1)] = read
        read_all[pl.ds(start, span), :] = read.astype(bf16)

    @pl.when(step_index == steps - 1)
    def _():
        attended = read_all[...]
        attended_t_ref[0] = attended
        middle = load_rows() + valid_ref[0] * mxu(attended, out_w_ref[...].astype(bf16), TN)
        middle_ref[0] = middle
        unit, _ = norm_parts(middle)
        normed_two_ref[0] = (unit * norm_ref[2:3] + norm_ref[3:4]).astype(bf16)


def attend(scalars, atoms, other, qkv_w, norms, table, types, hydrogen, out_w, up_state, down_state):
    mols, half, width = other.shape
    slots = 2 * half
    groups = 8
    heads = width // 8 // groups
    kinds = 32
    span = width // groups
    whole = lambda a: pl.BlockSpec(a.shape, lambda m, g, s: (0,) * a.ndim)
    each = lambda *shape: pl.BlockSpec((1,) + shape, lambda m, g, s: (m,) + (0,) * len(shape))
    at_once = 2
    steps = groups // at_once
    state_steps = mols * steps // 2
    state_rows = down_state.shape[0] // state_steps
    state_at = lambda m, g: jnp.minimum(m * steps + g, state_steps - 1)
    state_block = pl.BlockSpec((state_rows, width), lambda m, g, s: (state_at(m, g), 0))
    shape = jax.ShapeDtypeStruct
    rows = shape((mols, width, slots), bf16)
    return pl.pallas_call(
        functools.partial(attend_kernel, groups, state_steps),
        grid_spec=pltpu.PrefetchScalarGridSpec(
            num_scalar_prefetch=1,
            grid=(mols, steps),
            in_specs=[pl.BlockSpec((1, half, width), lambda m, g, s: (s[1] * mols + m, 0, 0)), each(half, width), whole(qkv_w),
                      whole(norms), whole(table), whole(types), whole(hydrogen), whole(out_w),
                      pl.BlockSpec((width, state_rows), lambda m, g, s: (0, state_at(m, g))), state_block],
            out_specs=[pl.BlockSpec((1, heads * at_once, slots, slots), lambda m, g, s: (m, g, 0, 0)),
                       pl.BlockSpec((1, span * at_once, slots), lambda m, g, s: (m, g, 0)),
                       each(width, slots), each(width, slots), each(groups, slots, span), each(width, slots), each(width, slots),
                       each(slots, width), each(slots, width), state_block, state_block, each(kinds, slots), each(slots, 1)],
            scratch_shapes=[pltpu.VMEM((groups, slots, 256), bf16), pltpu.VMEM((width, slots), f32), pltpu.VMEM((width, slots), f32),
                            pltpu.VMEM((width, slots), bf16), pltpu.VMEM((groups * heads, 2 * kinds, kinds), f32),
                            pltpu.VMEM((groups * heads * 2 * kinds, kinds), bf16),
                            pltpu.VMEM((groups * heads * 2 * kinds, slots), bf16), pltpu.VMEM((slots, slots), f32),
                            pltpu.VMEM((width, slots), bf16), pltpu.VMEM(qkv_w.shape, bf16)],
        ),
        out_shape=[shape((mols, groups * heads, slots, slots), bf16), shape((mols, width, slots), f32), rows, rows,
                   shape((mols, groups, slots, span), bf16), rows, rows, shape((mols, slots, width), f32),
                   shape((mols, slots, width), bf16), shape(down_state.shape, f32), shape(down_state.shape, bf16),
                   shape((mols, kinds, slots), bf16), shape((mols, slots, 1), f32)],
        compiler_params=pltpu.CompilerParams(vmem_limit_bytes=vmem_bytes),
        cost_estimate=pl.CostEstimate(flops=22 * 10**9, bytes_accessed=24 * 10**6, transcendentals=8 * 10**6),
        name="attend",
    )(scalars, atoms, other, qkv_w, norms, table, types, hydrogen, out_w, up_state, down_state)


def feed_kernel(
    piece_rows, out_rows, block_count,
    place_ref, normed_ref, middle_ref, own_grad_ref, other_grad_ref, valid_ref, attended_t_ref, norm_ref, out_w_ref,
    up_own_ref, down_own_ref, first_ref, second_ref, bias_ref,
    keep_out, send_out, bias_grad_ref, mixed_ref, middle_grad_ref, attended_grad_t_ref, out_grad_ref, norm_grad_ref,
    rows_grad, sum_out, sum_back, up_used, down_used, out_low, keep_ref, send_ref, semaphores, *ordered,
):
    step = pl.program_id(0)
    steps = pl.num_programs(0)
    core = place_ref[0]
    me = place_ref[4]
    mols, half, width = other_grad_ref.shape
    rows = mols * 2 * half

    def given():
        return jnp.concatenate([part for m in range(mols) for part in (own_grad_ref[m], other_grad_ref[m])], axis=0)

    @pl.when(step == 0)
    def _():
        rows_grad[...] = (valid_ref[...] * given().astype(f32)).astype(bf16)
        out_low[...] = out_w_ref[...].astype(bf16)
        sum_out[...] = jnp.zeros_like(sum_out)
        sum_back[...] = jnp.zeros_like(sum_back)

    is_own = step < steps // 2

    def choose(condition, up_ref, down_ref):
        @pl.when(condition)
        def _():
            up_used[...] = up_ref[...]
            down_used[...] = down_ref[...]

    choose(is_own, up_own_ref, down_own_ref)
    choose(jnp.logical_not(is_own) & (core == 0), first_ref, second_ref)
    choose(jnp.logical_not(is_own) & (core == 1), second_ref, first_ref)
    up = up_used[...]
    down = down_used[...]
    normed = normed_ref[...]
    grads = rows_grad[...]
    chunks = [slice(start, start + rows // 2) for start in (0, rows // 2)]
    firsts = [(mxu(normed[chunk], up, NT) + bias_ref[...], mxu(grads[chunk], down, NT)) for chunk in chunks]
    actives, hidden_grads = [], []
    for chunk, (hidden, back) in zip(chunks, firsts):
        cumulative = 0.5 * (1.0 + lax.erf(hidden * 0.7071067811865476))
        active = (hidden * cumulative).astype(bf16)
        slope = cumulative + hidden * jnp.exp(-0.5 * hidden * hidden) * 0.3989422804014327
        back = (back * slope).astype(bf16)
        sum_out[chunk] += mxu(active, down)
        sum_back[chunk] += mxu(back, up)
        actives.append(active)
        hidden_grads.append(back)
    activated = jnp.concatenate(actives, axis=0)
    hidden_grad = jnp.concatenate(hidden_grads, axis=0)
    up_grad = mxu(hidden_grad, normed, TN).astype(bf16)
    down_grad = mxu(activated, grads, TN).astype(bf16)
    bias_grad_ref[...] = jnp.sum(hidden_grad.astype(f32), axis=0, keepdims=True)
    block_rows = up.shape[0]
    place_half = step // (steps // 2)
    first_piece = step % (steps // 2) * (up.shape[0] // piece_rows)

    def place_rows(kept, sent):
        for piece in range(up.shape[0] // piece_rows):
            at = jnp.bitwise_xor(first_piece + piece, me)
            keep_ref[place_half, at, 0:piece_rows] = kept[piece * piece_rows : (piece + 1) * piece_rows]
            send_ref[place_half, at, 0:piece_rows] = sent[piece * piece_rows : (piece + 1) * piece_rows]

    @pl.when(core == 0)
    def _():
        place_rows(up_grad, down_grad)

    @pl.when(core == 1)
    def _():
        place_rows(down_grad, up_grad)

    def leaving(spot, number):
        pairs = [(keep_ref.at[spot], keep_out.at[spot]), (send_ref.at[spot], send_out.at[spot])]
        return [pltpu.make_async_copy(source, target, semaphores.at[number, index]) for index, (source, target) in enumerate(pairs)]

    def step_pieces(number):
        first = number % (steps // 2) * (block_rows // piece_rows)
        spots = [(number // (steps // 2), jnp.bitwise_xor(first + piece, me), slice(0, piece_rows)) for piece in range(block_rows // piece_rows)]
        return [copy for index, spot in enumerate(spots) for copy in leaving(spot, number * (block_rows // piece_rows) + index)]

    for copy in step_pieces(step):
        copy.start()

    @pl.when(step == steps - 1)
    def _():
        middle = middle_ref[...]
        valid = valid_ref[...]
        mixed_ref[...] = (middle + valid * sum_out[...]).astype(bf16)
        unit, inverse = norm_parts(middle)
        grad_two = sum_back[...]
        norm_grad_ref[0:1] = jnp.sum(grad_two * unit, axis=0, keepdims=True)
        norm_grad_ref[1:2] = jnp.sum(grad_two, axis=0, keepdims=True)
        middle_grad = given().astype(f32) + norm_back(grad_two, unit, inverse, norm_ref[2:3])
        middle_grad_ref[...] = middle_grad
        branch_grad = (valid * middle_grad).astype(bf16)
        total = None
        for m in range(mols):
            part = branch_grad[m * 2 * half : (m + 1) * 2 * half]
            attended_grad_t_ref[m] = mxu(out_low[...], part, NT).astype(bf16)
            term = mxu(attended_t_ref[m], part)
            total = term if total is None else total + term
        out_grad_ref[...] = total
        if out_rows:
            half_pieces = keep_ref.shape[1]
            count = 2 * half_pieces
            for piece in range(2 * count):
                ordered[0][piece] = total[piece * out_rows : (piece + 1) * out_rows]
            for piece in range(count):
                at = jnp.bitwise_xor(piece, place_ref[5])
                spot = (at // half_pieces, at % half_pieces, slice(piece_rows, piece_rows + out_rows))
                keep_ref[spot] = ordered[0][core * count + piece].astype(bf16)
                send_ref[spot] = ordered[0][(1 - core) * count + piece].astype(bf16)
            rest = slice(piece_rows, piece_rows + out_rows)
            pairs = [(keep_ref.at[:, :, rest], keep_out.at[:, :, rest]), (send_ref.at[:, :, rest], send_out.at[:, :, rest])]
            tail = [pltpu.make_async_copy(source, target, ordered[1].at[index]) for index, (source, target) in enumerate(pairs)]
            for copy in tail:
                copy.start()
            for copy in tail:
                copy.wait()
        for number in range(block_count):
            for copy in step_pieces(number):
                copy.wait()


def feed(place, normed, middle, own_grad, other_grad, valid, attended_t, norms, out_w, up_own, down_own, first, second, bias,
         half_pieces, out_rows):
    mols, half, width = other_grad.shape
    rows = mols * 2 * half
    held = up_own.shape[0]
    block = 512
    per_half = held // block
    steps = 2 * per_half
    piece_rows = held // half_pieces
    whole = lambda a: pl.BlockSpec(a.shape, lambda j, s: (0,) * a.ndim)
    fixed = lambda *s: pl.BlockSpec(s, lambda j, s_: (0,) * len(s))
    mine = pl.BlockSpec((block, width), lambda j, s: (jnp.minimum(j, per_half - 1), 0))
    theirs = pl.BlockSpec((block, width), lambda j, s: (jnp.maximum(j - per_half, 0), 0))
    shape = jax.ShapeDtypeStruct
    return pl.pallas_call(
        functools.partial(feed_kernel, piece_rows, out_rows, steps),
        grid_spec=pltpu.PrefetchScalarGridSpec(
            num_scalar_prefetch=1,
            grid=(steps,),
            in_specs=[whole(normed), whole(middle), pl.BlockSpec((mols, half, width), lambda j, s: (s[1], 0, 0)), whole(other_grad), whole(valid), whole(attended_t),
                      whole(norms), whole(out_w), mine, mine, theirs, theirs, pl.BlockSpec((1, block), lambda j, s: (0, j))],
            out_specs=[pl.BlockSpec(memory_space=pl.ANY), pl.BlockSpec(memory_space=pl.ANY),
                       pl.BlockSpec((1, block), lambda j, s: (0, j)),
                       fixed(rows, width), fixed(rows, width), fixed(mols, width, 2 * half),
                       fixed(width, width), fixed(2, width)],
            scratch_shapes=[pltpu.VMEM((rows, width), bf16), pltpu.VMEM((rows, width), f32), pltpu.VMEM((rows, width), f32),
                            pltpu.VMEM((block, width), bf16), pltpu.VMEM((block, width), bf16), pltpu.VMEM(out_w.shape, bf16),
                            pltpu.VMEM((2, half_pieces, piece_rows + out_rows, width), bf16),
                            pltpu.VMEM((2, half_pieces, piece_rows + out_rows, width), bf16),
                            pltpu.SemaphoreType.DMA((2 * half_pieces, 2))]
                           + [pltpu.VMEM((4 * half_pieces, out_rows, width), f32), pltpu.SemaphoreType.DMA((2,))] * (out_rows > 0),
        ),
        out_shape=[shape((2, half_pieces, piece_rows + out_rows, width), bf16), shape((2, half_pieces, piece_rows + out_rows, width), bf16), shape((1, 2 * held), f32), shape((rows, width), bf16),
                   shape((rows, width), f32), shape((mols, width, 2 * half), bf16),
                   shape((width, width), f32), shape((2, width), f32)],
        compiler_params=pltpu.CompilerParams(vmem_limit_bytes=vmem_bytes),
        cost_estimate=pl.CostEstimate(flops=14 * 10**9, bytes_accessed=14 * 10**6, transcendentals=2 * 10**6),
        name="feed",
    )(place, normed, middle, own_grad, other_grad, valid, attended_t, norms, out_w, up_own, down_own, first, second, bias)


def score_kernel(
    prob_ref, grad_t_ref, read_t_ref, value_ref, key_t_ref, query_t_ref, type_t_ref, after_ref,
    query_grad_ref, key_grad_ref, value_grad_ref, pair_grad_ref,
):
    molecule = pl.program_id(1)
    heads, slots = prob_ref.shape[1], prob_ref.shape[2]
    span = grad_t_ref.shape[1]
    head_width = span // heads
    scale = head_width**-0.5
    values = value_ref[0, 0]
    grads = grad_t_ref[0]
    keys = key_t_ref[0]
    queries = query_t_ref[0]
    kinds = type_t_ref[0]
    count = kinds.shape[0]
    owner = lax.broadcasted_iota(jnp.int32, (span, slots), 0) // head_width
    wide_grads = grads.astype(f32)
    zero = jnp.zeros_like(wide_grads)
    dotted = wide_grads * read_t_ref[0]

    def pair_of(array, head):
        return array[(head // 2) * 16 : (head // 2) * 16 + 16]

    def own_half(both, head):
        return both[0:8] if head % 2 == 0 else both[8:16]

    def prob_grads(head):
        return mxu(values, jnp.where(owner == head, wide_grads, zero).astype(bf16))

    def score_grads(head, prob_grad):
        center = jnp.sum(dotted[head * head_width : (head + 1) * head_width], axis=0, keepdims=True)
        return (prob_ref[0, head].astype(f32) * (prob_grad - center)).astype(bf16)

    query_parts, key_parts, value_parts, type_parts = [], [], [], []

    def products(head, score_grad):
        left = jnp.concatenate([pair_of(keys, head), kinds], axis=0)
        both = mxu(left, score_grad)
        query_parts.append(own_half(both, head) * scale)
        type_parts.append(both[16:])
        key_parts.append(own_half(mxu(pair_of(queries, head), score_grad, NT), head) * scale)

    ahead = 3
    waiting = [prob_grads(head) for head in range(ahead)]
    done = []
    for head in range(heads):
        done.append(score_grads(head, waiting[head]))
        value_parts.append(own_half(mxu(pair_of(grads, head), prob_ref[0, head], NT), head))
        if head + ahead < heads:
            waiting.append(prob_grads(head + ahead))
        if head:
            products(head - 1, done[head - 1])
    products(heads - 1, done[heads - 1])
    query_grad_ref[0] = jnp.concatenate(query_parts, axis=0).astype(bf16)
    key_grad_ref[0] = jnp.concatenate(key_parts, axis=0).astype(bf16)
    value_grad_ref[0] = jnp.concatenate(value_parts, axis=0).astype(bf16)
    high, low = two_parts(jnp.concatenate(type_parts, axis=0))
    pairs = mxu(kinds, high, NT) + mxu(kinds, low, NT)

    @pl.when(molecule == 0)
    def _():
        pair_grad_ref[...] = pairs

    @pl.when(molecule > 0)
    def _():
        pair_grad_ref[...] += pairs


def attend_back(first, count, probs, grad_t, read_t, values, key_t, query_t, type_t, after):
    mols, all_heads, slots, _ = probs.shape
    groups = values.shape[1]
    heads = all_heads // groups
    width = grad_t.shape[1]
    span = width // groups
    kinds = type_t.shape[1]
    rows = pl.BlockSpec((1, span, slots), lambda g, m: (m, first + g, 0))
    new_rows = pl.BlockSpec((1, span, slots), lambda g, m: (m, g, 0))
    shape = jax.ShapeDtypeStruct
    part = shape((mols, count * span, slots), bf16)
    return pl.pallas_call(
        score_kernel,
        grid=(count, mols),
        in_specs=[pl.BlockSpec((1, heads, slots, slots), lambda g, m: (m, first + g, 0, 0)), rows, rows,
                  pl.BlockSpec((1, 1, slots, span), lambda g, m: (m, first + g, 0, 0)), rows, rows,
                  pl.BlockSpec((1, kinds, slots), lambda g, m: (m, 0, 0)), pl.BlockSpec(memory_space=pl.ANY)],
        out_specs=[new_rows, new_rows, new_rows, pl.BlockSpec((kinds, heads * kinds), lambda g, m: (0, g))],
        out_shape=[part, part, part, shape((kinds, count * heads * kinds), f32)],
        compiler_params=pltpu.CompilerParams(vmem_limit_bytes=vmem_less),
        cost_estimate=pl.CostEstimate(flops=5 * 10**9 * count, bytes_accessed=3 * 10**6 * count, transcendentals=0),
        name="attend_back",
    )(probs, grad_t, read_t, values, key_t, query_t, type_t, after)


def project_kernel(
    pieces, calls, place_ref, normed_t_ref, weight_ref, own_ref, other_ref, middle_grad_ref, norm_ref, norm_two_ref, bias_grad_ref, after_ref, *refs,
):
    part_refs, refs = refs[: 4 * calls], refs[4 * calls :]
    keep_ref, send_ref, own_out_ref, other_out_ref, ordered, grad_t_ref = refs
    part_rows = part_refs[0].shape[1]
    for call in range(calls):
        for kind in range(3):
            start = kind * part_rows * calls + call * part_rows
            grad_t_ref[:, start : start + part_rows] = part_refs[4 * call + kind][...]
    pair_refs = part_refs[3::4]
    per_pair = pair_refs[0].shape[1] // 128
    me = place_ref[2]
    mols, width, slots = normed_t_ref.shape
    half = slots // 2
    rows = width // pieces
    block = 256
    for start in range(0, width, block):
        total = sum(mxu(normed_t_ref[m, start : start + block], grad_t_ref[m], NT) for m in range(mols))
        for piece in range(block // rows):
            ordered[start // rows + piece, :, 0 : total.shape[1]] = total[piece * rows : (piece + 1) * rows]
    weight = weight_ref[...].astype(bf16)
    gain_grad, offset_grad = 0.0, 0.0
    for m in range(mols):
        normed_grad = mxu(weight, grad_t_ref[m]).T
        unit, inverse = norm_parts(jnp.concatenate([own_ref[place_ref[1] * mols + m], other_ref[m]], axis=0).astype(f32))
        gain_grad += jnp.sum(normed_grad * unit, axis=0, keepdims=True)
        offset_grad += jnp.sum(normed_grad, axis=0, keepdims=True)
        result = middle_grad_ref[m * slots : (m + 1) * slots] + norm_back(normed_grad, unit, inverse, norm_ref[0:1])
        own_out_ref[m] = result[:half]
        other_out_ref[m] = result[half:].astype(bf16)
    columns = weight_ref.shape[1]
    kinds = pair_refs[0].shape[0]
    for chunk in range(width // kinds):
        at = chunk % per_pair * 128
        ordered[:, chunk, columns : columns + 128] = pair_refs[chunk // per_pair][:, at : at + 128]
    bias = bias_grad_ref[...]
    held = bias.shape[1] // 2
    side = place_ref[1].astype(f32)
    turned = jnp.concatenate([bias[:, held:], bias[:, :held]], axis=1)
    bias = bias * (1.0 - side) + turned * side
    rest = [bias[:, start : start + width] for start in range(0, 2 * held, width)]
    vectors = [gain_grad, offset_grad, norm_two_ref[...]] + rest + [jnp.zeros((128 - 4 - len(rest), width), f32)]
    vectors = jnp.concatenate(vectors, axis=0)
    ordered[:, :, columns + 128 : columns + 256] = vectors.T.reshape(kinds, width // kinds, 128)
    core = place_ref[0]
    count = pieces // 2
    for piece in range(count):
        at = jnp.bitwise_xor(piece, me)
        keep_ref[at] = ordered[core * count + piece].astype(bf16)
        send_ref[at] = ordered[(1 - core) * count + piece].astype(bf16)


def project_back(place, parts, normed_t, weight, own, other, middle_grad, norms, norm_two, bias_grad, after, pieces):
    mols, width, slots = normed_t.shape
    columns = weight.shape[1]
    shape = jax.ShapeDtypeStruct
    vmem = pl.BlockSpec(memory_space=pltpu.VMEM)
    return pl.pallas_call(
        functools.partial(project_kernel, pieces, len(parts)),
        in_specs=[pl.BlockSpec(memory_space=pltpu.SMEM)] + [vmem] * 8 + [pl.BlockSpec(memory_space=pl.ANY)] + [vmem] * 4 * len(parts),
        out_specs=[vmem] * 4,
        out_shape=[shape((pieces // 2, width // pieces, columns + 256), bf16), shape((pieces // 2, width // pieces, columns + 256), bf16),
                   shape((mols, slots // 2, width), f32),
                   shape((mols, slots // 2, width), bf16)],
        scratch_shapes=[pltpu.VMEM((pieces, width // pieces, columns + 256), f32), pltpu.VMEM((mols, columns, slots), bf16)],
        compiler_params=pltpu.CompilerParams(vmem_limit_bytes=vmem_less),
        cost_estimate=pl.CostEstimate(flops=4 * 10**9, bytes_accessed=10 * 10**6, transcendentals=0),
        name="project_back",
    )(place, normed_t, weight, own, other, middle_grad, norms, norm_two, bias_grad, after, *[array for part in parts for array in part])


def swap(array, axis, bit, size):
    return lax.ppermute(array, axis, [(i, i ^ (1 << bit)) for i in range(size)])


def add_low(left, right):
    return (left.astype(f32) + right.astype(f32)).astype(bf16)


def tied(array, after):
    return array if after is None else lax.optimization_barrier((array, after))[0]


def halve(array, axes, digit, sizes, after=None):
    index = axes.index(digit)
    keep = lax.index_in_dim(array, 0, index, keepdims=False)
    send = lax.index_in_dim(array, 1, index, keepdims=False)
    return add_low(tied(keep, after), swap(send, *digit, sizes[digit[0]])), axes[:index] + axes[index + 1 :]


def jump(array, digits, sizes):
    axis = digits[0][0]
    mask = sum(1 << bit for _, bit in digits)
    return lax.ppermute(array, axis, [(i, i ^ mask) for i in range(sizes[axis])])


def quarter(array, axes, pair, sizes, after=None):
    first, second = axes.index(pair[0]), axes.index(pair[1])
    array = jnp.moveaxis(array, (first, second), (0, 1))
    total = tied(array[0, 0], after).astype(f32)
    for place, digits in (((1, 0), pair[:1]), ((0, 1), pair[1:]), ((1, 1), pair)):
        total = total + jump(array[place], digits, sizes).astype(f32)
    return total.astype(bf16), [digit for digit in axes if digit not in pair]


def double(array, digit, sizes, after=None):
    return jnp.stack([tied(array, after), swap(array, *digit, sizes[digit[0]])])


def quadruple(array, pair, sizes, after=None):
    pieces = [tied(array, after)] + [jump(array, digits, sizes) for digits in (pair[1:], pair[:1], pair)]
    return jnp.stack(pieces).reshape((2, 2) + array.shape)


def split_middle(digits):
    middle = digits[1:-1]
    return middle[: len(middle) % 2], [middle[i : i + 2] for i in range(len(middle) % 2, len(middle), 2)]


def scatter_first(array, digits, sizes, after=None):
    cut = array.shape[-1] // 2
    left, _ = halve(array[..., :cut], digits, digits[0], sizes, after)
    right, _ = halve(array[..., cut:], digits, digits[-1], sizes, after)
    return left, right


def scatter_second(parts, digits, sizes, after=None):
    left, _ = halve(parts[0], digits[1:], digits[-1], sizes, after)
    right, _ = halve(parts[1], digits[:-1], digits[0], sizes, after)
    return jnp.concatenate([left, right], axis=-1)


def scatter_middle(both, digits, sizes, after=None):
    single, pairs = split_middle(digits)
    axes = digits[1:-1]
    for pair in pairs[::-1]:
        both, axes = quarter(both, axes, pair, sizes, after)
    for digit in single:
        both, axes = halve(both, axes, digit, sizes)
    return both


def gather_middle(both, digits, sizes, after=None):
    single, pairs = split_middle(digits)
    for digit in single:
        both = double(both, digit, sizes)
    for pair in pairs:
        both = quadruple(both, pair, sizes, after)
    return both


def gather_second(both, digits, sizes, after=None):
    cut = both.shape[-1] // 2
    return double(both[..., :cut], digits[-1], sizes, after), double(both[..., cut:], digits[0], sizes, after)


def gather_first(parts, digits, sizes, after=None):
    left = double(parts[0], digits[0], sizes, after)
    right = double(parts[1], digits[-1], sizes, after)
    return left, jnp.swapaxes(right, 0, 1)


def beside(parts):
    return jnp.concatenate(parts, axis=-1)


def gather_order(digits):
    single, pairs = split_middle(digits)
    return [digits[0], digits[-1]] + [digit for pair in pairs[::-1] for digit in pair] + single


def place_list(order, digits):
    result = []
    for number in range(2 ** len(order)):
        bits = {digit: (number >> (len(order) - 1 - i)) & 1 for i, digit in enumerate(order)}
        result.append(sum(bits[digit] << (len(digits) - 1 - i) for i, digit in enumerate(digits)))
    return result


def absolute(array, digits, places):
    for index, (axis, bit) in enumerate(digits):
        flag = (places[axis] >> bit) & 1
        array = jnp.where(flag == 1, jnp.flip(array, index), array)
    return array


def muon_load(high_ref, low_ref, source_ref, scale, tall):
    block = 256
    for start in range(0, source_ref.shape[0], block):
        at = slice(start, start + block)
        high_ref[at], low_ref[at] = two_parts(source_ref[at] * scale)


def symmetric_product(left, right):
    half = left.shape[0] // 2
    left_high, left_low = two_parts(left)
    right_high, right_low = two_parts(right)
    rows = jnp.concatenate([left_high, left_low, left_high], axis=1)
    columns = jnp.concatenate([right_high, right_high, right_low], axis=0)
    top = mxu(rows[:half], columns)
    corner = mxu(rows[half:], columns[:, half:])
    return jnp.concatenate([top, jnp.concatenate([top[:, half:].T, corner], axis=1)], axis=0)


def muon_product(tall, steps, high_ref, low_ref, gram_ref, poly_ref, product_ref):
    size = gram_ref.shape[0]
    row = lax.broadcasted_iota(jnp.int32, (size, size), 0)
    column = lax.broadcasted_iota(jnp.int32, (size, size), 1)

    def polynomial():
        gram = gram_ref[...]
        poly_ref[...] = coef_second * gram + coef_third * symmetric_product(gram, gram)

    def inner(index, carry):
        poly = poly_ref[...]
        gram = gram_ref[...]
        step = coef_first * gram + symmetric_product(poly, gram)
        gram_ref[...] = coef_first * step + symmetric_product(poly, step)
        polynomial()
        product = product_ref[...]
        product_ref[...] = coef_first * product + symmetric_product(poly_ref[...], product)
        return carry

    if tall:
        both = mxu(high_ref[...], jnp.concatenate([high_ref[...], low_ref[...]], axis=1), TN)
    else:
        both = mxu(high_ref[...], jnp.concatenate([high_ref[...], low_ref[...]], axis=0), NT)
    crossing = both[:, size:]
    gram_ref[...] = both[:, :size] + crossing + crossing.T
    polynomial()
    product_ref[...] = poly_ref[...] + jnp.where(row == column, coef_first, 0.0)
    if not isinstance(steps, int) or steps > 1:
        lax.fori_loop(0, steps - 1, inner, 0)


def muon_blocks(tall, high_ref, low_ref, product_ref, length):
    high, low = two_parts(product_ref[...])
    block = 256
    if tall:
        right = jnp.concatenate([high, high, low], axis=0)
    else:
        left = jnp.concatenate([high, high, low], axis=1)
    for start in range(0, length, block):
        at = slice(start, start + block)
        if tall:
            left = jnp.concatenate([high_ref[at], low_ref[at], high_ref[at]], axis=1)
        else:
            right = jnp.concatenate([high_ref[:, at], low_ref[:, at], high_ref[:, at]], axis=0)
        yield at, mxu(left, right)


def inverse_norm(values):
    return 1.0 / (jnp.sqrt(jnp.full((1, 1), values, f32)) + 1e-07)


def muon_scratch(shape, size):
    return [pltpu.VMEM(shape, bf16), pltpu.VMEM(shape, bf16)] + [pltpu.VMEM((size, size), f32)] * 3


def copies_of(pairs, semaphores):
    copies = [pltpu.make_async_copy(source, target, semaphores.at[index]) for index, (source, target) in enumerate(pairs)]
    for copy in copies:
        copy.start()
    return copies


def muon_feed_kernel(
    numbers, place_ref, sum_ref, own_state_ref, other_state_ref, direction_ref,
    sums, own_state, other_state, direction, moment, high, low, gram, poly, product, semaphores, out_semaphores,
):
    me = place_ref[4]
    held, width = own_state.shape
    count = len(numbers) // 2
    rows = held // count
    incoming = copies_of(
        [(sum_ref.at[0:count], sums.at[0:count]), (own_state_ref, own_state),
         (sum_ref.at[count : 2 * count], sums.at[count : 2 * count]), (other_state_ref, other_state)],
        semaphores,
    )
    total = jnp.zeros((1, width), f32)
    for index, number in enumerate(numbers):
        if index % count == 0:
            incoming[2 * (index // count)].wait()
            incoming[2 * (index // count) + 1].wait()
        state_ref = own_state if index < count else other_state
        start = pl.multiple_of(jnp.bitwise_xor(number % count, me) * rows, rows)
        state = state_ref[pl.ds(start, rows), :].astype(f32)
        value = momentum_keep * state + sums[index, 0:rows].astype(f32)
        moment[pl.ds(start + (0 if index < count else held), rows), :] = value
        total += jnp.sum(value * value, axis=0, keepdims=True)
    muon_load(high, low, moment, inverse_norm(jnp.sum(total)), True)
    muon_product(True, 3, high, low, gram, poly, product)
    for at, value in muon_blocks(True, high, low, product, 2 * held):
        high[at], low[at] = two_parts(value)
    muon_product(True, 2, high, low, gram, poly, product)
    outgoing = []
    for at, value in muon_blocks(True, high, low, product, held):
        direction[at] = value.astype(bf16)
        outgoing += copies_of([(direction.at[at], direction_ref.at[at])], out_semaphores.at[pl.ds(len(outgoing), 1)])
    for copy in outgoing:
        copy.wait()


def muon_feed(place, sums, own_state, other_state, numbers):
    held, width = own_state.shape
    any_memory = pl.BlockSpec(memory_space=pl.ANY)
    return pl.pallas_call(
        functools.partial(muon_feed_kernel, numbers),
        in_specs=[pl.BlockSpec(memory_space=pltpu.SMEM)] + [any_memory] * 3,
        out_specs=any_memory,
        out_shape=jax.ShapeDtypeStruct((held, width), bf16),
        scratch_shapes=[pltpu.VMEM(sums.shape, bf16), pltpu.VMEM((held, width), f32), pltpu.VMEM((held, width), bf16),
                        pltpu.VMEM((held, width), bf16), pltpu.VMEM((2 * held, width), f32)]
                       + muon_scratch((2 * held, width), width)
                       + [pltpu.SemaphoreType.DMA((4,)), pltpu.SemaphoreType.DMA((held // 256,))],
        compiler_params=pltpu.CompilerParams(vmem_limit_bytes=vmem_less),
        cost_estimate=pl.CostEstimate(flops=26 * 10**9, bytes_accessed=8 * 10**6, transcendentals=0),
        name="muon_feed",
    )(place, sums, own_state, other_state)


def muon_whole_kernel(
    numbers, plan, rate, me_ref, sum_ref, swapped_ref, state_ref, weight_ref, moment_ref, updated_ref,
    sums, swapped, state, weight, high, low, gram, poly, product, semaphores, out_semaphores,
):
    me = me_ref[0]
    rows = sums.shape[1]
    columns = state.shape[1]
    incoming = copies_of([(state_ref, state), (sum_ref, sums), (swapped_ref, swapped), (weight_ref, weight)], semaphores)
    for copy in incoming[:3]:
        copy.wait()
    total = jnp.zeros((1, columns), f32)
    for core_place, ref in enumerate((sums, swapped)):
        for index, number in enumerate(numbers):
            number += core_place * len(numbers)
            start = pl.multiple_of(jnp.bitwise_xor(number, me) * rows, rows)
            value = momentum_keep * state[pl.ds(start, rows), :] + ref[index, :, 0:columns].astype(f32)
            state[pl.ds(start, rows), :] = value
            total += jnp.sum(value * value, axis=0, keepdims=True)
    moment_out = copies_of([(state, moment_ref)], out_semaphores.at[pl.ds(0, 1)])
    muon_load(high, low, state, inverse_norm(jnp.sum(total)), False)

    def outer(index, carry):
        muon_product(False, plan[0] if len(set(plan)) == 1 else plan[0] - index, high, low, gram, poly, product)
        for at, value in muon_blocks(False, high, low, product, columns):
            high[:, at], low[:, at] = two_parts(value)
        return carry

    lax.fori_loop(0, len(plan), outer, 0)
    incoming[3].wait()
    outgoing = moment_out
    for start in range(0, weight.shape[0], 64):
        at = slice(start, start + 64)
        weight[at] = weight[at] - rate * (high[at].astype(f32) + low[at].astype(f32))
        outgoing = outgoing + copies_of([(weight.at[at], updated_ref.at[at])], out_semaphores.at[pl.ds(len(outgoing), 1)])
    for copy in outgoing:
        copy.wait()


def muon_whole(me, sums, swapped, state, weight, numbers, plan, rate):
    any_memory = pl.BlockSpec(memory_space=pl.ANY)
    shape = jax.ShapeDtypeStruct(state.shape, f32)
    return pl.pallas_call(
        functools.partial(muon_whole_kernel, numbers, plan, rate),
        in_specs=[pl.BlockSpec(memory_space=pltpu.SMEM)] + [any_memory] * 4,
        out_specs=[any_memory] * 2,
        out_shape=[shape, shape],
        scratch_shapes=[pltpu.VMEM(sums.shape, bf16), pltpu.VMEM(sums.shape, bf16), pltpu.VMEM(state.shape, f32),
                        pltpu.VMEM(state.shape, f32)]
                       + muon_scratch(state.shape, state.shape[0])
                       + [pltpu.SemaphoreType.DMA((4,)), pltpu.SemaphoreType.DMA((1 + state.shape[0] // 64,))],
        compiler_params=pltpu.CompilerParams(vmem_limit_bytes=vmem_less),
        cost_estimate=pl.CostEstimate(flops=state.size * 25000, bytes_accessed=16 * 10**6, transcendentals=0),
        name="muon_whole",
    )(me, sums, swapped, state, weight)


def feed_moments_kernel(
    numbers, place_ref, own_ref, swapped_ref, up_state_ref, down_state_ref, up_ref, down_ref,
    own, swapped, up_state, down_state, up_sum, down_sum, in_semaphores, out_semaphores,
):
    me = place_ref[4]
    core = place_ref[0]
    _, rows, _ = own.shape
    block = 256
    blocks = [slice(start, start + block) for start in range(0, up_sum.shape[0], block)]
    sums = copies_of([(own_ref, own), (swapped_ref, swapped)], in_semaphores.at[pl.ds(0, 2)])
    states = []
    for at in blocks:
        pairs = [(up_state_ref.at[:, at], up_state.at[:, at]), (down_state_ref.at[at], down_state.at[at])]
        states.append(copies_of(pairs, in_semaphores.at[pl.ds(2 + 2 * len(states), 2)]))
    for copy in sums:
        copy.wait()

    def write(up_from, down_from):
        for index, number in enumerate(numbers):
            start = pl.multiple_of(jnp.bitwise_xor(number, me) * rows, rows)
            up_sum[pl.ds(start, rows), :] = up_from[index].astype(f32)
            down_sum[pl.ds(start, rows), :] = down_from[index].astype(f32)

    @pl.when(core == 0)
    def _():
        write(own, swapped)

    @pl.when(core == 1)
    def _():
        write(swapped, own)

    results = []
    for index, at in enumerate(blocks):
        for copy in states[index]:
            copy.wait()
        up_state[:, at] = momentum_keep * up_state[:, at] + up_sum[at].T
        down_state[at] = momentum_keep * down_state[at] + down_sum[at]
        pairs = [(up_state.at[:, at], up_ref.at[:, at]), (down_state.at[at], down_ref.at[at])]
        results += copies_of(pairs, out_semaphores.at[pl.ds(2 * index, 2)])
    for copy in results:
        copy.wait()


def feed_moments(place, own, swapped, up_state, down_state, numbers):
    any_memory = pl.BlockSpec(memory_space=pl.ANY)
    blocks = down_state.shape[0] // 256
    return pl.pallas_call(
        functools.partial(feed_moments_kernel, numbers),
        in_specs=[pl.BlockSpec(memory_space=pltpu.SMEM)] + [any_memory] * 4,
        out_specs=[any_memory] * 2,
        out_shape=[jax.ShapeDtypeStruct(up_state.shape, f32), jax.ShapeDtypeStruct(down_state.shape, f32)],
        scratch_shapes=[pltpu.VMEM(own.shape, bf16), pltpu.VMEM(own.shape, bf16), pltpu.VMEM(up_state.shape, f32)]
                       + [pltpu.VMEM(down_state.shape, f32)] * 3
                       + [pltpu.SemaphoreType.DMA((2 + 2 * blocks,)), pltpu.SemaphoreType.DMA((2 * blocks,))],
        compiler_params=pltpu.CompilerParams(vmem_limit_bytes=vmem_less),
        cost_estimate=pl.CostEstimate(flops=10**6, bytes_accessed=10 * 10**6, transcendentals=0),
        name="feed_moments",
    )(place, own, swapped, up_state, down_state)


def feed_update_kernel(
    rate_first, rate_second, place_ref, own_ref, swapped_ref, up_weight_ref, down_weight_ref, up_ref, down_ref,
    both, up_weight, down_weight, in_semaphores, out_semaphores,
):
    core = place_ref[0]
    block = 256
    blocks = [slice(start, start + block) for start in range(0, down_weight.shape[0], block)]
    incoming = []
    for at in blocks:
        pairs = [(own_ref.at[at], both.at[core, at]), (swapped_ref.at[at], both.at[1 - core, at]),
                 (up_weight_ref.at[:, at], up_weight.at[:, at]), (down_weight_ref.at[at], down_weight.at[at])]
        incoming.append(copies_of(pairs, in_semaphores.at[pl.ds(4 * len(incoming), 4)]))
    results = []
    for index, at in enumerate(blocks):
        for copy in incoming[index]:
            copy.wait()
        up_weight[:, at] = up_weight[:, at] - rate_first * both[0, at].astype(f32).T
        down_weight[at] = down_weight[at] - rate_second * both[1, at].astype(f32)
        pairs = [(up_weight.at[:, at], up_ref.at[:, at]), (down_weight.at[at], down_ref.at[at])]
        results += copies_of(pairs, out_semaphores.at[pl.ds(2 * index, 2)])
    for copy in results:
        copy.wait()


def feed_update(place, own, swapped, up_weight, down_weight, rate_first, rate_second):
    any_memory = pl.BlockSpec(memory_space=pl.ANY)
    blocks = down_weight.shape[0] // 256
    return pl.pallas_call(
        functools.partial(feed_update_kernel, rate_first, rate_second),
        in_specs=[pl.BlockSpec(memory_space=pltpu.SMEM)] + [any_memory] * 4,
        out_specs=[any_memory] * 2,
        out_shape=[jax.ShapeDtypeStruct(up_weight.shape, f32), jax.ShapeDtypeStruct(down_weight.shape, f32)],
        scratch_shapes=[pltpu.VMEM((2,) + own.shape, bf16), pltpu.VMEM(up_weight.shape, f32), pltpu.VMEM(down_weight.shape, f32),
                        pltpu.SemaphoreType.DMA((4 * blocks,)), pltpu.SemaphoreType.DMA((2 * blocks,))],
        compiler_params=pltpu.CompilerParams(vmem_limit_bytes=vmem_less),
        cost_estimate=pl.CostEstimate(flops=10**6, bytes_accessed=10 * 10**6, transcendentals=0),
        name="feed_update",
    )(place, own, swapped, up_weight, down_weight)


def plain_update_kernel(rates, *refs):
    count = len(rates)
    for index, rate in enumerate(rates):
        sum_ref, state_ref, weight_ref = refs[3 * index : 3 * index + 3]
        moment_ref, updated_ref = refs[3 * count + 2 * index : 3 * count + 2 * index + 2]
        moment = momentum_keep * state_ref[...] + sum_ref[...]
        moment_ref[...] = moment
        updated_ref[...] = weight_ref[...] - rate * moment


def plain_update(parts):
    vmem = pl.BlockSpec(memory_space=pltpu.VMEM)
    return pl.pallas_call(
        functools.partial(plain_update_kernel, [part[3] for part in parts]),
        in_specs=[vmem] * 3 * len(parts),
        out_specs=[vmem] * 2 * len(parts),
        out_shape=[jax.ShapeDtypeStruct(part[1].shape, f32) for part in parts for _ in range(2)],
        compiler_params=pltpu.CompilerParams(vmem_limit_bytes=16 * 2**20),
        cost_estimate=pl.CostEstimate(flops=10**5, bytes_accessed=2 * 10**6, transcendentals=0),
        name="plain_update",
    )(*[array for part in parts for array in part[:3]])


def step_factor(rows, columns):
    return math.sqrt(max(1.0, rows / columns))


def on_device(
    dp_size, mp_size,
    atoms, atom_counts, hydrogen, atom_types, cotangent, qkv_weight, out_weight, up_weight, down_weight, ffn_bias, norm_params,
    pair_table, qkv_state, out_state, up_state, down_state, bias_state, norm_state, pair_state,
):
    sizes = {"dp": dp_size, "mp": mp_size}
    place_dp, place_mp = lax.axis_index("dp"), lax.axis_index("mp")
    places = {"dp": place_dp, "mp": place_mp}
    core = place_dp & 1
    dp_bits = dp_size.bit_length() - 1
    mols, half, width = atoms.shape
    mine = mols // 2
    slots = 2 * half
    types_count, _, head_count = pair_table.shape
    kinds = 32

    def other_slots(array):
        return swap(lax.dynamic_slice_in_dim(array, (1 - place_mp) * mine, mine, 0), "mp", 0, mp_size)

    atoms_other = other_slots(atoms)
    up_own = up_weight.T.astype(bf16)
    down_own = down_weight.astype(bf16)
    bias_other = swap(ffn_bias, "mp", 0, mp_size)
    leaving_grad = lax.dynamic_slice_in_dim(cotangent, (1 - place_mp) * mine, mine, 0).reshape(-1, width)
    leaving = jnp.concatenate([jnp.where(core == 0, up_own, down_own), leaving_grad], axis=0)
    leaving, atoms_other, bias_other = lax.optimization_barrier((leaving, atoms_other, bias_other))
    crossed = swap(leaving, "mp", 0, mp_size)
    cot_other = crossed[up_own.shape[0] :].reshape(mine, half, width)
    bias_rel = jnp.concatenate([ffn_bias, bias_other])[None]

    scalars = jnp.concatenate([jnp.stack([core, place_mp]).astype(jnp.int32), atom_counts])
    (probs, read_t, query_t, key_t, values, normed_t, attended_t, middle, normed_two, own_state, leaving_state, type_t, valid) = attend(
        scalars, atoms, atoms_other, qkv_weight, norm_params, pair_table, atom_types, hydrogen, out_weight, up_state, down_state
    )
    crossed, normed_two = lax.optimization_barrier((crossed, normed_two))
    crossed_again = swap(crossed, "dp", 0, dp_size)
    other_state = swap(leaving_state, "mp", 0, mp_size)

    core_digit = ("dp", 0)
    half_digits = [("dp", bit) for bit in range(dp_bits - 1, 0, -1)]
    half_pieces = dp_size // 2
    chip_digits = [("mp", 0)] + half_digits
    some_digits = chip_digits[-4:]
    plain_digits = chip_digits[:-4]
    pieces = 2 ** (1 + len(some_digits))
    half_place = place_dp >> 1
    some_place = (place_mp * half_pieces + half_place) & (pieces // 2 - 1)
    piece_rows = up_own.shape[0] // half_pieces
    out_rows = width // (4 * half_pieces)
    aligned = out_rows % 16 == 0
    place = jnp.stack(
        [core, place_mp, some_place, core * (pieces // 2) + some_place, half_place, place_mp * half_pieces + half_place]
    ).astype(jnp.int32)

    rows = mine * slots
    (keep, send, bias_grad, mixed, middle_grad, attended_grad_t, out_grad, norm_grad_two) = feed(
        place, normed_two.reshape(rows, width), middle.reshape(rows, width), cotangent, cot_other, valid.reshape(rows, 1), attended_t,
        norm_params, out_weight, up_own, down_own, crossed, crossed_again, bias_rel, half_pieces, out_rows if aligned else 0,
    )

    digit_shape = (2,) * len(chip_digits)
    if not aligned:
        out_grad = out_grad.astype(bf16).reshape((2,) + digit_shape + (out_rows, width))
        out_grad = absolute(out_grad, [core_digit] + chip_digits, places).reshape((2, 2, half_pieces, out_rows, width))
        keep, send = jnp.concatenate([keep, out_grad[0]], axis=-2), jnp.concatenate([send, out_grad[1]], axis=-2)
    early = add_low(keep, swap(send, "dp", 0, dp_size)).reshape(digit_shape + (piece_rows + out_rows, width))
    early_ends = scatter_first(early, chip_digits, sizes)
    early_both = scatter_second(early_ends, chip_digits, sizes)

    def corner(*arrays):
        return jnp.stack([array[(0,) * (array.ndim - 2)][:16, :128] for array in arrays])

    groups = values.shape[1]
    calls = 4
    mixed = mixed.reshape(mine, slots, width)
    mixed_moved = swap(mixed[:, half:], "mp", 0, mp_size)
    waits = [place, corner(early), corner(early, mixed_moved), corner(*early_ends, other_state), corner(early_both)]
    parts = [
        attend_back(i * groups // calls, groups // calls, probs, attended_grad_t, read_t, values, key_t, query_t, type_t, waits[i])
        for i in range(calls)
    ]
    late_keep, late_send, atoms_grad_own, atoms_grad_other = project_back(
        place, parts, normed_t, qkv_weight, atoms, atoms_other, middle_grad, norm_params, norm_grad_two, bias_grad, waits[4], pieces
    )

    def own_last(array):
        return swap(array, "dp", 0, dp_size)

    def back_slots(own, moved):
        moved = moved.astype(own.dtype)
        return jnp.where(place_mp == 0, jnp.concatenate([own, moved], 0), jnp.concatenate([moved, own], 0))

    atoms_moved = swap(atoms_grad_other, "mp", 0, mp_size)
    early_order, late_order = gather_order(chip_digits), gather_order(some_digits)
    late = add_low(late_keep, own_last(late_send))
    late_shape = late.shape
    late = late.reshape((2,) * len(some_digits) + late_shape[1:])
    early_both = scatter_middle(early_both, chip_digits, sizes, late_keep)
    late_ends = scatter_first(late, some_digits, sizes)
    early_middle = gather_middle(early_both, chip_digits, sizes, late_ends)
    out_own = double(early_middle[..., piece_rows:, :], chip_digits[-1], sizes)
    late_both = scatter_second(late_ends, some_digits, sizes, out_own)
    early_half = gather_second(early_middle[..., :piece_rows, :], chip_digits, sizes, (late_both, atoms_moved))
    out_own = double(out_own, chip_digits[0], sizes, early_half).reshape((2 * half_pieces, out_rows, width))
    late_both = scatter_middle(late_both, some_digits, sizes, out_own)
    for axis, bit in plain_digits:
        late_both = add_low(late_both, swap(late_both, axis, bit, sizes[axis]))
    out_swapped = tied(own_last(out_own), late_both)
    out_numbers, out_me = place_list(early_order, chip_digits), core * 2 * half_pieces + place[5]
    if not aligned:
        out_sum = jnp.stack([out_own, out_swapped]).reshape((2,) + digit_shape + (out_rows, width))
        out_sum = absolute(out_sum, [core_digit] + early_order, places)
        spots = [0] + [1 + early_order.index(digit) for digit in chip_digits]
        out_sum = out_sum.transpose(spots + [len(spots), len(spots) + 1]).reshape(2, -1, 16, width)
        out_own, out_swapped = out_sum
        out_numbers, out_me = list(range(out_own.shape[0])), out_me * 0
    out_moment, out_updated = muon_whole(
        out_me[None].astype(jnp.int32), out_own, out_swapped, out_state, out_weight, out_numbers, (1, 1, 1, 1, 1),
        rate_out * step_factor(*out_weight.shape),
    )
    late_middle = gather_middle(late_both, some_digits, sizes, out_updated)
    mixed_out = back_slots(mixed[:, :half], mixed_moved)
    atoms_grad = back_slots(atoms_grad_own, atoms_moved)
    early_sum = beside(gather_first(early_half, chip_digits, sizes, (late_middle, mixed_out, atoms_grad)))
    early_sum = early_sum.reshape((2 * half_pieces, piece_rows, width))
    direction = muon_feed(place, early_sum, own_state, other_state, place_list(early_order, chip_digits))
    own_sum = early_sum[:half_pieces]
    own_numbers = place_list(early_order[1:], half_digits)
    late_half = gather_second(late_middle, some_digits, sizes, direction)
    up_moment, down_moment = feed_moments(place, tied(own_sum, late_half), own_last(own_sum), up_state, down_state, own_numbers)
    late_sum = beside(gather_first(late_half, some_digits, sizes, up_moment)).reshape(late_shape)
    hidden_units = mp_size * up_weight.shape[1]
    up_updated, down_updated = feed_update(
        place, tied(direction, late_sum), own_last(direction), up_weight, down_weight,
        rate_up * step_factor(width, hidden_units), rate_down * step_factor(hidden_units, width),
    )
    late_swapped = own_last(late_sum)
    late_sum = tied(late_sum, up_updated)
    qkv_moment, qkv_updated = muon_whole(
        place[3:4], late_sum, late_swapped, qkv_state, qkv_weight, place_list(late_order, some_digits), (3, 2),
        rate_qkv * step_factor(*qkv_weight.shape),
    )

    order = late_order
    small = jnp.stack([late_sum[..., 3 * width :], late_swapped[..., 3 * width :]])
    small = absolute(small.reshape((2,) * (1 + len(order)) + small.shape[2:]), [core_digit] + order, places)
    spots = (0,) + tuple(1 + order.index(digit) for digit in some_digits)
    small = small.transpose(spots + (len(spots), len(spots) + 1)).reshape(kinds, width // kinds, 256).astype(f32)
    pair_sum = small[..., :128].reshape(kinds, head_count, kinds).transpose(0, 2, 1)[:types_count, :types_count]
    vectors = small[..., 128:136].reshape(width, 8).T
    norm_sum = vectors[:4]
    bias_sum = lax.dynamic_slice_in_dim(vectors[4:].reshape(-1), place_mp * ffn_bias.shape[0], ffn_bias.shape[0], 0)

    flat = (-1, 128)
    norm_moment, norm_updated, bias_moment, bias_updated, pair_moment, pair_updated = plain_update([
        (norm_sum, norm_state, norm_params, rate_norm),
        (bias_sum.reshape(flat), bias_state.reshape(flat), ffn_bias.reshape(flat), rate_bias),
        (pair_sum, pair_state, pair_table, rate_pair),
    ])
    bias_moment, bias_updated = bias_moment.reshape(-1), bias_updated.reshape(-1)

    return (
        mixed_out,
        atoms_grad,
        qkv_moment,
        qkv_updated,
        out_moment,
        out_updated,
        up_moment,
        up_updated,
        down_moment,
        down_updated,
        bias_moment,
        bias_updated,
        norm_moment,
        norm_updated,
        pair_moment,
        pair_updated,
    )


def solution(mesh):
    rows = P("dp", "mp", None)
    in_specs = (
        rows, P("dp"), P("dp", None), P("dp", None), rows, P(), P(), P(None, "mp"), P("mp", None), P("mp"), P(), P(),
        P(), P(), P(None, "mp"), P("mp", None), P("mp"), P(), P(),
    )
    out_specs = (
        rows, rows, P(), P(), P(), P(), P(None, "mp"), P(None, "mp"), P("mp", None), P("mp", None), P("mp"), P("mp"),
        P(), P(), P(), P(),
    )
    body = functools.partial(on_device, mesh.shape["dp"], mesh.shape["mp"])
    return jax.shard_map(body, mesh=mesh, in_specs=in_specs, out_specs=out_specs, check_vma=False)
```
